128 devices in a mesh: replica: 16 (over z, x_hi, core), shard: 8 (over x_lo, y).
Axes of the slice: x: 4 (x_hi: 2, x_lo: 2; x = x_hi * 2 + x_lo), y: 4, z: 4, core: 2. Of those that a mesh axis runs over, the one named last changes fastest.
Arguments:
- tokens: bfloat16 [16384, 1024], P(('replica', 'shard')), may hold values from -6 to 6
- grad_out: bfloat16 [16384, 1024], P(('replica', 'shard')), may hold values from -6 to 6
- slope_index: int32 [16], replicated, may hold values from 0 to 15, each once
- ln1_gain: bfloat16 [2, 1024], P(None, 'shard'), may hold values from 0.5 to 1.5
- ln1_bias: bfloat16 [2, 1024], P(None, 'shard'), may hold values from -1 to 1
- qkv_weight: bfloat16 [2, 1024, 3072], P(None, 'shard'), may hold values from -0.1875 to 0.1875
- q_bias: bfloat16 [2, 1024], P(None, 'shard'), may hold values from -1 to 1
- v_bias: bfloat16 [2, 1024], P(None, 'shard'), may hold values from -1 to 1
- dense_weight: bfloat16 [2, 1024, 1024], P(None, 'shard'), may hold values from -0.375 to 0.375
- dense_bias: bfloat16 [2, 1024], P(None, 'shard'), may hold values from -1 to 1
- ln2_gain: bfloat16 [2, 1024], P(None, 'shard'), may hold values from 0.5 to 1.5
- ln2_bias: bfloat16 [2, 1024], P(None, 'shard'), may hold values from -1 to 1
- up_weight: bfloat16 [2, 1024, 4096], P(None, 'shard'), may hold values from -0.1875 to 0.1875
- up_bias: bfloat16 [2, 4096], P(None, 'shard'), may hold values from -1 to 1
- down_weight: bfloat16 [2, 4096, 1024], P(None, 'shard'), may hold values from -0.09375 to 0.09375
- down_bias: bfloat16 [2, 1024], P(None, 'shard'), may hold values from -1 to 1
Outputs:
- output: float32 [16384, 1024], P(('replica', 'shard'))
- grad_tokens: float32 [16384, 1024], P(('replica', 'shard'))
- grad_ln1_gain: float32 [2, 1024], P(None, 'shard')
- grad_ln1_bias: float32 [2, 1024], P(None, 'shard')
- grad_qkv_weight: float32 [2, 1024, 3072], P(None, 'shard')
- grad_q_bias: float32 [2, 1024], P(None, 'shard')
- grad_v_bias: float32 [2, 1024], P(None, 'shard')
- grad_dense_weight: float32 [2, 1024, 1024], P(None, 'shard')
- grad_dense_bias: float32 [2, 1024], P(None, 'shard')
- grad_ln2_gain: float32 [2, 1024], P(None, 'shard')
- grad_ln2_bias: float32 [2, 1024], P(None, 'shard')
- grad_up_weight: float32 [2, 1024, 4096], P(None, 'shard')
- grad_up_bias: float32 [2, 4096], P(None, 'shard')
- grad_down_weight: float32 [2, 4096, 1024], P(None, 'shard')
- grad_down_bias: float32 [2, 1024], P(None, 'shard')
The draws below stay inside these ranges and needn't reach their ends.
Inputs may be any that keep to these rules, and one draw needn't show every extreme that they name: `slope_index`: each head has its own slope number, every number once.
All inputs are finite; a program needn't handle non-finite values.
Results may differ from the reference program's by a relative error of at most 0.025.
Values may be sent and summed in bfloat16 or wider, within the bound.
A program may use at most 256 MiB of HBM per device.

```python
import jax
import jax.numpy as jnp
from jax import lax

D = 1024
HEADS = 16
FF = 4096
LAYERS = 2
SEQ = 1024
TOKENS = 16384


def level_of(rng, extent, split, smallest, top_value):
    level = 1.0
    for position, parts in split:
        heights = jax.random.uniform(jax.random.fold_in(jax.random.fold_in(rng, 6), position), (parts,), jnp.float32, smallest / len(split), top_value / len(split))
        level = level * jnp.repeat(jnp.exp(heights), extent[position] // parts).reshape((-1,) + (1,) * (len(extent) - 1 - position))
    return level


def scatter_about(own_key, extent, spread, bound, shards=(), held_as=jnp.bfloat16):
    loudness = level_of(own_key, extent, shards, -0.22, 0.18) if shards else 1.0
    array = jax.random.normal(own_key, extent, jnp.float32) * spread * loudness
    return jnp.minimum(jnp.maximum(array, -bound), bound).astype(held_as)


def setup_inputs(seed: int = 0) -> dict:
    arg_keys = jax.random.split(jax.random.key(seed), 17)
    tokens = scatter_about(arg_keys[0], (TOKENS, D), 1.0, 6.0, ((0, 128),))
    grad_out = scatter_about(arg_keys[1], (TOKENS, D), 1.0, 6.0, ((0, 128),))
    slope_index = jax.random.permutation(arg_keys[2], HEADS).astype(jnp.int32)
    ln1_gain = jnp.clip(1.0 + 0.1 * jax.random.normal(arg_keys[3], (LAYERS, D), jnp.float32), 0.5, 1.5).astype(jnp.bfloat16)
    ln1_bias = scatter_about(arg_keys[4], (LAYERS, D), 0.2, 1.0, ((1, 8),))
    qkv_weight = scatter_about(arg_keys[5], (LAYERS, D, 3 * D), D ** -0.5, 0.1875, ((1, 8),))
    q_bias = scatter_about(arg_keys[6], (LAYERS, D), 0.2, 1.0, ((1, 8),))
    v_bias = scatter_about(arg_keys[7], (LAYERS, D), 0.2, 1.0, ((1, 8),))
    dense_weight = scatter_about(arg_keys[8], (LAYERS, D, D), (D // 4) ** -0.5, 0.375, ((1, 8),))
    dense_bias = scatter_about(arg_keys[9], (LAYERS, D), 0.2, 1.0, ((1, 8),))
    ln2_gain = jnp.clip(1.0 + 0.1 * jax.random.normal(arg_keys[10], (LAYERS, D), jnp.float32), 0.5, 1.5).astype(jnp.bfloat16)
    ln2_bias = scatter_about(arg_keys[11], (LAYERS, D), 0.2, 1.0, ((1, 8),))
    up_weight = scatter_about(arg_keys[12], (LAYERS, D, FF), D ** -0.5, 0.1875, ((1, 8),))
    up_bias = scatter_about(arg_keys[13], (LAYERS, FF), 0.2, 1.0, ((1, 8),))
    down_weight = scatter_about(arg_keys[14], (LAYERS, FF, D), FF ** -0.5, 0.09375, ((1, 8),))
    down_bias = scatter_about(arg_keys[15], (LAYERS, D), 0.2, 1.0, ((1, 8),))
    return dict(tokens=tokens, grad_out=grad_out, slope_index=slope_index, ln1_gain=ln1_gain, ln1_bias=ln1_bias, qkv_weight=qkv_weight, q_bias=q_bias, v_bias=v_bias, dense_weight=dense_weight, dense_bias=dense_bias, ln2_gain=ln2_gain, ln2_bias=ln2_bias, up_weight=up_weight, up_bias=up_bias, down_weight=down_weight, down_bias=down_bias)


eps = 1e-05

@jax.custom_vjp
def low(v):
    return lax.optimization_barrier(v.astype(jnp.bfloat16)).astype(jnp.float32)

@jax.custom_vjp
def low_back(v):
    return v

def low_keep(v):
    return (low(v), None)

def low_pass(kept, grad):
    return (grad,)

def back_keep(v):
    return (v, None)

def back_low(kept, grad):
    return (low(grad),)
low.defvjp(low_keep, low_pass)
low_back.defvjp(back_keep, back_low)

def product(left, right):
    return jnp.dot(left, right, precision=lax.Precision.HIGHEST)

def norm_rows(values, gain_vec, shift_vec):
    average = lax.optimization_barrier(jnp.mean(values, axis=-1, keepdims=True))
    centred = values - average
    variance = lax.optimization_barrier(jnp.mean(centred * centred, axis=-1, keepdims=True))
    return centred * lax.rsqrt(variance + eps) * gain_vec + shift_vec

def attend(queries, key_rows, value_rows, slopes):
    length = queries.shape[0]
    head_count = slopes.shape[0]
    head_size = queries.shape[1] // head_count
    scaling = head_size ** (-0.5)
    query_h = queries.reshape(length, head_count, head_size).transpose(1, 0, 2)
    key_h = key_rows.reshape(length, head_count, head_size).transpose(1, 0, 2)
    value_h = value_rows.reshape(length, head_count, head_size).transpose(1, 0, 2)
    scores = jnp.einsum('hqd,hkd->hqk', query_h, key_h, precision=lax.Precision.HIGHEST) * scaling
    positions = jnp.arange(length)
    offset = (positions[:, None] - positions[None, :]).astype(jnp.float32)
    scores = low_back(scores - slopes[:, None, None] * offset[None])
    scores = jnp.where((positions[:, None] >= positions[None, :])[None], scores, -1000000000.0)
    probability = low(jax.nn.softmax(scores, axis=-1))
    context = jnp.einsum('hqk,hkd->hqd', probability, value_h, precision=lax.Precision.HIGHEST)
    return context.transpose(1, 0, 2).reshape(length, head_count * head_size)

def layer(hidden, weights, slopes):
    gain_a, shift_a, w_qkv, bias_q, bias_v, w_dense, bias_dense, gain_b, shift_b, w_up, bias_up, w_down, bias_down = weights
    features = hidden.shape[1]
    input_a = low(norm_rows(hidden, gain_a, shift_a))
    bias_all = jnp.concatenate([bias_q, jnp.zeros_like(bias_q), bias_v])
    projected = low(low_back(product(input_a, w_qkv) + bias_all))
    context = attend(projected[:, :features], projected[:, features:2 * features], projected[:, 2 * features:], slopes)
    context = low(low_back(context))
    after_attn = hidden + low_back(product(context, w_dense) + bias_dense)
    input_b = low(norm_rows(after_attn, gain_b, shift_b))
    pre_act = low_back(product(input_b, w_up) + bias_up)
    active = low(jax.nn.gelu(pre_act, approximate=True))
    return after_attn + low_back(product(active, w_down) + bias_down)

def reference(tokens, grad_out, slope_index, ln1_gain, ln1_bias, qkv_weight, q_bias, v_bias, dense_weight, dense_bias, ln2_gain, ln2_bias, up_weight, up_bias, down_weight, down_bias):
    parameters = [member.astype(jnp.float32) for member in (ln1_gain, ln1_bias, qkv_weight, q_bias, v_bias, dense_weight, dense_bias, ln2_gain, ln2_bias, up_weight, up_bias, down_weight, down_bias)]
    slopes = jnp.exp2(-8.0 * (slope_index.astype(jnp.float32) + 1.0) / HEADS)

    def forward(inputs, weights):
        hidden = inputs
        for layer_id in range(LAYERS):
            hidden = layer(hidden, [member[layer_id] for member in weights], slopes)
        return hidden

    def one_sequence(summed, operands):
        inputs, cotangent = operands
        result, pull_back = jax.vjp(forward, inputs, parameters)
        grad_inputs, grad_params = pull_back(cotangent)
        return ([earlier + gradient for earlier, gradient in zip(summed, grad_params)], (result, grad_inputs))
    sequences = tokens.astype(jnp.float32).reshape(-1, SEQ, D)
    cotangents = grad_out.astype(jnp.float32).reshape(-1, SEQ, D)
    starting = [jnp.zeros_like(member) for member in parameters]
    totals, (results, grad_inputs) = lax.scan(one_sequence, starting, (sequences, cotangents))
    return (results.reshape(-1, D), grad_inputs.reshape(-1, D), totals[0], totals[1], totals[2], totals[3], totals[4], totals[5], totals[6], totals[7], totals[8], totals[9], totals[10], totals[11], totals[12])
```

```python
import functools

import jax
import jax.numpy as jnp
from jax import lax
from jax.experimental import pallas as pl
from jax.experimental.pallas import tpu as pltpu
from jax.sharding import Mesh
from jax.sharding import PartitionSpec as P

eps = 1e-05
MESH = pl.DeviceIdType.MESH
AXES = ("z", "xh", "c", "xl", "y")
BF = jnp.bfloat16
F32 = jnp.float32
BLK = 128
HALF = 64
WIDTH = 1024
RING = 4
CALL_VMEM = 56 * 1024 * 1024


def gelu(u):
    t = jnp.tanh(0.7978845608028654 * (u + 0.044715 * u * u * u))
    return 0.5 * u * (1.0 + t)


def gelu_slope(u):
    sq = u * u
    t = jnp.tanh(0.7978845608028654 * (u + 0.044715 * sq * u))
    return 0.5 * (1.0 + t) + 0.5 * u * (1.0 - t * t) * (
        0.7978845608028654 * (1.0 + 3.0 * 0.044715 * sq)
    )


def norm_parts(values):
    average = jnp.mean(values, axis=-1, keepdims=True)
    centred = values - average
    variance = jnp.mean(centred * centred, axis=-1, keepdims=True)
    r = lax.rsqrt(variance + eps)
    return centred * r, r


def comm_kernel(cfg, names, *refs):
    ref = dict(zip(names, refs))
    y, c, xl = lax.axis_index("y"), lax.axis_index("c"), lax.axis_index("xl")
    up, down, far = lax.rem(y + 1, RING), lax.rem(y + 3, RING), lax.rem(y + 2, RING)
    oc, ox = 1 - c, 1 - xl
    sib, nxt, prv, xnb = {"c": oc}, {"y": up}, {"y": down}, {"xl": ox}
    partners = [sib, nxt, prv] + ([xnb] if cfg["swap_in"] or cfg["swap_out"] else [])

    barrier = pltpu.get_barrier_semaphore()
    for partner in partners:
        pl.semaphore_signal(barrier, inc=1, device_id=partner, device_id_type=MESH)
    pl.semaphore_wait(barrier, len(partners))

    sent = []

    def push(src, dst, target):
        i = len(sent)
        copy = pltpu.make_async_remote_copy(
            src_ref=src,
            dst_ref=dst,
            send_sem=ref["send"].at[i],
            recv_sem=ref["recv"].at[i],
            device_id=target,
            device_id_type=MESH,
        )
        copy.start()
        sent.append(copy)
        return copy

    local = []

    def store(src, dst):
        copy = pltpu.make_async_copy(src, dst, ref["local"].at[len(local)])
        copy.start()
        local.append(copy)

    def rows(group, q, offset=0, size=BLK):
        return pl.ds(pl.multiple_of((group * RING + q) * BLK + offset, HALF), size)

    def gather_start(block):
        own = rows(c, y)
        low, high = rows(c, y, 0, HALF), rows(c, y, HALF, HALF)
        gbuf = ref["gbuf"]
        gbuf[own, :] = block
        first = [
            push(gbuf.at[low], gbuf.at[low], nxt),
            push(gbuf.at[high], gbuf.at[high], prv),
            push(gbuf.at[own], gbuf.at[own], sib),
            push(gbuf.at[high], gbuf.at[high], nxt),
            push(gbuf.at[low], gbuf.at[low], prv),
        ]
        return first

    def gather_rest(first, consume):
        gbuf = ref["gbuf"]
        low_n, high_p, own_s, high_n, low_p = first
        consume(c, y)
        low_n.wait_recv()
        part = gbuf.at[rows(c, down, 0, HALF)]
        fwd_n = push(part, part, nxt)
        high_p.wait_recv()
        part = gbuf.at[rows(c, up, HALF, HALF)]
        fwd_p = push(part, part, prv)
        own_s.wait_recv()
        consume(oc, y)
        high_n.wait_recv()
        part = gbuf.at[rows(c, down)]
        sib_a = push(part, part, sib)
        low_p.wait_recv()
        part = gbuf.at[rows(c, up)]
        sib_b = push(part, part, sib)
        consume(c, down)
        consume(c, up)
        sib_a.wait_recv()
        consume(oc, down)
        sib_b.wait_recv()
        consume(oc, up)
        fwd_n.wait_recv()
        fwd_p.wait_recv()
        part = gbuf.at[rows(c, far)]
        sib_c = push(part, part, sib)
        consume(c, far)
        sib_c.wait_recv()
        consume(oc, far)

    first = None
    if cfg["mid"] == "fin":
        first = gather_start(ref["grad_out"][...])

    acc = None
    if cfg["rs"]:
        order = [far, up, down, y]
        lhs = ref["lhs"]
        chunks = []
        if cfg["swap_in"]:
            rowbuf = ref["rowbuf"]
            for q in order:
                chunks.append(push(lhs.at[rows(ox, q)], rowbuf.at[rows(xl, q)], xnb))
            mine = pl.ds(pl.multiple_of(xl * RING * BLK, BLK), RING * BLK)
            rowbuf[mine, :] = lhs[mine, :]
        else:
            rowbuf = lhs

        def partial(group, q):
            return jnp.dot(
                rowbuf[rows(group, q), :], ref["w_rs"][...], preferred_element_type=F32
            )

        own, sib_out, sib_in = ref["own"], ref["sib_out"], ref["sib_in"]
        stage = ref["stage"]
        near_n, near_p, far_n, far_p = ref["near_n"], ref["near_p"], ref["far_n"], ref["far_p"]
        low, high = pl.ds(0, HALF), pl.ds(HALF, HALF)
        ring = {}
        passed = []

        def begin(slot):
            if chunks:
                chunks[slot].wait_recv()
            sib_out[slot] = partial(oc, order[slot]).astype(BF)
            passed.append(push(sib_out.at[slot], sib_in.at[slot], sib))
            own[slot] = partial(c, order[slot])

        def finish(slot):
            passed[slot].wait_recv()
            total = own[slot] + sib_in[slot].astype(F32)
            if slot == 0:
                stage[0] = total.astype(BF)
                ring["fn"] = push(stage.at[0, low], far_n, nxt)
                ring["fp"] = push(stage.at[0, high], far_p, prv)
            elif slot == 1:
                stage[1, high, :] = total[HALF:].astype(BF)
                ring["nh"] = push(stage.at[1, high], near_n.at[high], nxt)
                own[1, low, :] = total[:HALF]
            elif slot == 2:
                stage[2, low, :] = total[:HALF].astype(BF)
                ring["pl"] = push(stage.at[2, low], near_p.at[low], prv)
                own[2, high, :] = total[HALF:]
            else:
                own[3] = total

        begin(0)
        begin(1)
        finish(0)
        begin(2)
        finish(1)
        begin(3)
        finish(2)
        ring["fn"].wait_recv()
        stage[1, low, :] = (own[1, low, :] + far_n[...].astype(F32)).astype(BF)
        ring["nl"] = push(stage.at[1, low], near_n.at[low], nxt)
        ring["fp"].wait_recv()
        stage[2, high, :] = (own[2, high, :] + far_p[...].astype(F32)).astype(BF)
        ring["ph"] = push(stage.at[2, high], near_p.at[high], prv)
        finish(3)
        if cfg["swap_in"]:
            store(rowbuf, ref["rows_out"])
        for key in ("nh", "pl", "nl", "ph"):
            ring[key].wait_recv()
        acc = own[3] + near_n[...].astype(F32) + near_p[...].astype(F32)

    block = None
    if cfg["mid"] == "ln":
        xhat, _ = norm_parts(ref["resid"][...].astype(F32))
        block = (xhat * ref["gain"][...] + ref["shift"][...]).astype(BF)
    elif cfg["mid"] == "fwd":
        hidden = ref["resid"][...].astype(F32) + (acc + ref["bias_rs"][...])
        ref["hidden"][...] = hidden
        xhat, _ = norm_parts(hidden)
        block = (xhat * ref["gain"][...] + ref["shift"][...]).astype(BF)
    elif cfg["mid"] == "fin":
        ref["hidden"][...] = ref["resid"][...].astype(F32) + (acc + ref["bias_rs"][...])
    elif cfg["mid"] == "bwd":
        xhat, r = norm_parts(ref["resid"][...].astype(F32))
        ref["g_gain"][...] = jnp.sum(acc * xhat, axis=0, keepdims=True)
        ref["g_shift"][...] = jnp.sum(acc, axis=0, keepdims=True)
        scaled = acc * ref["gain"][...]
        grad = ref["stream"][...].astype(F32) + r * (
            scaled
            - jnp.mean(scaled, axis=-1, keepdims=True)
            - xhat * jnp.mean(scaled * xhat, axis=-1, keepdims=True)
        )
        ref["hidden"][...] = grad
        block = grad.astype(BF)

    if cfg["tail"] is not None:
        if first is None:
            first = gather_start(block)
        done = {}
        out_copies = []

        def consume(group, q):
            where = rows(group, q)
            value = jnp.dot(ref["gbuf"][where, :], ref["w_ag"][...], preferred_element_type=F32)
            if cfg["tail"] == "up":
                pre = value + ref["bias_ag"][...]
                ref["pre"][where, :] = pre
                ref["active"][where, :] = gelu(pre).astype(BF)
            elif cfg["tail"] == "dpre":
                ref["grad_pre"][where, :] = (value * gelu_slope(ref["pre_in"][where, :])).astype(BF)
            else:
                if cfg["tail"] == "qkv":
                    value = value + ref["bias_ag"][...]
                pbuf, xbuf = ref["pbuf"], ref["xbuf"]
                pbuf[where, :] = value.astype(BF)
                key = id(q)
                done[key] = done.get(key, 0) + 1
                if done[key] == 2:
                    out_copies.append(push(pbuf.at[rows(ox, q)], xbuf.at[rows(xl, q)], xnb))
                    xbuf[rows(xl, q), :] = pbuf[rows(xl, q), :]

        gather_rest(first, consume)
        store(ref["gbuf"], ref["gathered"])
        if cfg["swap_out"]:
            for copy in out_copies:
                copy.wait_recv()
            ref["att"][...] = ref["xbuf"][...]
    for copy in sent:
        copy.wait_send()
    for copy in local:
        copy.wait()


def comm_call(cid, *, mid, rs=False, swap_in=False, tail=None, **operands):
    swap_out = tail in ("qkv", "gctx")
    cfg = dict(rs=rs, swap_in=swap_in, swap_out=swap_out, mid=mid, tail=tail)
    whole = pl.BlockSpec(memory_space=pltpu.VMEM)
    in_names = list(operands)
    total_rows = 2 * RING * BLK
    outs = {}
    scratch = {}
    flops = 0
    if rs:
        k = operands["lhs"].shape[1]
        flops += 2 * total_rows * k * WIDTH
        if swap_in:
            outs["rows_out"] = ((total_rows, k), BF, pl.ANY)
            scratch["rowbuf"] = pltpu.VMEM((total_rows, k), BF)
        scratch["own"] = pltpu.VMEM((RING, BLK, WIDTH), F32)
        scratch["sib_out"] = pltpu.VMEM((RING, BLK, WIDTH), BF)
        scratch["sib_in"] = pltpu.VMEM((RING, BLK, WIDTH), BF)
        scratch["stage"] = pltpu.VMEM((3, BLK, WIDTH), BF)
        scratch["near_n"] = pltpu.VMEM((BLK, WIDTH), BF)
        scratch["near_p"] = pltpu.VMEM((BLK, WIDTH), BF)
        scratch["far_n"] = pltpu.VMEM((HALF, WIDTH), BF)
        scratch["far_p"] = pltpu.VMEM((HALF, WIDTH), BF)
    if mid != "ln":
        outs["hidden"] = ((BLK, WIDTH), F32, pltpu.VMEM)
    if mid == "bwd":
        outs["g_gain"] = ((1, WIDTH), F32, pltpu.VMEM)
        outs["g_shift"] = ((1, WIDTH), F32, pltpu.VMEM)
    if tail is not None:
        n = operands["w_ag"].shape[1]
        flops += 2 * total_rows * n * WIDTH
        outs["gathered"] = ((total_rows, WIDTH), BF, pl.ANY)
        scratch["gbuf"] = pltpu.VMEM((total_rows, WIDTH), BF)
        if tail == "up":
            outs["pre"] = ((total_rows, n), F32, pltpu.VMEM)
            outs["active"] = ((total_rows, n), BF, pltpu.VMEM)
        elif tail == "dpre":
            outs["grad_pre"] = ((total_rows, n), BF, pltpu.VMEM)
        else:
            outs["att"] = ((total_rows, n), BF, pltpu.VMEM)
            scratch["pbuf"] = pltpu.VMEM((total_rows, n), BF)
            scratch["xbuf"] = pltpu.VMEM((total_rows, n), BF)
    scratch["send"] = pltpu.SemaphoreType.DMA((32,))
    scratch["recv"] = pltpu.SemaphoreType.DMA((32,))
    scratch["local"] = pltpu.SemaphoreType.DMA((2,))
    results = pl.pallas_call(
        functools.partial(comm_kernel, cfg, in_names + list(outs) + list(scratch)),
        out_shape=[jax.ShapeDtypeStruct(shape, dtype) for shape, dtype, _ in outs.values()],
        in_specs=[whole] * len(in_names),
        out_specs=[pl.BlockSpec(memory_space=space) for _, _, space in outs.values()],
        scratch_shapes=list(scratch.values()),
        cost_estimate=pl.CostEstimate(flops=flops, bytes_accessed=20_000_000, transcendentals=0),
        compiler_params=pltpu.CompilerParams(
            collective_id=cid, has_side_effects=True, vmem_limit_bytes=CALL_VMEM
        ),
    )(*operands.values())
    return dict(zip(outs, results))


QB = 256


def head_only(values, head):
    lane = lax.broadcasted_iota(jnp.int32, values.shape, 1)
    keep = (lane // 64) == head
    return jnp.where(keep, values, jnp.zeros_like(values))


def probs_of(q_pad, keys, slope, start):
    count = keys.shape[0]
    scores = lax.dot_general(
        keys, q_pad, (((1,), (1,)), ((), ())), preferred_element_type=F32
    )
    key_pos = lax.broadcasted_iota(jnp.int32, (count, QB), 0)
    query_pos = lax.broadcasted_iota(jnp.int32, (count, QB), 1) + start
    scores = scores + slope * key_pos.astype(F32)
    scores = jnp.where(key_pos <= query_pos, scores, -1000000000.0)
    top = jnp.max(scores, axis=0, keepdims=True)
    exponent = jnp.exp(scores - top)
    total = jnp.sum(exponent, axis=0, keepdims=True)
    return exponent * (1.0 / total)


def attention_fwd_kernel(slopes, qkv, ctx):
    value_t = qkv[:, 2 * BLK : 3 * BLK].astype(F32).T.astype(BF)
    for start in range(0, qkv.shape[0], QB):
        count = start + QB
        queries = qkv[start : start + QB, 0:BLK] * jnp.asarray(0.125, BF)
        keys = qkv[0:count, BLK : 2 * BLK]
        parts = []
        for head in range(2):
            probs = probs_of(head_only(queries, head), keys, slopes[head], start).astype(BF)
            ctx_t = jnp.dot(value_t[:, 0:count], probs, preferred_element_type=F32)
            parts.append(ctx_t[head * 64 : head * 64 + 64])
        ctx[start : start + QB, :] = jnp.concatenate(parts, axis=0).T.astype(BF)


def attention_bwd_kernel(slopes, qkv, gctx, dqkv, dk, dv):
    key_t = qkv[:, BLK : 2 * BLK].astype(F32).T.astype(BF)
    dk[...] = jnp.zeros_like(dk)
    dv[...] = jnp.zeros_like(dv)
    for start in range(0, qkv.shape[0], QB):
        count = start + QB
        queries = qkv[start : start + QB, 0:BLK] * jnp.asarray(0.125, BF)
        keys = qkv[0:count, BLK : 2 * BLK]
        values = qkv[0:count, 2 * BLK : 3 * BLK]
        grads = gctx[start : start + QB, :]
        parts = []
        for head in range(2):
            q_pad = head_only(queries, head)
            g_pad = head_only(grads, head)
            probs = probs_of(q_pad, keys, slopes[head], start)
            grad_probs = lax.dot_general(
                values, g_pad, (((1,), (1,)), ((), ())), preferred_element_type=F32
            )
            inner = jnp.sum(probs * grad_probs, axis=0, keepdims=True)
            grad_scores = (probs * (grad_probs - inner)).astype(BF)
            dk[0:count, :] += jnp.dot(grad_scores, q_pad, preferred_element_type=F32)
            dv[0:count, :] += jnp.dot(probs.astype(BF), g_pad, preferred_element_type=F32)
            dq_t = jnp.dot(key_t[:, 0:count], grad_scores, preferred_element_type=F32)
            parts.append(dq_t[head * 64 : head * 64 + 64] * 0.125)
        dqkv[start : start + QB, 0:BLK] = jnp.concatenate(parts, axis=0).T.astype(BF)
    dqkv[:, BLK : 2 * BLK] = dk[...].astype(BF)
    dqkv[:, 2 * BLK : 3 * BLK] = dv[...].astype(BF)


def attention_call(kernel, slopes, qkv, *more, width, scratch=()):
    whole = pl.BlockSpec(memory_space=pltpu.VMEM)
    return pl.pallas_call(
        kernel,
        out_shape=jax.ShapeDtypeStruct((qkv.shape[0], width), BF),
        in_specs=[pl.BlockSpec(memory_space=pltpu.SMEM), whole] + [whole] * len(more),
        out_specs=whole,
        scratch_shapes=list(scratch),
        cost_estimate=pl.CostEstimate(
            flops=4_000_000_000, bytes_accessed=2_000_000, transcendentals=2_000_000
        ),
        compiler_params=pltpu.CompilerParams(vmem_limit_bytes=CALL_VMEM),
    )(slopes, qkv, *more)


def attention_forward(slopes, qkv):
    return attention_call(attention_fwd_kernel, slopes, qkv, width=BLK)


def attention_backward(slopes, qkv, gctx):
    scratch = [pltpu.VMEM((qkv.shape[0], BLK), F32)] * 2
    return attention_call(
        attention_bwd_kernel, slopes, qkv, gctx, width=3 * BLK, scratch=scratch
    )


def columns_to_rank(own_rows, parts):
    c = lax.axis_index("c")
    depth, cols = own_rows.shape
    per = cols // (parts * 2 * RING)
    split = own_rows.reshape(depth, parts, 2, RING, per)
    split = lax.dynamic_index_in_dim(split, c, 2, keepdims=False)
    split = split.transpose(2, 0, 1, 3).reshape(RING, depth, parts * per)
    mine = lax.all_to_all(split, "y", 0, 0, tiled=True)
    mine = mine.reshape(RING * depth, parts * per)
    other = lax.ppermute(mine, "xl", [(0, 1), (1, 0)])
    xl = lax.axis_index("xl")
    return jnp.where(
        xl == 0,
        jnp.concatenate([mine, other], axis=0),
        jnp.concatenate([other, mine], axis=0),
    )


def rows_to_rank(own_rows):
    other = lax.ppermute(own_rows, ("c", "xl"), [(0, 1), (3, 2)])
    return jnp.where(lax.axis_index("c") == lax.axis_index("xl"), own_rows, other)


def rank_to_shard(value):
    other = lax.ppermute(value, "c", [(0, 1), (1, 0)])
    return jnp.where(lax.axis_index("c") == lax.axis_index("xl"), value, other)


def rank_sum(value):
    return lax.psum(value.astype(BF), ("z", "xh", "xl"))


def columns_to_shard(value, parts):
    rows, cols = value.shape
    split = value.reshape(2 * RING, rows // (2 * RING), cols)
    got = lax.all_to_all(split, ("c", "y"), 0, 0, tiled=True)
    per = cols // parts
    got = got.reshape(2 * RING, rows // (2 * RING), parts, per).transpose(1, 2, 0, 3)
    return rank_to_shard(got.reshape(rows // (2 * RING), 2 * RING * cols)).astype(F32)


def rows_to_shard(value):
    return rank_to_shard(value).astype(F32)


def weight_grad(left, right):
    return lax.dot_general(left, right, (((0,), (0,)), ((), ())), preferred_element_type=F32)


def on_device(
    tokens,
    grad_out,
    slope_index,
    ln1_gain,
    ln1_bias,
    qkv_weight,
    q_bias,
    v_bias,
    dense_weight,
    dense_bias,
    ln2_gain,
    ln2_bias,
    up_weight,
    up_bias,
    down_weight,
    down_bias,
):
    layers = qkv_weight.shape[0]
    heads = slope_index.shape[0]
    rank = lax.axis_index("c") * RING + lax.axis_index("y")
    slopes_all = jnp.exp2(-8.0 * (slope_index.astype(F32) + 1.0) / heads)
    slopes = lax.dynamic_slice(slopes_all, (rank * 2,), (2,))

    vectors = jnp.stack([ln1_gain, ln1_bias, dense_bias, ln2_gain, ln2_bias, down_bias])
    vectors = lax.all_gather(vectors, ("xl", "y"), axis=2, tiled=True).astype(F32)
    w_qkv = [columns_to_rank(qkv_weight[i], 3) for i in range(layers)]
    w_up = [columns_to_rank(up_weight[i], 1) for i in range(layers)]
    w_dense = [rows_to_rank(dense_weight[i]) for i in range(layers)]
    w_down = [rows_to_rank(down_weight[i]) for i in range(layers)]
    b_up = rows_to_rank(up_bias).astype(F32)
    b_q = rows_to_rank(q_bias).astype(F32)
    b_v = rows_to_rank(v_bias).astype(F32)

    def vector(number, i):
        return vectors[number, i][None, :]

    def bias_qkv(i):
        return jnp.concatenate([b_q[i], jnp.zeros_like(b_q[i]), b_v[i]])[None, :]

    streams, mids, saved = [tokens], [], []
    step = comm_call(
        1, mid="ln", tail="qkv", resid=tokens, gain=vector(0, 0), shift=vector(1, 0),
        w_ag=w_qkv[0], bias_ag=bias_qkv(0),
    )
    output = None
    for i in range(layers):
        keep = {"input_a": step["gathered"], "qkv": step["att"]}
        context = attention_forward(slopes, step["att"])
        step = comm_call(
            2, mid="fwd", rs=True, swap_in=True, tail="up", lhs=context, w_rs=w_dense[i],
            resid=streams[i], bias_rs=vector(2, i), gain=vector(3, i), shift=vector(4, i),
            w_ag=w_up[i], bias_ag=b_up[i][None, :],
        ) if i else comm_call(
            3, mid="fwd", rs=True, swap_in=True, tail="up", lhs=context, w_rs=w_dense[i],
            resid=streams[i], bias_rs=vector(2, i), gain=vector(3, i), shift=vector(4, i),
            w_ag=w_up[i], bias_ag=b_up[i][None, :],
        )
        mids.append(step["hidden"])
        keep.update(
            context=step["rows_out"], input_b=step["gathered"], pre=step["pre"],
            active=step["active"],
        )
        saved.append(keep)
        if i + 1 < layers:
            step = comm_call(
                4, mid="fwd", rs=True, tail="qkv", lhs=step["active"], w_rs=w_down[i],
                resid=mids[i], bias_rs=vector(5, i), gain=vector(0, i + 1),
                shift=vector(1, i + 1), w_ag=w_qkv[i + 1], bias_ag=bias_qkv(i + 1),
            )
            streams.append(step["hidden"])
        else:
            step = comm_call(
                5, mid="fin", rs=True, tail="dpre", lhs=step["active"], w_rs=w_down[i],
                resid=mids[i], bias_rs=vector(5, i), grad_out=grad_out,
                w_ag=w_down[i].T, pre_in=keep["pre"],
            )
            output = step["hidden"]

    grad_stream = grad_out
    grads = [None] * layers
    small = [None] * layers
    for i in reversed(range(layers)):
        keep = saved[i]
        grad_mlp, grad_pre = step["gathered"], step["grad_pre"]
        cols = rank * BLK
        bias_down = jnp.sum(
            lax.dynamic_slice_in_dim(grad_mlp, cols, BLK, 1).astype(F32), axis=0
        )
        g_down = weight_grad(keep["active"], grad_mlp)
        g_up = weight_grad(keep["input_b"], grad_pre)
        bias_up = jnp.sum(grad_pre.astype(F32), axis=0)
        step = comm_call(
            6, mid="bwd", rs=True, tail="gctx", lhs=grad_pre, w_rs=w_up[i].T,
            resid=mids[i], gain=vector(3, i), stream=grad_stream, w_ag=w_dense[i].T,
        ) if i else comm_call(
            7, mid="bwd", rs=True, tail="gctx", lhs=grad_pre, w_rs=w_up[i].T,
            resid=mids[i], gain=vector(3, i), stream=grad_stream, w_ag=w_dense[i].T,
        )
        grad_after, grad_attn = step["hidden"], step["gathered"]
        gain_b, shift_b = step["g_gain"], step["g_shift"]
        bias_dense = jnp.sum(
            lax.dynamic_slice_in_dim(grad_attn, cols, BLK, 1).astype(F32), axis=0
        )
        g_dense = weight_grad(keep["context"], grad_attn)
        dqkv = attention_backward(slopes, keep["qkv"], step["att"])
        bias_qv = jnp.sum(dqkv.astype(F32), axis=0)
        if i:
            step = comm_call(
                8, mid="bwd", rs=True, swap_in=True, tail="dpre", lhs=dqkv, w_rs=w_qkv[i].T,
                resid=streams[i], gain=vector(0, i), stream=grad_after,
                w_ag=w_down[i - 1].T, pre_in=saved[i - 1]["pre"],
            )
        else:
            step = comm_call(
                9, mid="bwd", rs=True, swap_in=True, lhs=dqkv, w_rs=w_qkv[i].T,
                resid=streams[i], gain=vector(0, i), stream=grad_after,
            )
        grad_stream = step["hidden"]
        g_qkv = weight_grad(keep["input_a"], step["rows_out"])
        flat = jnp.concatenate([bias_qv[:BLK], bias_qv[2 * BLK :], bias_dense, bias_up, bias_down])
        small[i] = rows_to_shard(rank_sum(flat))
        grads[i] = dict(
            qkv=columns_to_shard(rank_sum(g_qkv), 3),
            up=columns_to_shard(rank_sum(g_up), 1),
            dense=rows_to_shard(rank_sum(g_dense)),
            down=rows_to_shard(rank_sum(g_down)),
            norms=jnp.concatenate([step["g_gain"], step["g_shift"], gain_b, shift_b]),
        )
    norms = lax.psum(jnp.stack([g["norms"] for g in grads], axis=1), AXES)
    shard = lax.axis_index("xl") * RING + lax.axis_index("y")
    norms = lax.dynamic_slice_in_dim(norms, shard * BLK, BLK, 2)
    flat = jnp.stack(small)

    def stacked(name):
        return jnp.stack([g[name] for g in grads])

    ff = up_bias.shape[1]
    return (
        output,
        grad_stream,
        norms[0],
        norms[1],
        stacked("qkv"),
        flat[:, 0:BLK],
        flat[:, BLK : 2 * BLK],
        stacked("dense"),
        flat[:, 2 * BLK : 3 * BLK],
        norms[2],
        norms[3],
        stacked("up"),
        flat[:, 3 * BLK : 3 * BLK + ff],
        stacked("down"),
        flat[:, 3 * BLK + ff :],
    )


def solution(mesh):
    replica, shard = mesh.devices.shape
    fine = Mesh(mesh.devices.reshape(replica // 4, 2, 2, shard // RING, RING), AXES)
    rows = P(AXES, None)
    flat = P(None, ("xl", "y"))
    wide = P(None, ("xl", "y"), None)
    return jax.shard_map(
        on_device,
        mesh=fine,
        in_specs=(
            rows, rows, P(), flat, flat, wide, flat, flat, wide, flat, flat, flat, wide, flat,
            wide, flat,
        ),
        out_specs=(
            rows, rows, flat, flat, wide, flat, flat, wide, flat, flat, flat, wide, flat, wide,
            flat,
        ),
        check_vma=False,
    )
```

```python
import functools
from types import SimpleNamespace

import jax
import jax.numpy as jnp
from jax import lax
from jax.experimental import pallas as pl
from jax.experimental.pallas import tpu as pltpu
from jax.sharding import Mesh
from jax.sharding import PartitionSpec as P

eps = 1e-05
MESH = pl.DeviceIdType.MESH
AXES = ("z", "xh", "c", "xl", "y")
BF = jnp.bfloat16
F32 = jnp.float32
BLK = 128
HALF = 64
WIDTH = 1024
RING = 4
CALL_VMEM = 56 * 1024 * 1024


def gelu(u):
    t = jnp.tanh(0.7978845608028654 * (u + 0.044715 * u * u * u))
    return 0.5 * u * (1.0 + t)


def gelu_slope(u):
    sq = u * u
    t = jnp.tanh(0.7978845608028654 * (u + 0.044715 * sq * u))
    return 0.5 * (1.0 + t) + 0.5 * u * (1.0 - t * t) * (
        0.7978845608028654 * (1.0 + 3.0 * 0.044715 * sq)
    )


def norm_parts(values):
    average = jnp.mean(values, axis=-1, keepdims=True)
    centred = values - average
    variance = jnp.mean(centred * centred, axis=-1, keepdims=True)
    r = lax.rsqrt(variance + eps)
    return centred * r, r


def comm_kernel(cfg, names, *refs):
    ref = SimpleNamespace(**dict(zip(names, refs)))
    env = neighbours()
    z, c, xl, y = env.z, env.c, env.xl, env.y
    up, down, far = lax.rem(y + 1, RING), lax.rem(y + 3, RING), lax.rem(y + 2, RING)
    oc, ox = 1 - c, 1 - xl
    sib, nxt, prv, xnb = {"c": oc}, {"y": up}, {"y": down}, {"xl": ox}
    shard, rank = xl * RING + y, c * RING + y
    if cfg.ship:
        plane = [
            (lax.rem(xl + dx, 2), lax.rem(y + dy, RING))
            for dx, dy in ((0, 2), (1, 2), (1, 1), (1, 3), (0, 1), (0, 3), (1, 0))
        ]
        peers = [{"xl": px, "y": py} for px, py in plane]
        z_far = {"z": lax.rem(z + 2, RING)}
        partners = [sib] + peers + [env.z_next, env.z_prev, z_far]
    else:
        partners = [sib, nxt, prv] + ([xnb] if cfg.swap_in or cfg.swap_out else [])

    if cfg.reduce:
        partners = partners + env.reduce_partners
    enter(partners)

    sent = []

    def push(src, dst, target):
        i = len(sent)
        copy = pltpu.make_async_remote_copy(
            src_ref=src,
            dst_ref=dst,
            send_sem=ref.send.at[i],
            recv_sem=ref.recv.at[i],
            device_id=target,
            device_id_type=MESH,
        )
        copy.start()
        sent.append(copy)
        return copy

    local = []
    stored = [0]

    def store(src, dst):
        copy = pltpu.make_async_copy(src, dst, ref.local.at[stored[0]])
        copy.start()
        stored[0] += 1
        local.append(copy)

    def rows(group, q, offset=0, size=BLK):
        return pl.ds(pl.multiple_of((group * RING + q) * BLK + offset, HALF), size)

    def ship_columns(raw, layer, dst, parts):
        per = dst.shape[3] // parts
        quarter = pl.ds(pl.multiple_of(z * dst.shape[2], dst.shape[2]), dst.shape[2])
        copies, keeps = [], []
        for j in range(parts):
            for (_, py), peer in zip(plane, peers):
                cols = pl.ds(pl.multiple_of((j * 2 * RING + c * RING + py) * per, per), per)
                copies.append(
                    push(raw.at[layer, quarter, cols], dst.at[shard, z, :, pl.ds(j * per, per)], peer)
                )
            cols = pl.ds(pl.multiple_of((j * 2 * RING + rank) * per, per), per)
            store(raw.at[layer, quarter, cols], dst.at[shard, z, :, pl.ds(j * per, per)])
            keeps.append(local.pop())
        return dst, copies, keeps

    def ship_quarters(step):
        dst, copies, keeps = step
        for copy in copies:
            copy.wait_recv()
        for copy in keeps:
            copy.wait()
        view = dst.at[:, z]
        return [push(view, view, target) for target in (env.z_next, env.z_prev, z_far)]

    shipped_rows = []

    def ship_rows(raw, layer, dst):
        i = len(shipped_rows)
        copy = pltpu.make_async_remote_copy(
            src_ref=raw.at[layer],
            dst_ref=dst,
            send_sem=ref.row_send.at[i],
            recv_sem=ref.row_recv.at[i],
            device_id=xnb,
            device_id_type=MESH,
        )
        keep = pltpu.make_async_copy(raw.at[layer], dst, ref.row_local.at[i])
        shipped_rows.append((copy, keep))

        @pl.when(c == xl)
        def _():
            copy.start()
            keep.start()

    def ship_rows_wait():
        for copy, keep in shipped_rows:

            @pl.when(c == xl)
            def _():
                copy.wait_send()
                keep.wait()

            @pl.when(c != xl)
            def _():
                copy.wait_recv()

    shipped = []

    def ship_all():
        for kind, name, layer, parts in cfg.ship:
            if kind == "cols":
                dst = getattr(ref, "w_" + name)
                shipped.append(ship_columns(getattr(ref, "raw_" + name), layer, dst, parts))
            else:
                ship_rows(getattr(ref, "raw_" + name), layer, getattr(ref, "w_" + name))

    def gather_start(block):
        own = rows(c, y)
        low, high = rows(c, y, 0, HALF), rows(c, y, HALF, HALF)
        gbuf = ref.gbuf
        gbuf[own, :] = block
        first = [
            push(gbuf.at[low], gbuf.at[low], nxt),
            push(gbuf.at[high], gbuf.at[high], prv),
            push(gbuf.at[own], gbuf.at[own], sib),
            push(gbuf.at[high], gbuf.at[high], nxt),
            push(gbuf.at[low], gbuf.at[low], prv),
        ]
        return first

    def gather_rest(first, consume):
        gbuf = ref.gbuf
        low_n, high_p, own_s, high_n, low_p = first
        consume(c, y)
        low_n.wait_recv()
        part = gbuf.at[rows(c, down, 0, HALF)]
        fwd_n = push(part, part, nxt)
        high_p.wait_recv()
        part = gbuf.at[rows(c, up, HALF, HALF)]
        fwd_p = push(part, part, prv)
        own_s.wait_recv()
        consume(oc, y)
        high_n.wait_recv()
        part = gbuf.at[rows(c, down)]
        sib_a = push(part, part, sib)
        low_p.wait_recv()
        part = gbuf.at[rows(c, up)]
        sib_b = push(part, part, sib)
        consume(c, down)
        consume(c, up)
        advance(jobs, 1)
        sib_a.wait_recv()
        consume(oc, down)
        sib_b.wait_recv()
        consume(oc, up)
        fwd_n.wait_recv()
        fwd_p.wait_recv()
        part = gbuf.at[rows(c, far)]
        sib_c = push(part, part, sib)
        consume(c, far)
        sib_c.wait_recv()
        consume(oc, far)

    if cfg.mid == "ln":
        vec = ref.vec
        pack_copies = [push(ref.pack, vec.at[shard], peer) for peer in peers]
        vec[shard] = ref.pack[...]
        first_weights = ship_columns(ref.raw_first, 0, ref.w_first, 3)
        for copy in pack_copies:
            copy.wait_recv()
        ref.vec_out[...] = vec[...]

        def full_vector(row):
            return jnp.concatenate(
                [vec[s, row : row + 1, :] for s in range(2 * RING)], axis=1
            ).astype(F32)

    ship_all()
    arriving = []
    jobs, job_sent, reduced = [], [], []
    if cfg.reduce:
        bufs = [getattr(ref, name) for name in REDUCE_NAMES]
        half = len(bufs) // 2
        jobs = [
            reduce_job(env, True, 0, ref.grads, ref.totals, bufs[:half], job_sent, reduced),
            reduce_job(env, False, 1, ref.grads, ref.totals, bufs[half:], job_sent, reduced),
        ]
        advance(jobs, 1)

    first = None
    if cfg.mid == "fin":
        first = gather_start(ref.grad_out[...])

    acc = None
    if cfg.rs:
        order = [far, up, down, y]
        lhs = ref.lhs
        chunks = []
        if cfg.swap_in:
            rowbuf = ref.rowbuf
            for q in order:
                chunks.append(push(lhs.at[rows(ox, q)], rowbuf.at[rows(xl, q)], xnb))
            mine = pl.ds(pl.multiple_of(xl * RING * BLK, BLK), RING * BLK)
            rowbuf[mine, :] = lhs[mine, :]
        else:
            rowbuf = lhs

        def partial(group, q):
            return jnp.dot(
                rowbuf[rows(group, q), :], ref.w_rs[...], preferred_element_type=F32
            )

        own, sib_out, sib_in = ref.own, ref.sib_out, ref.sib_in
        stage = ref.stage
        near_n, near_p, far_n, far_p = ref.near_n, ref.near_p, ref.far_n, ref.far_p
        low, high = pl.ds(0, HALF), pl.ds(HALF, HALF)
        ring = SimpleNamespace()
        passed = []

        def begin(slot):
            if chunks:
                chunks[slot].wait_recv()
            sib_out[slot] = partial(oc, order[slot]).astype(BF)
            passed.append(push(sib_out.at[slot], sib_in.at[slot], sib))
            own[slot] = partial(c, order[slot])

        def finish(slot):
            passed[slot].wait_recv()
            total = own[slot] + sib_in[slot].astype(F32)
            if slot == 0:
                stage[0] = total.astype(BF)
                ring.fn = push(stage.at[0, low], far_n, nxt)
                ring.fp = push(stage.at[0, high], far_p, prv)
            elif slot == 1:
                stage[1, high, :] = total[HALF:].astype(BF)
                ring.nh = push(stage.at[1, high], near_n.at[high], nxt)
                own[1, low, :] = total[:HALF]
            elif slot == 2:
                stage[2, low, :] = total[:HALF].astype(BF)
                ring.pl = push(stage.at[2, low], near_p.at[low], prv)
                own[2, high, :] = total[HALF:]
            else:
                own[3] = total

        begin(0)
        begin(1)
        finish(0)
        begin(2)
        finish(1)
        begin(3)
        finish(2)
        ring.fn.wait_recv()
        stage[1, low, :] = (own[1, low, :] + far_n[...].astype(F32)).astype(BF)
        ring.nl = push(stage.at[1, low], near_n.at[low], nxt)
        ring.fp.wait_recv()
        stage[2, high, :] = (own[2, high, :] + far_p[...].astype(F32)).astype(BF)
        ring.ph = push(stage.at[2, high], near_p.at[high], prv)
        finish(3)
        advance(jobs, 2)
        if cfg.swap_in:
            store(rowbuf, ref.rows_out)
        for copy in (ring.nh, ring.pl, ring.nl, ring.ph):
            copy.wait_recv()
        acc = own[3] + near_n[...].astype(F32) + near_p[...].astype(F32)

    block = None
    if cfg.mid == "ln":
        xhat, _ = norm_parts(ref.resid[...].astype(F32))
        block = (xhat * full_vector(0) + full_vector(2)).astype(BF)
    elif cfg.mid == "fwd":
        hidden = ref.resid[...].astype(F32) + (acc + ref.bias_rs[...])
        ref.hidden[...] = hidden
        xhat, _ = norm_parts(hidden)
        block = (xhat * ref.gain[...] + ref.shift[...]).astype(BF)
    elif cfg.mid == "fin":
        ref.hidden[...] = ref.resid[...].astype(F32) + (acc + ref.bias_rs[...])
    elif cfg.mid == "bwd":
        xhat, r = norm_parts(ref.resid[...].astype(F32))
        ref.g_gain[...] = jnp.sum(acc * xhat, axis=0, keepdims=True)
        ref.g_shift[...] = jnp.sum(acc, axis=0, keepdims=True)
        scaled = acc * ref.gain[...]
        grad = ref.stream[...].astype(F32) + r * (
            scaled
            - jnp.mean(scaled, axis=-1, keepdims=True)
            - xhat * jnp.mean(scaled * xhat, axis=-1, keepdims=True)
        )
        ref.hidden[...] = grad
        block = grad.astype(BF)

    if cfg.tail is not None:
        if first is None:
            first = gather_start(block)
        if cfg.mid == "ln":
            quarters = ship_quarters(first_weights)
            arriving.extend(copy for step in shipped for copy in ship_quarters(step))
            for copy in quarters:
                copy.wait_recv()
            store(ref.w_first, ref.w_qkv_first)
            weights = ref.w_first[...].reshape(WIDTH, 3 * BLK)
            q_row, v_row = vec[rank, 12:13, :].astype(F32), vec[rank, 14:15, :].astype(F32)
            bias_tail = jnp.concatenate([q_row, jnp.zeros_like(q_row), v_row], axis=1)
        else:
            arriving.extend(copy for step in shipped for copy in ship_quarters(step))
            weights = ref.w_ag
            bias_tail = ref.bias_ag[...] if hasattr(ref, "bias_ag") else None
        done = {}
        out_copies = []

        def consume(group, q):
            where = rows(group, q)
            value = jnp.dot(ref.gbuf[where, :], weights[...], preferred_element_type=F32)
            if cfg.tail == "up":
                pre = value + bias_tail
                ref.pre[where, :] = pre
                ref.active[where, :] = gelu(pre).astype(BF)
            elif cfg.tail == "dpre":
                ref.grad_pre[where, :] = (value * gelu_slope(ref.pre_in[where, :])).astype(BF)
            else:
                if cfg.tail == "qkv":
                    value = value + bias_tail
                pbuf, xbuf = ref.pbuf, ref.xbuf
                pbuf[where, :] = value.astype(BF)
                key = id(q)
                done[key] = done.get(key, 0) + 1
                if done[key] == 2:
                    out_copies.append(push(pbuf.at[rows(ox, q)], xbuf.at[rows(xl, q)], xnb))
                    xbuf[rows(xl, q), :] = pbuf[rows(xl, q), :]

        gather_rest(first, consume)
        store(ref.gbuf, ref.gathered)
        if cfg.swap_out:
            for copy in out_copies:
                copy.wait_recv()
            ref.att[...] = ref.xbuf[...]
    for copy in arriving:
        copy.wait_recv()
    if cfg.reduce:
        run_jobs(jobs)
        for copy in reduced:
            copy.wait()
    ship_rows_wait()
    for copy in sent + job_sent:
        copy.wait_send()
    for copy in local:
        copy.wait()


RANK_WIDTHS = dict(qkv=(8, 4, 32, 384), up=(8, 4, 32, 512), dense=(128, 1024), down=(512, 1024))


def comm_call(
    cid, *, mid, rs=False, swap_in=False, tail=None, ship=(), reduce=False, **operands
):
    swap_out = tail in ("qkv", "gctx")
    cfg = SimpleNamespace(
        rs=rs, swap_in=swap_in, swap_out=swap_out, mid=mid, tail=tail, ship=ship,
        reduce=reduce,
    )
    whole = pl.BlockSpec(memory_space=pltpu.VMEM)
    in_names = list(operands)
    operands = SimpleNamespace(**operands)
    total_rows = 2 * RING * BLK
    outs = SimpleNamespace()
    scratch = SimpleNamespace()
    flops = 0
    if rs:
        k = operands.lhs.shape[1]
        flops += 2 * total_rows * k * WIDTH
        if swap_in:
            outs.rows_out = ((total_rows, k), BF, pl.ANY)
            scratch.rowbuf = pltpu.VMEM((total_rows, k), BF)
        scratch.own = pltpu.VMEM((RING, BLK, WIDTH), F32)
        scratch.sib_out = pltpu.VMEM((RING, BLK, WIDTH), BF)
        scratch.sib_in = pltpu.VMEM((RING, BLK, WIDTH), BF)
        scratch.stage = pltpu.VMEM((3, BLK, WIDTH), BF)
        scratch.near_n = pltpu.VMEM((BLK, WIDTH), BF)
        scratch.near_p = pltpu.VMEM((BLK, WIDTH), BF)
        scratch.far_n = pltpu.VMEM((HALF, WIDTH), BF)
        scratch.far_p = pltpu.VMEM((HALF, WIDTH), BF)
    for kind, name, _, _ in ship:
        setattr(outs, "w_" + name, (RANK_WIDTHS[name], BF, pl.ANY))
    if mid == "ln":
        outs.w_qkv_first = (RANK_WIDTHS["qkv"], BF, pl.ANY)
        outs.vec_out = ((2 * RING,) + operands.pack.shape, BF, pltpu.VMEM)
        scratch.vec = pltpu.VMEM((2 * RING,) + operands.pack.shape, BF)
        scratch.w_first = pltpu.VMEM(RANK_WIDTHS["qkv"], BF)
    else:
        outs.hidden = ((BLK, WIDTH), F32, pltpu.VMEM)
    if mid == "bwd":
        outs.g_gain = ((1, WIDTH), F32, pltpu.VMEM)
        outs.g_shift = ((1, WIDTH), F32, pltpu.VMEM)
    if tail is not None:
        n = 3 * BLK if mid == "ln" else operands.w_ag.shape[1]
        flops += 2 * total_rows * n * WIDTH
        outs.gathered = ((total_rows, WIDTH), BF, pl.ANY)
        scratch.gbuf = pltpu.VMEM((total_rows, WIDTH), BF)
        if tail == "up":
            outs.pre = ((total_rows, n), F32, pltpu.VMEM)
            outs.active = ((total_rows, n), BF, pltpu.VMEM)
        elif tail == "dpre":
            outs.grad_pre = ((total_rows, n), BF, pltpu.VMEM)
        else:
            outs.att = ((total_rows, n), BF, pltpu.VMEM)
            scratch.pbuf = pltpu.VMEM((total_rows, n), BF)
            scratch.xbuf = pltpu.VMEM((total_rows, n), BF)
    if reduce:
        outs.totals = (operands.grads.shape, BF, pl.ANY)
        for name, shape in zip(REDUCE_NAMES, reduce_scratch() * 2):
            setattr(scratch, name, shape)
    scratch.send = pltpu.SemaphoreType.DMA((80 if ship else 32,))
    scratch.recv = pltpu.SemaphoreType.DMA((80 if ship else 32,))
    scratch.local = pltpu.SemaphoreType.DMA((12,))
    if ship:
        scratch.row_send = pltpu.SemaphoreType.DMA((2,))
        scratch.row_recv = pltpu.SemaphoreType.DMA((2,))
        scratch.row_local = pltpu.SemaphoreType.DMA((2,))
    results = pl.pallas_call(
        functools.partial(comm_kernel, cfg, in_names + list(vars(outs)) + list(vars(scratch))),
        out_shape=[jax.ShapeDtypeStruct(shape, dtype) for shape, dtype, _ in vars(outs).values()],
        in_specs=[
            pl.BlockSpec(memory_space=pl.ANY) if name.startswith("raw_") else whole
            for name in in_names
        ],
        out_specs=[pl.BlockSpec(memory_space=space) for _, _, space in vars(outs).values()],
        scratch_shapes=list(vars(scratch).values()),
        cost_estimate=pl.CostEstimate(flops=flops, bytes_accessed=20_000_000, transcendentals=0),
        compiler_params=pltpu.CompilerParams(
            collective_id=cid, has_side_effects=True, vmem_limit_bytes=CALL_VMEM
        ),
    )(*vars(operands).values())
    result = SimpleNamespace(**dict(zip(vars(outs), results)))
    for name in ("w_qkv", "w_up", "w_qkv_first"):
        if hasattr(result, name):
            weight = getattr(result, name)
            setattr(result, name, weight.reshape(WIDTH, weight.shape[3]))
    return result


QB = 256


def head_only(values, head):
    lane = lax.broadcasted_iota(jnp.int32, values.shape, 1)
    keep = (lane // 64) == head
    return jnp.where(keep, values, jnp.zeros_like(values))


def probs_of(q_pad, keys, slope, start):
    count = keys.shape[0]
    scores = lax.dot_general(
        keys, q_pad, (((1,), (1,)), ((), ())), preferred_element_type=F32
    )
    key_pos = lax.broadcasted_iota(jnp.int32, (count, QB), 0)
    query_pos = lax.broadcasted_iota(jnp.int32, (count, QB), 1) + start
    scores = scores + slope * key_pos.astype(F32)
    scores = jnp.where(key_pos <= query_pos, scores, -1000000000.0)
    top = jnp.max(scores, axis=0, keepdims=True)
    exponent = jnp.exp(scores - top)
    total = jnp.sum(exponent, axis=0, keepdims=True)
    return exponent * (1.0 / total)


def attention_fwd_kernel(slopes, qkv, ctx):
    value_t = qkv[:, 2 * BLK : 3 * BLK].astype(F32).T.astype(BF)
    for start in range(0, qkv.shape[0], QB):
        count = start + QB
        queries = qkv[start : start + QB, 0:BLK] * jnp.asarray(0.125, BF)
        keys = qkv[0:count, BLK : 2 * BLK]
        parts = []
        for head in range(2):
            probs = probs_of(head_only(queries, head), keys, slopes[head], start).astype(BF)
            ctx_t = jnp.dot(value_t[:, 0:count], probs, preferred_element_type=F32)
            parts.append(ctx_t[head * 64 : head * 64 + 64])
        ctx[start : start + QB, :] = jnp.concatenate(parts, axis=0).T.astype(BF)


def attention_bwd_kernel(slopes, qkv, gctx, dqkv, dk, dv):
    key_t = qkv[:, BLK : 2 * BLK].astype(F32).T.astype(BF)
    dk[...] = jnp.zeros_like(dk)
    dv[...] = jnp.zeros_like(dv)
    for start in range(0, qkv.shape[0], QB):
        count = start + QB
        queries = qkv[start : start + QB, 0:BLK] * jnp.asarray(0.125, BF)
        keys = qkv[0:count, BLK : 2 * BLK]
        values = qkv[0:count, 2 * BLK : 3 * BLK]
        grads = gctx[start : start + QB, :]
        parts = []
        for head in range(2):
            q_pad = head_only(queries, head)
            g_pad = head_only(grads, head)
            probs = probs_of(q_pad, keys, slopes[head], start)
            grad_probs = lax.dot_general(
                values, g_pad, (((1,), (1,)), ((), ())), preferred_element_type=F32
            )
            inner = jnp.sum(probs * grad_probs, axis=0, keepdims=True)
            grad_scores = (probs * (grad_probs - inner)).astype(BF)
            dk[0:count, :] += jnp.dot(grad_scores, q_pad, preferred_element_type=F32)
            dv[0:count, :] += jnp.dot(probs.astype(BF), g_pad, preferred_element_type=F32)
            dq_t = jnp.dot(key_t[:, 0:count], grad_scores, preferred_element_type=F32)
            parts.append(dq_t[head * 64 : head * 64 + 64] * 0.125)
        dqkv[start : start + QB, 0:BLK] = jnp.concatenate(parts, axis=0).T.astype(BF)
    dqkv[:, BLK : 2 * BLK] = dk[...].astype(BF)
    dqkv[:, 2 * BLK : 3 * BLK] = dv[...].astype(BF)


def attention_call(kernel, slopes, qkv, *more, width, scratch=()):
    whole = pl.BlockSpec(memory_space=pltpu.VMEM)
    return pl.pallas_call(
        kernel,
        out_shape=jax.ShapeDtypeStruct((qkv.shape[0], width), BF),
        in_specs=[pl.BlockSpec(memory_space=pltpu.SMEM), whole] + [whole] * len(more),
        out_specs=whole,
        scratch_shapes=list(scratch),
        cost_estimate=pl.CostEstimate(
            flops=4_000_000_000, bytes_accessed=2_000_000, transcendentals=2_000_000
        ),
        compiler_params=pltpu.CompilerParams(vmem_limit_bytes=CALL_VMEM),
    )(slopes, qkv, *more)


def attention_forward(slopes, qkv):
    return attention_call(attention_fwd_kernel, slopes, qkv, width=BLK)


def attention_backward(slopes, qkv, gctx):
    scratch = [pltpu.VMEM((qkv.shape[0], BLK), F32)] * 2
    return attention_call(
        attention_bwd_kernel, slopes, qkv, gctx, width=3 * BLK, scratch=scratch
    )


PIECE = 208
COLS = 512
LANES = 256


def neighbours():
    z, xh, c, xl, y = (lax.axis_index(name) for name in AXES)
    x = xh * 2 + xl

    def at_x(value):
        value = lax.rem(value, RING)
        return {"xh": value // 2, "xl": lax.rem(value, 2)}

    env = SimpleNamespace(z=z, xh=xh, c=c, xl=xl, y=y, x=x)
    env.x_next, env.x_prev = at_x(x + 1), at_x(x + 3)
    env.z_next, env.z_prev = {"z": lax.rem(z + 1, RING)}, {"z": lax.rem(z + 3, RING)}
    env.across, env.diagonal, env.sib = {"xh": 1 - xh}, {"xl": 1 - xl, "c": 1 - c}, {"c": 1 - c}
    env.mates = [(1 - c, y)]
    for dy in (2, 1, 3):
        env.mates += [(c, lax.rem(y + dy, RING)), (1 - c, lax.rem(y + dy, RING))]
    env.reduce_partners = [env.x_next, env.x_prev, env.z_next, env.z_prev, env.across, env.diagonal]
    env.reduce_partners += [{"c": core, "y": other} for core, other in env.mates]
    return env


def enter(partners):
    barrier = pltpu.get_barrier_semaphore()
    for partner in partners:
        pl.semaphore_signal(barrier, inc=1, device_id=partner, device_id_type=MESH)
    pl.semaphore_wait(barrier, len(partners))


def advance(jobs, steps):
    for _ in range(steps):
        for one in list(jobs):
            if next(one, 1) == 1:
                jobs.remove(one)


def run_jobs(jobs):
    while jobs:
        advance(jobs, 1)


def reduce_job(env, x_first, half, grads, out, bufs, sent, local):
    (far_n, far_p, near_n, near_p, stage_n, stage_p, total, far2_n, far2_p, near2_n, near2_p,
     stage2_n, stage2_p, summed, final_piece, final, send, recv, keep) = bufs
    c, xl, x, z = env.c, env.xl, env.x, env.z
    rank = c * RING + env.y
    lanes = pl.ds(half * LANES, LANES)
    count = [0]

    def push(src, dst, target):
        i = count[0]
        count[0] += 1
        copy = pltpu.make_async_remote_copy(
            src_ref=src, dst_ref=dst, send_sem=send.at[i], recv_sem=recv.at[i],
            device_id=target, device_id_type=MESH,
        )
        copy.start()
        sent.append(copy)
        return copy

    a, b = (x, z) if x_first else (z, x)
    a_next, a_prev = (env.x_next, env.x_prev) if x_first else (env.z_next, env.z_prev)
    b_next, b_prev = (env.z_next, env.z_prev) if x_first else (env.x_next, env.x_prev)

    def piece(index, start, size):
        if x_first:
            return grads.at[index, pl.ds(start, size), :, lanes]
        return grads.at[pl.ds(start, size), index, :, lanes]

    def load(view):
        return view[...].astype(F32)

    far, up, down = (lax.rem(a + d, RING) for d in (2, 1, 3))
    lo, hi = pl.ds(0, 2), pl.ds(2, 2)
    fn = push(piece(far, 0, 2), far_n, a_next)
    fp = push(piece(far, 2, 2), far_p, a_prev)
    nh = push(piece(up, 2, 2), near_n.at[hi], a_next)
    pl_ = push(piece(down, 0, 2), near_p.at[lo], a_prev)
    yield 0
    fn.wait_recv()
    stage_n[...] = (load(piece(up, 0, 2)) + far_n[...].astype(F32)).astype(BF)
    nl = push(stage_n, near_n.at[lo], a_next)
    fp.wait_recv()
    stage_p[...] = (load(piece(down, 2, 2)) + far_p[...].astype(F32)).astype(BF)
    ph = push(stage_p, near_p.at[hi], a_prev)
    yield 0
    yield 0
    for copy in (nh, pl_, nl, ph):
        copy.wait_recv()
    for q in range(RING):
        own = load(piece(a, q, 1))
        total[q] = (
            own.reshape(PIECE, LANES) + near_n[q].astype(F32) + near_p[q].astype(F32)
        ).astype(BF)

    far, up, down = (lax.rem(b + d, RING) for d in (2, 1, 3))
    cut = 96
    lo, hi = pl.ds(0, cut), pl.ds(cut, PIECE - cut)
    fn = push(total.at[far, lo], far2_n, b_next)
    fp = push(total.at[far, hi], far2_p, b_prev)
    nh = push(total.at[up, hi], near2_n.at[hi], b_next)
    pl_ = push(total.at[down, lo], near2_p.at[lo], b_prev)
    yield 0
    fn.wait_recv()
    stage2_n[...] = (total[up, lo, :].astype(F32) + far2_n[...].astype(F32)).astype(BF)
    nl = push(stage2_n, near2_n.at[lo], b_next)
    fp.wait_recv()
    stage2_p[...] = (total[down, hi, :].astype(F32) + far2_p[...].astype(F32)).astype(BF)
    ph = push(stage2_p, near2_p.at[hi], b_prev)
    yield 0
    for copy in (nh, pl_, nl, ph):
        copy.wait_recv()
    summed[...] = (
        total[b].astype(F32) + near2_n[...].astype(F32) + near2_p[...].astype(F32)
    ).astype(BF)

    def slot(number):
        return pl.ds(pl.multiple_of(number * 16, 16), 16)

    copies = [
        push(
            summed.at[slot(core * RING + other)], final_piece.at[slot(rank)],
            {"c": core, "y": other},
        )
        for core, other in env.mates
    ]
    final_piece[slot(rank), :] = summed[slot(rank), :]
    final_piece[2 * RING * 16 :, :] = summed[2 * RING * 16 :, :]
    yield 0
    for copy in copies:
        copy.wait_recv()

    trade = pltpu.make_async_remote_copy(
        src_ref=final_piece, dst_ref=final.at[x, z], send_sem=keep.at[0],
        recv_sem=keep.at[1], device_id=env.diagonal, device_id_type=MESH,
    )

    @pl.when(c != xl)
    def _():
        trade.start()

    @pl.when(c == xl)
    def _():
        final[x, z] = final_piece[...]

    yield 0

    @pl.when(c != xl)
    def _():
        trade.wait()

    mine, other = env.xh * 2 + c, (1 - env.xh) * 2 + c
    zn, zp, zf = (lax.rem(z + d, RING) for d in (1, 3, 2))

    def spread(first, second, target):
        view = final.at[first, second]
        return push(view, view, target)

    one_n = spread(mine, z, env.z_next)
    cross = spread(mine, z, env.across)
    one_p = spread(mine, z, env.z_prev)
    siblings = [spread(mine, z, env.sib)]
    yield 0
    cross.wait_recv()
    two_p = spread(other, z, env.z_prev)
    two_n = spread(other, z, env.z_next)
    siblings.append(spread(other, z, env.sib))
    yield 0
    one_n.wait_recv()
    fwd_n = spread(mine, zp, env.z_next)
    siblings.append(spread(mine, zp, env.sib))
    two_p.wait_recv()
    fwd_p = spread(other, zn, env.z_prev)
    siblings.append(spread(other, zn, env.sib))
    yield 0
    one_p.wait_recv()
    siblings.append(spread(mine, zn, env.sib))
    two_n.wait_recv()
    siblings.append(spread(other, zp, env.sib))
    yield 0
    fwd_n.wait_recv()
    siblings.append(spread(mine, zf, env.sib))
    fwd_p.wait_recv()
    siblings.append(spread(other, zf, env.sib))
    yield 0
    for copy in siblings:
        copy.wait_recv()
    back = pltpu.make_async_copy(final, out.at[:, :, :, lanes], keep.at[2])
    back.start()
    local.append(back)


def reduce_scratch():
    two, four = (2, PIECE, LANES), (4, PIECE, LANES)
    one, low, high = (PIECE, LANES), (96, LANES), (PIECE - 96, LANES)
    shapes = [two, two, four, four, two, two, four, low, high, one, one, low, high, one, one]
    return [pltpu.VMEM(shape, BF) for shape in shapes] + [
        pltpu.VMEM((RING, RING, PIECE, LANES), BF),
        pltpu.SemaphoreType.DMA((40,)),
        pltpu.SemaphoreType.DMA((40,)),
        pltpu.SemaphoreType.DMA((3,)),
    ]


REDUCE_NAMES = ["job%d" % i for i in range(38)]


def reduce_kernel(grads, out, *bufs):
    env = neighbours()
    enter(env.reduce_partners)
    sent, local = [], []
    half = len(bufs) // 2
    run_jobs(
        [
            reduce_job(env, True, 0, grads, out, bufs[:half], sent, local),
            reduce_job(env, False, 1, grads, out, bufs[half:], sent, local),
        ]
    )
    for copy in sent:
        copy.wait_send()
    for copy in local:
        copy.wait()


def reduce_call(cid, grads):
    return pl.pallas_call(
        reduce_kernel,
        out_shape=jax.ShapeDtypeStruct(grads.shape, BF),
        in_specs=[pl.BlockSpec(memory_space=pltpu.VMEM)],
        out_specs=pl.BlockSpec(memory_space=pl.ANY),
        scratch_shapes=reduce_scratch() * 2,
        compiler_params=pltpu.CompilerParams(
            collective_id=cid, has_side_effects=True, vmem_limit_bytes=CALL_VMEM
        ),
    )(grads)


def grads_kernel(input_a, dproj, input_b, grad_pre, context, grad_attn, active, grad_mlp, norms, out):
    rank = lax.axis_index("c") * RING + lax.axis_index("y")

    def product(left, right):
        return lax.dot_general(
            left, right, (((0,), (0,)), ((), ())), preferred_element_type=F32
        ).astype(BF)

    def column_sums(values):
        return jnp.sum(values.astype(F32), axis=0, keepdims=True)

    here = pl.ds(pl.multiple_of(rank * BLK, BLK), BLK)
    sums_p, sums_u = column_sums(dproj[...]), column_sums(grad_pre[...])
    rows = [sums_p[:, :BLK], sums_p[:, 2 * BLK :]]
    rows += [column_sums(grad_attn[:, here]), column_sums(grad_mlp[:, here])]
    rows += [sums_u[:, i * BLK : (i + 1) * BLK] for i in range(4)]
    vectors = jnp.concatenate(rows, axis=0)
    empty = jnp.zeros((16, BLK), BF)
    for t in range(2 * RING):
        cols = slice(t * BLK, (t + 1) * BLK)
        g_qkv = product(input_a[:, cols], dproj[...])
        g_up = product(input_b[:, cols], grad_pre[...])
        spare = jnp.concatenate(
            [jnp.where(rank == t, vectors, jnp.zeros_like(vectors)), norms[:, cols],
             jnp.zeros((4, BLK), F32)],
            axis=0,
        ).astype(BF)
        slot = slice(t * 16, t * 16 + 16)
        for i in range(8):
            x, zr = i // 2, i % 2
            part = slice(i * 16, i * 16 + 16)
            out[x, zr * 2, slot, 0:384] = g_qkv[part]
            out[x, zr * 2, slot, 384:512] = g_up[part, 0:128]
            out[x, zr * 2 + 1, slot, 0:384] = g_up[part, 128:512]
            out[x, zr * 2 + 1, slot, 384:512] = spare if i == 0 else empty
    g_dense = product(context[...], grad_attn[...])
    for i in range(8):
        x, zr = i // 2, i % 2
        g_down = product(active[:, i * 64 : i * 64 + 64], grad_mlp[...])
        for zc in range(2):
            lanes = slice(zc * COLS, zc * COLS + COLS)
            out[x, zr * 2 + zc, 128:144, :] = g_dense[i * 16 : i * 16 + 16, lanes]
            out[x, zr * 2 + zc, 144:208, :] = g_down[:, lanes]


def grads_call(*operands):
    whole = pl.BlockSpec(memory_space=pltpu.VMEM)
    return pl.pallas_call(
        grads_kernel,
        out_shape=jax.ShapeDtypeStruct((RING, RING, PIECE, COLS), BF),
        in_specs=[whole] * len(operands),
        out_specs=whole,
        compiler_params=pltpu.CompilerParams(vmem_limit_bytes=CALL_VMEM),
    )(*operands)


def unpack_kernel(final0, final1, qkv, up, dense, down, spare):
    layer, x = pl.program_id(0), pl.program_id(1)

    def write(final):
        for zr in range(2):
            rows = slice(zr * 16, zr * 16 + 16)
            for k in range(2 * RING):
                slot = slice(k * 16, k * 16 + 16)
                left = final[0, zr * 2, slot, :].astype(F32)
                right = final[0, zr * 2 + 1, slot, :].astype(F32)
                for j in range(3):
                    at = j * WIDTH + k * BLK
                    qkv[0, rows, at : at + BLK] = left[:, j * BLK : (j + 1) * BLK]
                up[0, rows, k * 512 : k * 512 + 128] = left[:, 384:512]
                up[0, rows, k * 512 + 128 : k * 512 + 512] = right[:, 0:384]
            for zc in range(2):
                lanes = slice(zc * COLS, zc * COLS + COLS)
                dense[0, rows, lanes] = final[0, zr * 2 + zc, 128:144, :].astype(F32)
                down[0, zr * 64 : zr * 64 + 64, lanes] = final[0, zr * 2 + zc, 144:208, :].astype(F32)

        @pl.when(x == 0)
        def _():
            total = final[0, 1, 0:16, 384:512].astype(F32)
            for k in range(1, 2 * RING):
                total = total + final[0, 1, k * 16 : k * 16 + 16, 384:512].astype(F32)
            spare[0] = total

    @pl.when(layer == 0)
    def _():
        write(final0)

    @pl.when(layer == 1)
    def _():
        write(final1)


def unpack_call(final0, final1):
    layers = 2

    def block(index):
        def at(layer, x):
            return (jnp.where(layer == index, x, (RING - 1) * (1 - index)), 0, 0, 0)

        return pl.BlockSpec((1, RING, PIECE, COLS), at)

    def rows(count, width):
        return pl.BlockSpec((1, count, width), lambda layer, x: (layer, x, 0))

    return pl.pallas_call(
        unpack_kernel,
        grid=(layers, RING),
        out_shape=[
            jax.ShapeDtypeStruct((layers, BLK, 3 * WIDTH), F32),
            jax.ShapeDtypeStruct((layers, BLK, 4 * WIDTH), F32),
            jax.ShapeDtypeStruct((layers, BLK, WIDTH), F32),
            jax.ShapeDtypeStruct((layers, 4 * BLK, WIDTH), F32),
            jax.ShapeDtypeStruct((layers, 16, BLK), F32),
        ],
        in_specs=[block(0), block(1)],
        out_specs=[
            rows(32, 3 * WIDTH), rows(32, 4 * WIDTH), rows(32, WIDTH), rows(128, WIDTH),
            pl.BlockSpec((1, 16, BLK), lambda layer, x: (layer, 0, 0)),
        ],
        compiler_params=pltpu.CompilerParams(vmem_limit_bytes=CALL_VMEM),
    )(final0, final1)


def on_device(
    tokens,
    grad_out,
    slope_index,
    ln1_gain,
    ln1_bias,
    qkv_weight,
    q_bias,
    v_bias,
    dense_weight,
    dense_bias,
    ln2_gain,
    ln2_bias,
    up_weight,
    up_bias,
    down_weight,
    down_bias,
):
    layers = qkv_weight.shape[0]
    heads = slope_index.shape[0]
    rank = lax.axis_index("c") * RING + lax.axis_index("y")
    slopes_all = jnp.exp2(-8.0 * (slope_index.astype(F32) + 1.0) / heads)
    slopes = lax.dynamic_slice(slopes_all, (rank * 2,), (2,))

    pack = jnp.concatenate(
        [ln1_gain, ln1_bias, dense_bias, ln2_gain, ln2_bias, down_bias, q_bias, v_bias]
        + [up_bias.reshape(8, BLK), jnp.zeros((8, BLK), BF)]
    )
    step = comm_call(
        1, mid="ln", tail="qkv", resid=tokens, pack=pack, raw_first=qkv_weight,
        raw_up=up_weight, raw_dense=dense_weight,
        ship=(("cols", "up", 0, 1), ("rows", "dense", 0, 0)),
    )
    gathered = step.vec_out.astype(F32)
    ranked = lax.dynamic_index_in_dim(gathered, rank, 0, keepdims=False)
    gathered = gathered.transpose(1, 0, 2).reshape(gathered.shape[1], WIDTH)
    w_qkv, w_up, w_dense, w_down = [step.w_qkv_first], [step.w_up], [step.w_dense], []

    def vector(number, i):
        return gathered[number * layers + i][None, :]

    def bias_qkv(i):
        return jnp.concatenate([ranked[12 + i], jnp.zeros_like(ranked[0]), ranked[14 + i]])[None, :]

    def bias_up(i):
        return ranked[16 + 4 * i : 20 + 4 * i].reshape(1, 512)

    streams, mids, saved = [tokens], [], []
    output = None
    for i in range(layers):
        keep = SimpleNamespace(input_a=step.gathered, qkv=step.att)
        context = attention_forward(slopes, step.att)
        extra = {}
        if i == 0:
            extra = dict(
                ship=(("cols", "qkv", 1, 3), ("rows", "down", 0, 0)),
                raw_qkv=qkv_weight, raw_down=down_weight,
            )
        step = comm_call(
            2 + i, mid="fwd", rs=True, swap_in=True, tail="up", lhs=context, w_rs=w_dense[i],
            resid=streams[i], bias_rs=vector(2, i), gain=vector(3, i), shift=vector(4, i),
            w_ag=w_up[i], bias_ag=bias_up(i), **extra,
        )
        if i == 0:
            w_qkv.append(step.w_qkv)
            w_down.append(step.w_down)
        mids.append(step.hidden)
        vars(keep).update(
            context=step.rows_out, input_b=step.gathered, pre=step.pre,
            active=step.active,
        )
        saved.append(keep)
        if i + 1 < layers:
            step = comm_call(
                4, mid="fwd", rs=True, tail="qkv", lhs=step.active, w_rs=w_down[i],
                resid=mids[i], bias_rs=vector(5, i), gain=vector(0, i + 1),
                shift=vector(1, i + 1), w_ag=w_qkv[i + 1], bias_ag=bias_qkv(i + 1),
                ship=(("cols", "up", 1, 1), ("rows", "dense", 1, 0), ("rows", "down", 1, 0)),
                raw_up=up_weight, raw_dense=dense_weight, raw_down=down_weight,
            )
            w_up.append(step.w_up)
            w_dense.append(step.w_dense)
            w_down.append(step.w_down)
            streams.append(step.hidden)
        else:
            step = comm_call(
                5, mid="fin", rs=True, tail="dpre", lhs=step.active, w_rs=w_down[i],
                resid=mids[i], bias_rs=vector(5, i), grad_out=grad_out,
                w_ag=w_down[i].T, pre_in=keep.pre,
            )
            output = step.hidden

    grad_stream = grad_out
    packed = [None] * layers
    for i in reversed(range(layers)):
        keep = saved[i]
        grad_mlp, grad_pre = step.gathered, step.grad_pre
        extra = {} if i else dict(reduce=True, grads=packed[1])
        step = comm_call(
            7 - i, mid="bwd", rs=True, tail="gctx", lhs=grad_pre, w_rs=w_up[i].T,
            resid=mids[i], gain=vector(3, i), stream=grad_stream, w_ag=w_dense[i].T, **extra,
        )
        grad_after, grad_attn = step.hidden, step.gathered
        gain_b, shift_b = step.g_gain, step.g_shift
        if i == 0:
            final1 = step.totals
        dqkv = attention_backward(slopes, keep.qkv, step.att)
        if i:
            step = comm_call(
                8, mid="bwd", rs=True, swap_in=True, tail="dpre", lhs=dqkv, w_rs=w_qkv[i].T,
                resid=streams[i], gain=vector(0, i), stream=grad_after,
                w_ag=w_down[i - 1].T, pre_in=saved[i - 1].pre,
            )
        else:
            step = comm_call(
                9, mid="bwd", rs=True, swap_in=True, lhs=dqkv, w_rs=w_qkv[i].T,
                resid=streams[i], gain=vector(0, i), stream=grad_after,
            )
        grad_stream = step.hidden
        packed[i] = grads_call(
            keep.input_a, step.rows_out, keep.input_b, grad_pre, keep.context, grad_attn,
            keep.active, grad_mlp,
            jnp.concatenate([step.g_gain, step.g_shift, gain_b, shift_b]),
        )
    final0 = reduce_call(10, packed[0])
    g_qkv, g_up, g_dense, g_down, spare = unpack_call(final0, final1)
    return (
        output,
        grad_stream,
        spare[:, 8],
        spare[:, 9],
        g_qkv,
        spare[:, 0],
        spare[:, 1],
        g_dense,
        spare[:, 2],
        spare[:, 10],
        spare[:, 11],
        g_up,
        spare[:, 4:8].reshape(layers, -1),
        g_down,
        spare[:, 3],
    )


def solution(mesh):
    replica, shard = mesh.devices.shape
    fine = Mesh(mesh.devices.reshape(replica // 4, 2, 2, shard // RING, RING), AXES)
    rows = P(AXES, None)
    flat = P(None, ("xl", "y"))
    wide = P(None, ("xl", "y"), None)
    return jax.shard_map(
        on_device,
        mesh=fine,
        in_specs=(
            rows, rows, P(), flat, flat, wide, flat, flat, wide, flat, flat, flat, wide, flat,
            wide, flat,
        ),
        out_specs=(
            rows, rows, flat, flat, wide, flat, flat, wide, flat, flat, flat, wide, flat, wide,
            flat,
        ),
        check_vma=False,
    )
```

```python
import functools
from types import SimpleNamespace

import jax
import jax.numpy as jnp
from jax import lax
from jax.experimental import pallas as pl
from jax.experimental.pallas import tpu as pltpu
from jax.sharding import Mesh
from jax.sharding import PartitionSpec as P

eps = 1e-05
MESH = pl.DeviceIdType.MESH
AXES = ("z", "xh", "c", "xl", "y")
BF = jnp.bfloat16
F32 = jnp.float32
BLK = 128
HALF = 64
WIDTH = 1024
RING = 4
CALL_VMEM = 62 * 1024 * 1024


def norm_parts(values):
    average = jnp.mean(values, axis=-1, keepdims=True)
    centred = values - average
    variance = jnp.mean(centred * centred, axis=-1, keepdims=True)
    r = lax.rsqrt(variance + eps)
    return centred * r, r


PIECE = 208
COLS = 512
LANES = 256


def neighbours():
    z, xh, c, xl, y = (lax.axis_index(name) for name in AXES)
    x = xh * 2 + xl

    def at_x(value):
        value = lax.rem(value, RING)
        return {"xh": value // 2, "xl": lax.rem(value, 2)}

    env = SimpleNamespace(z=z, xh=xh, c=c, xl=xl, y=y, x=x)
    env.x_next, env.x_prev = at_x(x + 1), at_x(x + 3)
    env.z_next, env.z_prev = {"z": lax.rem(z + 1, RING)}, {"z": lax.rem(z + 3, RING)}
    env.across, env.diagonal, env.sib = {"xh": 1 - xh}, {"xl": 1 - xl, "c": 1 - c}, {"c": 1 - c}
    env.mates = [(1 - c, y)]
    for dy in (2, 1, 3):
        env.mates += [(c, lax.rem(y + dy, RING)), (1 - c, lax.rem(y + dy, RING))]
    env.reduce_partners = [env.x_next, env.x_prev, env.z_next, env.z_prev, env.across, env.diagonal]
    env.reduce_partners += [{"c": core, "y": other} for core, other in env.mates]
    return env


def enter(partners):
    barrier = pltpu.get_barrier_semaphore()
    for partner in partners:
        pl.semaphore_signal(barrier, inc=1, device_id=partner, device_id_type=MESH)
    pl.semaphore_wait(barrier, len(partners))


def advance(jobs, steps):
    for _ in range(steps):
        for one in list(jobs):
            if next(one, 1) == 1:
                jobs.remove(one)


def run_jobs(jobs):
    while jobs:
        advance(jobs, 1)


def reduce_job(env, x_first, half, grads, out, bufs, sent, local):
    (far_n, far_p, near_n, near_p, total, far2_n, far2_p, near2_n, near2_p,
     summed, final_piece, final, send, recv, keep) = bufs
    c, xl, x, z = env.c, env.xl, env.x, env.z
    rank = c * RING + env.y
    lanes = pl.ds(half * LANES, LANES)
    count = [0]

    def push(src, dst, target):
        i = count[0]
        count[0] += 1
        copy = pltpu.make_async_remote_copy(
            src_ref=src, dst_ref=dst, send_sem=send.at[i], recv_sem=recv.at[i],
            device_id=target, device_id_type=MESH,
        )
        copy.start()
        sent.append(copy)
        return copy

    a, b = (x, z) if x_first else (z, x)
    a_next, a_prev = (env.x_next, env.x_prev) if x_first else (env.z_next, env.z_prev)
    b_next, b_prev = (env.z_next, env.z_prev) if x_first else (env.x_next, env.x_prev)

    def piece(index, start, size):
        if x_first:
            return grads.at[index, pl.ds(start, size), :, lanes]
        return grads.at[pl.ds(start, size), index, :, lanes]

    def load(view):
        return view[...].astype(F32)

    far, up, down = (lax.rem(a + d, RING) for d in (2, 1, 3))
    lo, hi = pl.ds(0, 2), pl.ds(2, 2)
    fn = push(piece(far, 0, 2), far_n, a_next)
    fp = push(piece(far, 2, 2), far_p, a_prev)
    nh = push(piece(up, 2, 2), near_n.at[hi], a_next)
    pl_ = push(piece(down, 0, 2), near_p.at[lo], a_prev)
    yield 0
    fn.wait_recv()
    far_n[...] = (load(piece(up, 0, 2)) + far_n[...].astype(F32)).astype(BF)
    nl = push(far_n, near_n.at[lo], a_next)
    fp.wait_recv()
    far_p[...] = (load(piece(down, 2, 2)) + far_p[...].astype(F32)).astype(BF)
    ph = push(far_p, near_p.at[hi], a_prev)
    yield 0
    yield 0
    for copy in (nh, pl_, nl, ph):
        copy.wait_recv()
    for q in range(RING):
        own = load(piece(a, q, 1))
        total[q] = (
            own.reshape(PIECE, LANES) + near_n[q].astype(F32) + near_p[q].astype(F32)
        ).astype(BF)

    far, up, down = (lax.rem(b + d, RING) for d in (2, 1, 3))
    cut = 96
    lo, hi = pl.ds(0, cut), pl.ds(cut, PIECE - cut)
    fn = push(total.at[far, lo], far2_n, b_next)
    fp = push(total.at[far, hi], far2_p, b_prev)
    nh = push(total.at[up, hi], near2_n.at[hi], b_next)
    pl_ = push(total.at[down, lo], near2_p.at[lo], b_prev)
    yield 0
    fn.wait_recv()
    far2_n[...] = (total[up, lo, :].astype(F32) + far2_n[...].astype(F32)).astype(BF)
    nl = push(far2_n, near2_n.at[lo], b_next)
    fp.wait_recv()
    far2_p[...] = (total[down, hi, :].astype(F32) + far2_p[...].astype(F32)).astype(BF)
    ph = push(far2_p, near2_p.at[hi], b_prev)
    yield 0
    for copy in (nh, pl_, nl, ph):
        copy.wait_recv()
    summed[...] = (
        total[b].astype(F32) + near2_n[...].astype(F32) + near2_p[...].astype(F32)
    ).astype(BF)

    def slot(number):
        return pl.ds(pl.multiple_of(number * 16, 16), 16)

    copies = [
        push(
            summed.at[slot(core * RING + other)], final_piece.at[slot(rank)],
            {"c": core, "y": other},
        )
        for core, other in env.mates
    ]
    final_piece[slot(rank), :] = summed[slot(rank), :]
    final_piece[2 * RING * 16 :, :] = summed[2 * RING * 16 :, :]
    yield 0
    for copy in copies:
        copy.wait_recv()

    trade = pltpu.make_async_remote_copy(
        src_ref=final_piece, dst_ref=final.at[x, z], send_sem=keep.at[0],
        recv_sem=keep.at[1], device_id=env.diagonal, device_id_type=MESH,
    )

    @pl.when(c != xl)
    def _():
        trade.start()

    @pl.when(c == xl)
    def _():
        final[x, z] = final_piece[...]

    yield 0

    @pl.when(c != xl)
    def _():
        trade.wait()

    mine, other = env.xh * 2 + c, (1 - env.xh) * 2 + c
    zn, zp, zf = (lax.rem(z + d, RING) for d in (1, 3, 2))

    def spread(first, second, target):
        view = final.at[first, second]
        return push(view, view, target)

    one_n = spread(mine, z, env.z_next)
    cross = spread(mine, z, env.across)
    one_p = spread(mine, z, env.z_prev)
    siblings = [spread(mine, z, env.sib)]
    yield 0
    cross.wait_recv()
    two_p = spread(other, z, env.z_prev)
    two_n = spread(other, z, env.z_next)
    siblings.append(spread(other, z, env.sib))
    yield 0
    one_n.wait_recv()
    fwd_n = spread(mine, zp, env.z_next)
    siblings.append(spread(mine, zp, env.sib))
    two_p.wait_recv()
    fwd_p = spread(other, zn, env.z_prev)
    siblings.append(spread(other, zn, env.sib))
    yield 0
    one_p.wait_recv()
    siblings.append(spread(mine, zn, env.sib))
    two_n.wait_recv()
    siblings.append(spread(other, zp, env.sib))
    yield 0
    fwd_n.wait_recv()
    siblings.append(spread(mine, zf, env.sib))
    fwd_p.wait_recv()
    siblings.append(spread(other, zf, env.sib))
    yield 0
    for copy in siblings:
        copy.wait_recv()
    back = pltpu.make_async_copy(final, out.at[:, :, :, lanes], keep.at[2])
    back.start()
    local.append(back)


def reduce_scratch():
    two, four = (2, PIECE, LANES), (4, PIECE, LANES)
    one, low, high = (PIECE, LANES), (96, LANES), (PIECE - 96, LANES)
    shapes = [two, two, four, four, four, low, high, one, one, one, one]
    return [pltpu.VMEM(shape, BF) for shape in shapes] + [
        pltpu.VMEM((RING, RING, PIECE, LANES), BF),
        pltpu.SemaphoreType.DMA((40,)),
        pltpu.SemaphoreType.DMA((40,)),
        pltpu.SemaphoreType.DMA((3,)),
    ]


REDUCE_NAMES = ["job%d" % i for i in range(30)]


def reduce_kernel(grads, out, *bufs):
    env = neighbours()
    enter(env.reduce_partners)
    sent, local = [], []
    half = len(bufs) // 2
    run_jobs(
        [
            reduce_job(env, True, 0, grads, out, bufs[:half], sent, local),
            reduce_job(env, False, 1, grads, out, bufs[half:], sent, local),
        ]
    )
    for copy in sent:
        copy.wait_send()
    for copy in local:
        copy.wait()


def reduce_call(cid, grads):
    return pl.pallas_call(
        reduce_kernel,
        out_shape=jax.ShapeDtypeStruct(grads.shape, BF),
        in_specs=[pl.BlockSpec(memory_space=pltpu.VMEM)],
        out_specs=pl.BlockSpec(memory_space=pl.ANY),
        scratch_shapes=reduce_scratch() * 2,
        compiler_params=pltpu.CompilerParams(
            collective_id=cid, has_side_effects=True, vmem_limit_bytes=CALL_VMEM
        ),
    )(grads)


QB = 256


def head_only(values, head):
    lane = lax.broadcasted_iota(jnp.int32, values.shape, 1)
    keep = (lane // 64) == head
    return jnp.where(keep, values, jnp.zeros_like(values))


def probs_of(q_pad, keys, slope, start):
    count = keys.shape[0]
    scores = lax.dot_general(keys, q_pad, NT, preferred_element_type=F32)
    key_pos = lax.broadcasted_iota(jnp.int32, (count, QB), 0)
    query_pos = lax.broadcasted_iota(jnp.int32, (count, QB), 1) + start
    scores = scores + slope * key_pos.astype(F32)
    scores = jnp.where(key_pos <= query_pos, scores, -1000000000.0)
    top = jnp.max(scores, axis=0, keepdims=True)
    exponent = jnp.exp(scores - top)
    total = jnp.sum(exponent, axis=0, keepdims=True)
    return exponent * (1.0 / total)


def attention_forward(slopes, qkv, ctx):
    value_t = qkv[:, 2 * BLK : 3 * BLK].astype(F32).T.astype(BF)
    for start in range(0, qkv.shape[0], QB):
        count = start + QB
        queries = qkv[start : start + QB, 0:BLK] * jnp.asarray(0.125, BF)
        keys = qkv[0:count, BLK : 2 * BLK]
        parts = []
        for head in range(2):
            probs = probs_of(head_only(queries, head), keys, slopes[head], start).astype(BF)
            ctx_t = jnp.dot(value_t[:, 0:count], probs, preferred_element_type=F32)
            parts.append(ctx_t[head * 64 : head * 64 + 64])
        ctx[start : start + QB, :] = jnp.concatenate(parts, axis=0).T.astype(BF)


def attention_backward(slopes, qkv, gctx, dqkv, dk, dv):
    key_t = qkv[:, BLK : 2 * BLK].astype(F32).T.astype(BF)
    dk[...] = jnp.zeros_like(dk)
    dv[...] = jnp.zeros_like(dv)
    for start in range(0, qkv.shape[0], QB):
        count = start + QB
        queries = qkv[start : start + QB, 0:BLK] * jnp.asarray(0.125, BF)
        keys = qkv[0:count, BLK : 2 * BLK]
        values = qkv[0:count, 2 * BLK : 3 * BLK]
        grads = gctx[start : start + QB, :]
        parts = []
        for head in range(2):
            q_pad = head_only(queries, head)
            g_pad = head_only(grads, head)
            probs = probs_of(q_pad, keys, slopes[head], start)
            grad_probs = lax.dot_general(values, g_pad, NT, preferred_element_type=F32)
            inner = jnp.sum(probs * grad_probs, axis=0, keepdims=True)
            grad_scores = (probs * (grad_probs - inner)).astype(BF)
            dk[0:count, :] += jnp.dot(grad_scores, q_pad, preferred_element_type=F32)
            dv[0:count, :] += jnp.dot(probs.astype(BF), g_pad, preferred_element_type=F32)
            dq_t = jnp.dot(key_t[:, 0:count], grad_scores, preferred_element_type=F32)
            parts.append(dq_t[head * 64 : head * 64 + 64] * 0.125)
        dqkv[start : start + QB, 0:BLK] = jnp.concatenate(parts, axis=0).T.astype(BF)
    dqkv[:, BLK : 2 * BLK] = dk[...].astype(BF)
    dqkv[:, 2 * BLK : 3 * BLK] = dv[...].astype(BF)


def chain_kernel(names, *refs):
    ref = SimpleNamespace(**dict(zip(names, refs)))
    env = neighbours()
    z, c, xl, y = env.z, env.c, env.xl, env.y
    shard, rank = xl * RING + y, c * RING + y
    up, down, far = lax.rem(y + 1, RING), lax.rem(y + 3, RING), lax.rem(y + 2, RING)
    oc, ox = 1 - c, 1 - xl
    sib, nxt, prv, xnb = env.sib, {"y": up}, {"y": down}, {"xl": ox}
    plane = [
        (lax.rem(xl + dx, 2), lax.rem(y + dy, RING))
        for dx, dy in ((0, 2), (1, 2), (1, 1), (1, 3), (0, 1), (0, 3), (1, 0))
    ]
    peers = [{"xl": px, "y": py} for px, py in plane]
    z_far = {"z": lax.rem(z + 2, RING)}
    enter(peers + [z_far] + env.reduce_partners)

    sent, jobs, job_sent, reduced, fillers = [], [], [], [], []
    counts = SimpleNamespace(push=0, store=0)

    def push(src, dst, target, track=True):
        i = counts.push
        counts.push += 1
        copy = pltpu.make_async_remote_copy(
            src_ref=src, dst_ref=dst, send_sem=ref.send.at[i], recv_sem=ref.recv.at[i],
            device_id=target, device_id_type=MESH,
        )
        copy.start()
        if track:
            sent.append(copy)
        return copy

    def store(src, dst):
        copy = pltpu.make_async_copy(src, dst, ref.local.at[counts.store])
        counts.store += 1
        copy.start()
        return copy

    def work(amount):
        for _ in range(min(amount, len(fillers))):
            fillers.pop(0)()

    def rows(group, q, offset=0, size=BLK):
        return pl.ds(pl.multiple_of((group * RING + q) * BLK + offset, HALF), size)

    def ship_columns(raw, layer, dst, parts):
        per = dst.shape[3] // parts
        quarter = pl.ds(pl.multiple_of(z * dst.shape[2], dst.shape[2]), dst.shape[2])
        copies, keeps = [], []
        for j in range(parts):
            for (_, py), peer in zip(plane, peers):
                cols = pl.ds(pl.multiple_of((j * 2 * RING + c * RING + py) * per, per), per)
                copies.append(
                    push(raw.at[layer, quarter, cols], dst.at[shard, z, :, pl.ds(j * per, per)], peer)
                )
            cols = pl.ds(pl.multiple_of((j * 2 * RING + rank) * per, per), per)
            keeps.append(store(raw.at[layer, quarter, cols], dst.at[shard, z, :, pl.ds(j * per, per)]))
        return dst, copies, keeps

    def ship_quarters(step):
        dst, copies, keeps = step
        for copy in copies:
            copy.wait_recv()
        for copy in keeps:
            copy.wait()
        view = dst.at[:, z]
        return [push(view, view, target) for target in (env.z_next, env.z_prev, z_far)]

    def ship_rows(raw, layer, dst):
        i = counts.push
        counts.push += 1
        copy = pltpu.make_async_remote_copy(
            src_ref=raw.at[layer], dst_ref=dst, send_sem=ref.send.at[i], recv_sem=ref.recv.at[i],
            device_id=xnb, device_id_type=MESH,
        )
        keep = pltpu.make_async_copy(raw.at[layer], dst, ref.local.at[counts.store])
        counts.store += 1

        @pl.when(c == xl)
        def _():
            copy.start()
            keep.start()

        def finish():
            @pl.when(c == xl)
            def _():
                copy.wait_send()
                keep.wait()

            @pl.when(c != xl)
            def _():
                copy.wait_recv()

        return finish

    def wait_all(copies):
        for copy in copies:
            copy.wait_recv()

    def tall(weight):
        return weight[...].reshape(WIDTH, weight.shape[3])

    def gather_start(gbuf, block):
        own = rows(c, y)
        low, high = rows(c, y, 0, HALF), rows(c, y, HALF, HALF)
        gbuf[own, :] = block
        return [
            push(gbuf.at[low], gbuf.at[low], nxt),
            push(gbuf.at[high], gbuf.at[high], prv),
            push(gbuf.at[own], gbuf.at[own], sib),
            push(gbuf.at[high], gbuf.at[high], nxt),
            push(gbuf.at[low], gbuf.at[low], prv),
        ]

    def gather_rest(gbuf, first, consume):
        low_n, high_p, own_s, high_n, low_p = first
        if consume:
            consume(c, y)
        yield 0
        low_n.wait_recv()
        part = gbuf.at[rows(c, down, 0, HALF)]
        fwd_n = push(part, part, nxt)
        high_p.wait_recv()
        part = gbuf.at[rows(c, up, HALF, HALF)]
        fwd_p = push(part, part, prv)
        own_s.wait_recv()
        if consume:
            consume(oc, y)
        yield 0
        high_n.wait_recv()
        part = gbuf.at[rows(c, down)]
        sib_a = push(part, part, sib)
        low_p.wait_recv()
        part = gbuf.at[rows(c, up)]
        sib_b = push(part, part, sib)
        if consume:
            consume(c, down)
            consume(c, up)
            sib_a.wait_recv()
            consume(oc, down)
            sib_b.wait_recv()
            consume(oc, up)
        yield 0
        fwd_n.wait_recv()
        fwd_p.wait_recv()
        part = gbuf.at[rows(c, far)]
        sib_c = push(part, part, sib)
        if consume:
            consume(c, far)
        else:
            yield 0
            sib_a.wait_recv()
            sib_b.wait_recv()
        sib_c.wait_recv()
        if consume:
            consume(oc, far)

    def gather(gbuf, block, consume, between=None, fill=1):
        steps = gather_rest(gbuf, gather_start(gbuf, block), consume)
        if between:
            between()
        while next(steps, 1) == 0:
            advance(jobs, 1)
            work(fill)

    def swap_in(src, dst):
        copies = [push(src.at[rows(ox, q)], dst.at[rows(xl, q)], xnb, False) for q in order]
        mine = pl.ds(pl.multiple_of(xl * RING * BLK, BLK), RING * BLK)
        dst[mine, :] = src[mine, :]
        return copies

    def swap_out(src, dst, q):
        copy = push(src.at[rows(ox, q)], dst.at[rows(xl, q)], xnb, False)
        dst[rows(xl, q), :] = src[rows(xl, q), :]
        return copy

    def swap_done(copies):
        for copy in copies:
            copy.wait()

    order = [far, up, down, y]
    turn = [0]
    leaving = []

    def scatter(lhs, weight, dims, chunks=None, hook=None, fill=5):
        for copy in leaving:
            copy.wait_send()
        leaving.clear()
        which = turn[0] % 2
        turn[0] += 1
        own, sib_out, sib_in, stage = ref.own, ref.sib_out, ref.sib_in.at[which], ref.stage
        near_n, near_p = ref.near_n.at[which], ref.near_p.at[which]
        far_n, far_p = ref.far_n.at[which], ref.far_p.at[which]
        low, high = pl.ds(0, HALF), pl.ds(HALF, HALF)
        ring = SimpleNamespace()
        passed = []

        def leave(src, dst, target):
            copy = push(src, dst, target, False)
            leaving.append(copy)
            return copy

        def partial(group, q):
            return lax.dot_general(
                lhs[rows(group, q), :], weight(), dims, preferred_element_type=F32
            )

        def begin(slot):
            if chunks:
                chunks[slot].wait_recv()
            sib_out[slot] = partial(oc, order[slot]).astype(BF)
            passed.append(leave(sib_out.at[slot], sib_in.at[slot], sib))
            own[slot] = partial(c, order[slot])

        def finish(slot):
            passed[slot].wait_recv()
            total = own[slot] + sib_in[slot].astype(F32)
            if slot == 0:
                stage[0] = total.astype(BF)
                ring.fn = leave(stage.at[0, low], far_n, nxt)
                ring.fp = leave(stage.at[0, high], far_p, prv)
            elif slot == 1:
                stage[1, high, :] = total[HALF:].astype(BF)
                ring.nh = leave(stage.at[1, high], near_n.at[high], nxt)
                own[1, low, :] = total[:HALF]
            elif slot == 2:
                stage[2, low, :] = total[:HALF].astype(BF)
                ring.pl = leave(stage.at[2, low], near_p.at[low], prv)
                own[2, high, :] = total[HALF:]
            else:
                own[3] = total

        begin(0)
        begin(1)
        finish(0)
        begin(2)
        finish(1)
        begin(3)
        finish(2)
        finish(3)
        if hook:
            hook()
        ring.fn.wait_recv()
        stage[1, low, :] = (own[1, low, :] + far_n[...].astype(F32)).astype(BF)
        ring.nl = leave(stage.at[1, low], near_n.at[low], nxt)
        ring.fp.wait_recv()
        stage[2, high, :] = (own[2, high, :] + far_p[...].astype(F32)).astype(BF)
        ring.ph = leave(stage.at[2, high], near_p.at[high], prv)
        advance(jobs, 1)
        work(fill)
        for copy in (ring.nh, ring.pl, ring.nl, ring.ph):
            copy.wait_recv()
        if chunks:
            for copy in chunks:
                copy.wait_send()
        return own[3] + near_n[...].astype(F32) + near_p[...].astype(F32)

    def norm_back(dy, values, stream, layer, row, gain):
        xhat, r = norm_parts(values)
        sums = ref.norms.at[layer]
        sums[row : row + 1, :] = jnp.sum(dy * xhat, axis=0, keepdims=True)
        sums[row + 1 : row + 2, :] = jnp.sum(dy, axis=0, keepdims=True)
        scaled = dy * gain
        return stream + r * (
            scaled
            - jnp.mean(scaled, axis=-1, keepdims=True)
            - xhat * jnp.mean(scaled * xhat, axis=-1, keepdims=True)
        )

    def product(left, right):
        return lax.dot_general(left, right, TN, preferred_element_type=F32).astype(BF)

    def column_sums(values):
        return jnp.sum(values.astype(F32), axis=0, keepdims=True)

    def grads_of(layer):
        return ref.grads1 if layer else ref.grads0

    def fill_up(layer, t):
        out, g_up = grads_of(layer), product(
            ref.gather_b[layer, :, t * BLK : (t + 1) * BLK], ref.grad_pre[layer]
        )
        for i in range(8):
            x, zr, part = i // 2, i % 2, slice(i * 16, i * 16 + 16)
            out[x, zr * 2, t * 16 : t * 16 + 16, 384:512] = g_up[part, 0:128]
            out[x, zr * 2 + 1, t * 16 : t * 16 + 16, 0:384] = g_up[part, 128:512]

    def fill_qkv(layer, t):
        out, g_qkv = grads_of(layer), product(
            ref.gather_a[layer, :, t * BLK : (t + 1) * BLK], ref.dproj[layer]
        )
        for i in range(8):
            x, zr, part = i // 2, i % 2, slice(i * 16, i * 16 + 16)
            out[x, zr * 2, t * 16 : t * 16 + 16, 0:384] = g_qkv[part]

    def fill_down(layer, t):
        out = grads_of(layer)
        g_down = product(ref.active[layer, :, t * BLK : (t + 1) * BLK], ref.gather_m[layer])
        for half in range(2):
            i = t * 2 + half
            x, zr = i // 2, i % 2
            for zc in range(2):
                lanes = slice(zc * COLS, zc * COLS + COLS)
                out[x, zr * 2 + zc, 144:208, :] = g_down[half * 64 : half * 64 + 64, lanes]

    def fill_dense(layer):
        out = grads_of(layer)
        g_dense = product(ref.ctx_rows[layer], ref.gather_t[layer])
        for i in range(8):
            x, zr = i // 2, i % 2
            for zc in range(2):
                lanes = slice(zc * COLS, zc * COLS + COLS)
                out[x, zr * 2 + zc, 128:144, :] = g_dense[i * 16 : i * 16 + 16, lanes]

    def fill_spare(layer):
        out = grads_of(layer)
        here = pl.ds(pl.multiple_of(rank * BLK, BLK), BLK)
        sums_p, sums_u = column_sums(ref.dproj[layer]), column_sums(ref.grad_pre[layer])
        parts = [sums_p[:, :BLK], sums_p[:, 2 * BLK :]]
        parts += [column_sums(ref.gather_t[layer, :, here]), column_sums(ref.gather_m[layer, :, here])]
        parts += [sums_u[:, i * BLK : (i + 1) * BLK] for i in range(4)]
        vectors = jnp.concatenate(parts, axis=0)
        empty = jnp.zeros((16, BLK), BF)
        for t in range(2 * RING):
            spare = jnp.concatenate(
                [jnp.where(rank == t, vectors, jnp.zeros_like(vectors)),
                 ref.norms[layer, 0:4, t * BLK : (t + 1) * BLK], jnp.zeros((4, BLK), F32)],
                axis=0,
            ).astype(BF)
            for i in range(8):
                x, zr = i // 2, i % 2
                out[x, zr * 2 + 1, t * 16 : t * 16 + 16, 384:512] = spare if i == 0 else empty

    def queue(function, layer, amount):
        for t in range(amount):
            fillers.append(functools.partial(function, layer, t))

    vec = ref.vec
    pack_copies = [push(ref.pack, vec.at[shard], peer) for peer in peers]
    first_weights = ship_columns(ref.raw_qkv, 0, ref.w_qkv.at[0], 3)
    vec[shard] = ref.pack[...]
    wait_all(pack_copies)

    def vector(number, layer):
        row = number * 2 + layer
        return jnp.concatenate([vec[s, row : row + 1, :] for s in range(2 * RING)], axis=1).astype(F32)

    def rank_vector(row):
        return vec[rank, row : row + 1, :].astype(F32)

    def normed(values, number, layer):
        xhat, _ = norm_parts(values)
        return (xhat * vector(number, layer) + vector(number + 1, layer)).astype(BF)

    swaps = []

    def project(layer):
        done = []
        bias = jnp.concatenate(
            [rank_vector(12 + layer), jnp.zeros((1, BLK), F32), rank_vector(14 + layer)], axis=1
        )

        def consume(group, q):
            where = rows(group, q)
            value = jnp.dot(
                ref.gather_a[layer, where, :], tall(ref.w_qkv.at[layer]), preferred_element_type=F32
            )
            ref.pbuf[where, :] = (value + bias).astype(BF)
            if any(q is other for other in done):
                swaps.append(swap_out(ref.pbuf, ref.qkv.at[layer], q))
            done.append(q)

        return consume

    def lift(layer):
        bias = jnp.concatenate([rank_vector(16 + 4 * layer + i) for i in range(4)], axis=1)

        def consume(group, q):
            where = rows(group, q)
            pre = jnp.dot(
                ref.gather_b[layer, where, :], tall(ref.w_up.at[layer]), preferred_element_type=F32
            ) + bias
            sq = pre * pre
            t = jnp.tanh(0.7978845608028654 * (pre + 0.044715 * sq * pre))
            ref.active[layer, where, :] = (0.5 * pre * (1.0 + t)).astype(BF)
            ref.slope[layer, where, :] = (
                0.5 * (1.0 + t)
                + 0.5 * pre * (1.0 - t * t) * (0.7978845608028654 * (1.0 + 3.0 * 0.044715 * sq))
            ).astype(BF)

        return consume

    def lower(layer):
        def consume(group, q):
            where = rows(group, q)
            value = lax.dot_general(
                ref.gather_m[layer, where, :], ref.w_down[layer], NT, preferred_element_type=F32
            )
            ref.grad_pre[layer, where, :] = (value * ref.slope[layer, where, :].astype(F32)).astype(BF)

        return consume

    def spread_context(layer):
        done = []

        def consume(group, q):
            where = rows(group, q)
            value = lax.dot_general(
                ref.gather_t[layer, where, :], ref.w_dense[layer], NT, preferred_element_type=F32
            )
            ref.ctx[where, :] = value.astype(BF)
            if any(q is other for other in done):
                swaps.append(swap_out(ref.ctx, ref.gctx, q))
            done.append(q)

        return consume

    shipping = SimpleNamespace()

    def ship_a():
        shipping.quarters = ship_quarters(first_weights)
        shipping.up0 = ship_columns(ref.raw_up, 0, ref.w_up.at[0], 1)
        shipping.dense0 = ship_rows(ref.raw_dense, 0, ref.w_dense.at[0])
        wait_all(shipping.quarters)

    def ship_b():
        shipping.quarters = ship_quarters(shipping.up0)
        shipping.qkv1 = ship_columns(ref.raw_qkv, 1, ref.w_qkv.at[1], 3)

    def ship_c():
        shipping.down0 = ship_rows(ref.raw_down, 0, ref.w_down.at[0])

    def ship_d():
        wait_all(shipping.quarters)
        shipping.quarters = ship_quarters(shipping.qkv1)
        shipping.up1 = ship_columns(ref.raw_up, 1, ref.w_up.at[1], 1)
        shipping.dense1 = ship_rows(ref.raw_dense, 1, ref.w_dense.at[1])

    def ship_e():
        wait_all(shipping.quarters)
        shipping.quarters = ship_quarters(shipping.up1)
        shipping.down1 = ship_rows(ref.raw_down, 1, ref.w_down.at[1])

    gather(ref.gather_a.at[0], normed(ref.tokens[...].astype(F32), 0, 0), project(0), ship_a)
    ship_b()
    jobs.append(gather_rest(ref.gather_m.at[1], gather_start(ref.gather_m.at[1], ref.grad_out[...]), None))
    advance(jobs, 1)
    for layer in range(2):
        swap_done(swaps)
        swaps.clear()
        attention_forward(ref.slopes, ref.qkv.at[layer], ref.ctx)
        chunks = swap_in(ref.ctx, ref.ctx_rows.at[layer])
        if layer == 0:
            advance(jobs, 1)
            shipping.dense0()
        else:
            shipping.dense1()
        acc = scatter(
            ref.ctx_rows.at[layer], lambda: ref.w_dense[layer], NN, chunks,
            ship_c if layer == 0 else None,
        )
        stream = ref.tokens[...].astype(F32) if layer == 0 else ref.stream1[...]
        middle = stream + (acc + vector(2, layer))
        ref.middle[layer] = middle
        if layer == 0:
            wait_all(shipping.quarters)
            shipping.quarters = []
        gather(ref.gather_b.at[layer], normed(middle, 3, layer), lift(layer), ship_d if layer == 0 else None)
        if layer == 0:
            shipping.down0()
        else:
            run_jobs(jobs)
            shipping.down1()
            lower_rows = lower(1)
            for core in range(2):
                for q in range(RING):
                    fillers.append(functools.partial(lower_rows, core, q))
        acc = scatter(ref.active.at[layer], lambda: ref.w_down[layer], NN, None, None, 8)
        result = ref.middle[layer] + (acc + vector(5, layer))
        if layer == 0:
            ref.stream1[...] = result
            wait_all(shipping.quarters)
            shipping.quarters = []
            gather(ref.gather_a.at[1], normed(result, 0, 1), project(1), ship_e)
            wait_all(shipping.quarters)
        else:
            ref.output[...] = result

    grad = ref.grad_out[...].astype(F32)
    for layer in (1, 0):
        work(len(fillers))
        queue(fill_up, layer, 8)
        queue(fill_down, layer, 4)
        if layer:
            ref.kept[...] = grad
        acc = scatter(ref.grad_pre.at[layer], lambda: tall(ref.w_up.at[layer]), NT)
        grad = norm_back(acc, ref.middle[layer], ref.kept[...], layer, 2, vector(3, layer))
        ref.kept[...] = grad
        gather(ref.gather_t.at[layer], grad.astype(BF), spread_context(layer), None, 2)
        fillers.insert(0, functools.partial(fill_dense, layer))
        advance(jobs, 1)
        swap_done(swaps)
        swaps.clear()
        attention_backward(ref.slopes, ref.qkv.at[layer], ref.gctx, ref.pbuf, ref.dk, ref.dv)
        advance(jobs, 1)
        chunks = swap_in(ref.pbuf, ref.dproj.at[layer])
        queue(fill_qkv, layer, 8)
        acc = scatter(ref.dproj.at[layer], lambda: tall(ref.w_qkv.at[layer]), NT, chunks)
        values = ref.stream1[...] if layer else ref.tokens[...].astype(F32)
        grad = norm_back(acc, values, ref.kept[...], layer, 0, vector(0, layer))
        fillers.append(functools.partial(fill_spare, layer))
        if layer:
            ref.kept[...] = grad
            gather(ref.gather_m.at[0], grad.astype(BF), lower(0), None, 3)
            work(len(fillers))
            bufs = [getattr(ref, name) for name in REDUCE_NAMES]
            half = len(bufs) // 2
            for one in range(2):
                jobs.append(
                    reduce_job(
                        env, one == 0, one, ref.grads1, ref.totals,
                        bufs[one * half : one * half + half], job_sent, reduced,
                    )
                )
            advance(jobs, 1)
        else:
            ref.grad_tokens[...] = grad
    run_jobs(jobs)
    work(len(fillers))
    for copy in sent + leaving + job_sent:
        copy.wait_send()
    for copy in reduced:
        copy.wait()


NN = (((1,), (0,)), ((), ()))
NT = (((1,), (1,)), ((), ()))
TN = (((0,), (0,)), ((), ()))


def chain_call(cid, **operands):
    full, packed = 2 * RING * BLK, (RING, RING, PIECE, COLS)
    vmem = pltpu.VMEM
    outs = dict(
        output=((BLK, WIDTH), F32, vmem),
        grad_tokens=((BLK, WIDTH), F32, vmem),
        grads0=(packed, BF, vmem),
        totals=(packed, BF, pl.ANY),
    )
    scratch = dict(
        vec=vmem((2 * RING,) + operands["pack"].shape, BF),
        w_qkv=vmem((2, 8, 4, 32, 384), BF),
        w_up=vmem((2, 8, 4, 32, 512), BF),
        w_dense=vmem((2, BLK, WIDTH), BF),
        w_down=vmem((2, 512, WIDTH), BF),
        gather_a=vmem((2, full, WIDTH), BF),
        gather_b=vmem((2, full, WIDTH), BF),
        gather_m=vmem((2, full, WIDTH), BF),
        gather_t=vmem((2, full, WIDTH), BF),
        pbuf=vmem((full, 384), BF),
        qkv=vmem((2, full, 384), BF),
        ctx=vmem((full, BLK), BF),
        ctx_rows=vmem((2, full, BLK), BF),
        active=vmem((2, full, 512), BF),
        slope=vmem((2, full, 512), BF),
        grad_pre=vmem((2, full, 512), BF),
        gctx=vmem((full, BLK), BF),
        dproj=vmem((2, full, 384), BF),
        dk=vmem((full, BLK), F32),
        dv=vmem((full, BLK), F32),
        stream1=vmem((BLK, WIDTH), F32),
        middle=vmem((2, BLK, WIDTH), F32),
        kept=vmem((BLK, WIDTH), F32),
        norms=vmem((2, 8, WIDTH), F32),
        own=vmem((RING, BLK, WIDTH), F32),
        sib_out=vmem((RING, BLK, WIDTH), BF),
        sib_in=vmem((2, RING, BLK, WIDTH), BF),
        stage=vmem((3, BLK, WIDTH), BF),
        near_n=vmem((2, BLK, WIDTH), BF),
        near_p=vmem((2, BLK, WIDTH), BF),
        far_n=vmem((2, HALF, WIDTH), BF),
        far_p=vmem((2, HALF, WIDTH), BF),
        grads1=vmem(packed, BF),
        send=pltpu.SemaphoreType.DMA((320,)),
        recv=pltpu.SemaphoreType.DMA((320,)),
        local=pltpu.SemaphoreType.DMA((24,)),
    )
    scratch.update(zip(REDUCE_NAMES, reduce_scratch() * 2))

    def space(name):
        if name.startswith("raw_"):
            return pl.ANY
        return pltpu.SMEM if name == "slopes" else vmem

    results = pl.pallas_call(
        functools.partial(chain_kernel, list(operands) + list(outs) + list(scratch)),
        out_shape=[jax.ShapeDtypeStruct(shape, dtype) for shape, dtype, _ in outs.values()],
        in_specs=[pl.BlockSpec(memory_space=space(name)) for name in operands],
        out_specs=[pl.BlockSpec(memory_space=where) for _, _, where in outs.values()],
        scratch_shapes=list(scratch.values()),
        compiler_params=pltpu.CompilerParams(
            collective_id=cid, has_side_effects=True, vmem_limit_bytes=CALL_VMEM
        ),
    )(*operands.values())
    return results


def unpack_kernel(final0, final1, qkv, up, dense, down, spare):
    layer, x = pl.program_id(0), pl.program_id(1)

    def write(final):
        for zr in range(2):
            rows = slice(zr * 16, zr * 16 + 16)
            for k in range(2 * RING):
                slot = slice(k * 16, k * 16 + 16)
                left = final[0, zr * 2, slot, :].astype(F32)
                right = final[0, zr * 2 + 1, slot, :].astype(F32)
                for j in range(3):
                    at = j * WIDTH + k * BLK
                    qkv[0, rows, at : at + BLK] = left[:, j * BLK : (j + 1) * BLK]
                up[0, rows, k * 512 : k * 512 + 128] = left[:, 384:512]
                up[0, rows, k * 512 + 128 : k * 512 + 512] = right[:, 0:384]
            for zc in range(2):
                lanes = slice(zc * COLS, zc * COLS + COLS)
                dense[0, rows, lanes] = final[0, zr * 2 + zc, 128:144, :].astype(F32)
                down[0, zr * 64 : zr * 64 + 64, lanes] = final[0, zr * 2 + zc, 144:208, :].astype(F32)

        @pl.when(x == 0)
        def _():
            total = final[0, 1, 0:16, 384:512].astype(F32)
            for k in range(1, 2 * RING):
                total = total + final[0, 1, k * 16 : k * 16 + 16, 384:512].astype(F32)
            spare[0] = total

    @pl.when(layer == 0)
    def _():
        write(final0)

    @pl.when(layer == 1)
    def _():
        write(final1)


def unpack_call(final0, final1):
    layers = 2

    def block(index):
        def at(layer, x):
            return (jnp.where(layer == index, x, (RING - 1) * (1 - index)), 0, 0, 0)

        return pl.BlockSpec((1, RING, PIECE, COLS), at)

    def rows(count, width):
        return pl.BlockSpec((1, count, width), lambda layer, x: (layer, x, 0))

    return pl.pallas_call(
        unpack_kernel,
        grid=(layers, RING),
        out_shape=[
            jax.ShapeDtypeStruct((layers, BLK, 3 * WIDTH), F32),
            jax.ShapeDtypeStruct((layers, BLK, 4 * WIDTH), F32),
            jax.ShapeDtypeStruct((layers, BLK, WIDTH), F32),
            jax.ShapeDtypeStruct((layers, 4 * BLK, WIDTH), F32),
            jax.ShapeDtypeStruct((layers, 16, BLK), F32),
        ],
        in_specs=[block(0), block(1)],
        out_specs=[
            rows(32, 3 * WIDTH), rows(32, 4 * WIDTH), rows(32, WIDTH), rows(128, WIDTH),
            pl.BlockSpec((1, 16, BLK), lambda layer, x: (layer, 0, 0)),
        ],
        compiler_params=pltpu.CompilerParams(vmem_limit_bytes=CALL_VMEM),
    )(final0, final1)


def on_device(
    tokens,
    grad_out,
    slope_index,
    ln1_gain,
    ln1_bias,
    qkv_weight,
    q_bias,
    v_bias,
    dense_weight,
    dense_bias,
    ln2_gain,
    ln2_bias,
    up_weight,
    up_bias,
    down_weight,
    down_bias,
):
    layers = qkv_weight.shape[0]
    heads = slope_index.shape[0]
    rank = lax.axis_index("c") * RING + lax.axis_index("y")
    slopes_all = jnp.exp2(-8.0 * (slope_index.astype(F32) + 1.0) / heads)
    slopes = lax.dynamic_slice(slopes_all, (rank * 2,), (2,))

    pack = jnp.concatenate(
        [ln1_gain, ln1_bias, dense_bias, ln2_gain, ln2_bias, down_bias, q_bias, v_bias]
        + [up_bias.reshape(8, BLK), jnp.zeros((8, BLK), BF)]
    )
    output, grad_stream, grads0, final1 = chain_call(
        1, slopes=slopes, tokens=tokens, grad_out=grad_out, pack=pack, raw_qkv=qkv_weight,
        raw_up=up_weight, raw_dense=dense_weight, raw_down=down_weight,
    )
    final0 = reduce_call(2, grads0)
    g_qkv, g_up, g_dense, g_down, spare = unpack_call(final0, final1)
    return (
        output,
        grad_stream,
        spare[:, 8],
        spare[:, 9],
        g_qkv,
        spare[:, 0],
        spare[:, 1],
        g_dense,
        spare[:, 2],
        spare[:, 10],
        spare[:, 11],
        g_up,
        spare[:, 4:8].reshape(layers, -1),
        g_down,
        spare[:, 3],
    )


def solution(mesh):
    replica, shard = mesh.devices.shape
    fine = Mesh(mesh.devices.reshape(replica // 4, 2, 2, shard // RING, RING), AXES)
    rows = P(AXES, None)
    flat = P(None, ("xl", "y"))
    wide = P(None, ("xl", "y"), None)
    return jax.shard_map(
        on_device,
        mesh=fine,
        in_specs=(
            rows, rows, P(), flat, flat, wide, flat, flat, wide, flat, flat, flat, wide, flat,
            wide, flat,
        ),
        out_specs=(
            rows, rows, flat, flat, wide, flat, flat, wide, flat, flat, flat, wide, flat, wide,
            flat,
        ),
        check_vma=False,
    )
```

```python
import functools
from types import SimpleNamespace

import jax
import jax.numpy as jnp
from jax import lax
from jax.experimental import pallas as pl
from jax.experimental.pallas import tpu as pltpu
from jax.sharding import Mesh
from jax.sharding import PartitionSpec as P

eps = 1e-05
MESH = pl.DeviceIdType.MESH
AXES = ("z", "xh", "c", "xl", "y")
BF = jnp.bfloat16
F32 = jnp.float32
BLK = 128
HALF = 64
QUARTER = 32
WIDTH = 1024
RING = 4
CALL_VMEM = 63 * 1024 * 1024


def norm_parts(values):
    average = jnp.mean(values, axis=-1, keepdims=True)
    centred = values - average
    variance = jnp.mean(centred * centred, axis=-1, keepdims=True)
    r = lax.rsqrt(variance + eps)
    return centred * r, r


PIECE_M = 256
PIECE_A = 160
LANES = 128


def neighbours():
    z, xh, c, xl, y = (lax.axis_index(name) for name in AXES)
    x = xh * 2 + xl

    def at_x(value):
        value = lax.rem(value, RING)
        return {"xh": value // 2, "xl": lax.rem(value, 2)}

    env = SimpleNamespace(z=z, xh=xh, c=c, xl=xl, y=y, x=x)
    env.x_next, env.x_prev = at_x(x + 1), at_x(x + 3)
    env.z_next, env.z_prev = {"z": lax.rem(z + 1, RING)}, {"z": lax.rem(z + 3, RING)}
    env.across, env.diagonal, env.sib = {"xh": 1 - xh}, {"xl": 1 - xl, "c": 1 - c}, {"c": 1 - c}
    env.mates = [(1 - c, y)]
    for dy in (2, 1, 3):
        env.mates += [(c, lax.rem(y + dy, RING)), (1 - c, lax.rem(y + dy, RING))]
    env.reduce_partners = [env.x_next, env.x_prev, env.z_next, env.z_prev, env.across, env.diagonal]
    env.reduce_partners += [{"c": core, "y": other} for core, other in env.mates]
    return env


def enter(partners):
    barrier = pltpu.get_barrier_semaphore()
    for partner in partners:
        pl.semaphore_signal(barrier, inc=1, device_id=partner, device_id_type=MESH)
    pl.semaphore_wait(barrier, len(partners))


def advance(jobs, steps):
    for _ in range(steps):
        for one in list(jobs):
            if next(one, 1) == 1:
                jobs.remove(one)


def run_jobs(jobs):
    while jobs:
        advance(jobs, 1)


def reduce_job(env, x_first, half, grads, out, bufs, sent, local):
    piece_rows = grads.shape[2]
    (far_n, far_p, near_n, near_p, total, far2_n, far2_p, near2_n, near2_p,
     summed, final_piece, final, send, recv, keep) = bufs
    c, xl, x, z = env.c, env.xl, env.x, env.z
    rank = c * RING + env.y
    lanes = pl.ds(half * LANES, LANES)
    count = [0]

    def push(src, dst, target):
        i = count[0]
        count[0] += 1
        copy = pltpu.make_async_remote_copy(
            src_ref=src, dst_ref=dst, send_sem=send.at[i], recv_sem=recv.at[i],
            device_id=target, device_id_type=MESH,
        )
        copy.start()
        sent.append(copy)
        return copy

    a, b = (x, z) if x_first else (z, x)
    a_next, a_prev = (env.x_next, env.x_prev) if x_first else (env.z_next, env.z_prev)
    b_next, b_prev = (env.z_next, env.z_prev) if x_first else (env.x_next, env.x_prev)

    def piece(index, start, size):
        if x_first:
            return grads.at[index, pl.ds(start, size), :, lanes]
        return grads.at[pl.ds(start, size), index, :, lanes]

    def load(view):
        return view[...].astype(F32)

    far, up, down = (lax.rem(a + d, RING) for d in (2, 1, 3))
    lo, hi = pl.ds(0, 2), pl.ds(2, 2)
    fn = push(piece(far, 0, 2), far_n, a_next)
    fp = push(piece(far, 2, 2), far_p, a_prev)
    nh = push(piece(up, 2, 2), near_n.at[hi], a_next)
    pl_ = push(piece(down, 0, 2), near_p.at[lo], a_prev)
    yield 0
    fn.wait_recv()
    far_n[...] = (load(piece(up, 0, 2)) + far_n[...].astype(F32)).astype(BF)
    nl = push(far_n, near_n.at[lo], a_next)
    fp.wait_recv()
    far_p[...] = (load(piece(down, 2, 2)) + far_p[...].astype(F32)).astype(BF)
    ph = push(far_p, near_p.at[hi], a_prev)
    yield 0
    yield 0
    for copy in (nh, pl_, nl, ph):
        copy.wait_recv()
    for q in range(RING):
        own = load(piece(a, q, 1))
        total[q] = (
            own.reshape(piece_rows, LANES) + near_n[q].astype(F32) + near_p[q].astype(F32)
        ).astype(BF)

    far, up, down = (lax.rem(b + d, RING) for d in (2, 1, 3))
    cut = piece_rows // 2
    lo, hi = pl.ds(0, cut), pl.ds(cut, cut)
    fn = push(total.at[far, lo], far2_n, b_next)
    fp = push(total.at[far, hi], far2_p, b_prev)
    nh = push(total.at[up, hi], near2_n.at[hi], b_next)
    pl_ = push(total.at[down, lo], near2_p.at[lo], b_prev)
    yield 0
    fn.wait_recv()
    far2_n[...] = (total[up, lo, :].astype(F32) + far2_n[...].astype(F32)).astype(BF)
    nl = push(far2_n, near2_n.at[lo], b_next)
    fp.wait_recv()
    far2_p[...] = (total[down, hi, :].astype(F32) + far2_p[...].astype(F32)).astype(BF)
    ph = push(far2_p, near2_p.at[hi], b_prev)
    yield 0
    for copy in (nh, pl_, nl, ph):
        copy.wait_recv()
    summed[...] = (
        total[b].astype(F32) + near2_n[...].astype(F32) + near2_p[...].astype(F32)
    ).astype(BF)

    def slot(number):
        return pl.ds(pl.multiple_of(number * 16, 16), 16)

    copies = [
        push(
            summed.at[slot(core * RING + other)], final_piece.at[slot(rank)],
            {"c": core, "y": other},
        )
        for core, other in env.mates
    ]
    final_piece[slot(rank), :] = summed[slot(rank), :]
    final_piece[2 * RING * 16 :, :] = summed[2 * RING * 16 :, :]
    yield 0
    for copy in copies:
        copy.wait_recv()

    trade = pltpu.make_async_remote_copy(
        src_ref=final_piece, dst_ref=final.at[x, z], send_sem=keep.at[0],
        recv_sem=keep.at[1], device_id=env.diagonal, device_id_type=MESH,
    )

    @pl.when(c != xl)
    def _():
        trade.start()

    @pl.when(c == xl)
    def _():
        final[x, z] = final_piece[...]

    yield 0

    @pl.when(c != xl)
    def _():
        trade.wait()

    mine, other = env.xh * 2 + c, (1 - env.xh) * 2 + c
    zn, zp, zf = (lax.rem(z + d, RING) for d in (1, 3, 2))

    def spread(first, second, target):
        view = final.at[first, second]
        return push(view, view, target)

    one_n = spread(mine, z, env.z_next)
    cross = spread(mine, z, env.across)
    one_p = spread(mine, z, env.z_prev)
    siblings = [spread(mine, z, env.sib)]
    yield 0
    cross.wait_recv()
    two_p = spread(other, z, env.z_prev)
    two_n = spread(other, z, env.z_next)
    siblings.append(spread(other, z, env.sib))
    yield 0
    one_n.wait_recv()
    fwd_n = spread(mine, zp, env.z_next)
    siblings.append(spread(mine, zp, env.sib))
    two_p.wait_recv()
    fwd_p = spread(other, zn, env.z_prev)
    siblings.append(spread(other, zn, env.sib))
    yield 0
    one_p.wait_recv()
    siblings.append(spread(mine, zn, env.sib))
    two_n.wait_recv()
    siblings.append(spread(other, zp, env.sib))
    yield 0
    fwd_n.wait_recv()
    siblings.append(spread(mine, zf, env.sib))
    fwd_p.wait_recv()
    siblings.append(spread(other, zf, env.sib))
    yield 0
    for copy in siblings:
        copy.wait_recv()
    back = pltpu.make_async_copy(final, out.at[:, :, :, lanes], keep.at[2])
    back.start()
    local.append(back)


def reduce_scratch(piece_rows):
    two, four = (2, piece_rows, LANES), (4, piece_rows, LANES)
    one, half = (piece_rows, LANES), (piece_rows // 2, LANES)
    shapes = [two, two, four, four, four, half, half, one, one, one, one]
    return [pltpu.VMEM(shape, BF) for shape in shapes] + [
        pltpu.VMEM((RING, RING, piece_rows, LANES), BF),
        pltpu.SemaphoreType.DMA((34,)),
        pltpu.SemaphoreType.DMA((34,)),
        pltpu.SemaphoreType.DMA((3,)),
    ]


REDUCE_NAMES = ["job%d" % i for i in range(60)]


QB = 256


def head_only(values, head):
    lane = lax.broadcasted_iota(jnp.int32, values.shape, 1)
    keep = (lane // 64) == head
    return jnp.where(keep, values, jnp.zeros_like(values))


def probs_of(q_pad, keys, slope, start):
    count = keys.shape[0]
    scores = lax.dot_general(keys, q_pad, NT, preferred_element_type=F32)
    key_pos = lax.broadcasted_iota(jnp.int32, (count, QB), 0)
    query_pos = lax.broadcasted_iota(jnp.int32, (count, QB), 1) + start
    scores = scores + slope * key_pos.astype(F32)
    scores = jnp.where(key_pos <= query_pos, scores, -1000000000.0)
    top = jnp.max(scores, axis=0, keepdims=True)
    exponent = jnp.exp(scores - top)
    total = jnp.sum(exponent, axis=0, keepdims=True)
    return exponent * (1.0 / total)


def attention_forward(slopes, qkv, ctx):
    value_t = qkv[:, 2 * BLK : 3 * BLK].astype(F32).T.astype(BF)
    for start in range(0, qkv.shape[0], QB):
        count = start + QB
        queries = qkv[start : start + QB, 0:BLK] * jnp.asarray(0.125, BF)
        keys = qkv[0:count, BLK : 2 * BLK]
        parts = []
        for head in range(2):
            probs = probs_of(head_only(queries, head), keys, slopes[head], start).astype(BF)
            ctx_t = jnp.dot(value_t[:, 0:count], probs, preferred_element_type=F32)
            parts.append(ctx_t[head * 64 : head * 64 + 64])
        ctx[start : start + QB, :] = jnp.concatenate(parts, axis=0).T.astype(BF)


def attention_backward(slopes, qkv, gctx, dqkv, dk, dv):
    key_t = qkv[:, BLK : 2 * BLK].astype(F32).T.astype(BF)
    dk[...] = jnp.zeros_like(dk)
    dv[...] = jnp.zeros_like(dv)
    for start in range(0, qkv.shape[0], QB):
        count = start + QB
        queries = qkv[start : start + QB, 0:BLK] * jnp.asarray(0.125, BF)
        keys = qkv[0:count, BLK : 2 * BLK]
        values = qkv[0:count, 2 * BLK : 3 * BLK]
        grads = gctx[start : start + QB, :]
        parts = []
        for head in range(2):
            q_pad = head_only(queries, head)
            g_pad = head_only(grads, head)
            probs = probs_of(q_pad, keys, slopes[head], start)
            grad_probs = lax.dot_general(values, g_pad, NT, preferred_element_type=F32)
            inner = jnp.sum(probs * grad_probs, axis=0, keepdims=True)
            grad_scores = (probs * (grad_probs - inner)).astype(BF)
            dk[0:count, :] += jnp.dot(grad_scores, q_pad, preferred_element_type=F32)
            dv[0:count, :] += jnp.dot(probs.astype(BF), g_pad, preferred_element_type=F32)
            dq_t = jnp.dot(key_t[:, 0:count], grad_scores, preferred_element_type=F32)
            parts.append(dq_t[head * 64 : head * 64 + 64] * 0.125)
        dqkv[start : start + QB, 0:BLK] = jnp.concatenate(parts, axis=0).T.astype(BF)
    dqkv[:, BLK : 2 * BLK] = dk[...].astype(BF)
    dqkv[:, 2 * BLK : 3 * BLK] = dv[...].astype(BF)


def chain_kernel(names, *refs):
    ref = SimpleNamespace(**dict(zip(names, refs)))
    env = neighbours()
    z, c, xl, y = env.z, env.c, env.xl, env.y
    shard, rank = xl * RING + y, c * RING + y
    up, down, far = lax.rem(y + 1, RING), lax.rem(y + 3, RING), lax.rem(y + 2, RING)
    oc, ox = 1 - c, 1 - xl
    sib, nxt, prv, xnb = env.sib, {"y": up}, {"y": down}, {"xl": ox}
    plane = [
        (lax.rem(xl + dx, 2), lax.rem(y + dy, RING))
        for dx, dy in ((0, 2), (1, 2), (1, 1), (1, 3), (0, 1), (0, 3), (1, 0))
    ]
    peers = [{"xl": px, "y": py} for px, py in plane]
    z_far = {"z": lax.rem(z + 2, RING)}
    enter(peers + [z_far] + env.reduce_partners)

    sent, jobs, fillers = [], [], []
    counts = SimpleNamespace(push=0, store=0)

    def push(src, dst, target, track=True):
        i = counts.push
        counts.push += 1
        copy = pltpu.make_async_remote_copy(
            src_ref=src, dst_ref=dst, send_sem=ref.send.at[i], recv_sem=ref.recv.at[i],
            device_id=target, device_id_type=MESH,
        )
        copy.start()
        if track:
            sent.append(copy)
        return copy

    def store(src, dst):
        copy = pltpu.make_async_copy(src, dst, ref.local.at[counts.store])
        counts.store += 1
        copy.start()
        return copy

    def work(amount):
        for _ in range(min(amount, len(fillers))):
            fillers.pop(0)()

    def tick(amount=2):
        advance(jobs, 1)
        work(amount)

    def run(*chains):
        live = list(chains)
        while live:
            advance(live, 1)
            tick()

    def rows(h, group, q, offset=0, size=HALF):
        start = h * 2 * RING * HALF + (group * RING + q) * HALF + offset
        return pl.ds(pl.multiple_of(start, QUARTER), size)

    def span(h, group):
        start = h * 2 * RING * HALF + group * RING * HALF
        return pl.ds(pl.multiple_of(start, HALF), RING * HALF)

    def places(h, group, q):
        return pl.ds(pl.multiple_of((group * RING + q) * BLK + h * HALF, HALF), HALF)

    def ship_columns(raw, layer, dst, parts):
        per = dst.shape[3] // parts
        quarter = pl.ds(pl.multiple_of(z * dst.shape[2], dst.shape[2]), dst.shape[2])
        copies, keeps = [], []
        for j in range(parts):
            for (_, py), peer in zip(plane, peers):
                cols = pl.ds(pl.multiple_of((j * 2 * RING + c * RING + py) * per, per), per)
                copies.append(
                    push(raw.at[layer, quarter, cols], dst.at[shard, z, :, pl.ds(j * per, per)], peer)
                )
            cols = pl.ds(pl.multiple_of((j * 2 * RING + rank) * per, per), per)
            keeps.append(store(raw.at[layer, quarter, cols], dst.at[shard, z, :, pl.ds(j * per, per)]))
        return dst, copies, keeps

    def ship_quarters(step):
        dst, copies, keeps = step
        for copy in copies:
            copy.wait_recv()
        for copy in keeps:
            copy.wait()
        view = dst.at[:, z]
        return [push(view, view, target) for target in (env.z_next, env.z_prev, z_far)]

    def ship_rows(raw, layer, dst):
        i = counts.push
        counts.push += 1
        copy = pltpu.make_async_remote_copy(
            src_ref=raw.at[layer], dst_ref=dst, send_sem=ref.send.at[i], recv_sem=ref.recv.at[i],
            device_id=xnb, device_id_type=MESH,
        )
        keep = pltpu.make_async_copy(raw.at[layer], dst, ref.local.at[counts.store])
        counts.store += 1

        @pl.when(c == xl)
        def _():
            copy.start()
            keep.start()

        def finish():
            @pl.when(c == xl)
            def _():
                copy.wait_send()
                keep.wait()

            @pl.when(c != xl)
            def _():
                copy.wait_recv()

        return finish

    def wait_all(copies):
        for copy in copies:
            copy.wait_recv()

    def tall(weight):
        return weight[...].reshape(WIDTH, weight.shape[3])

    def gather(gbuf, h, block):
        own = rows(h, c, y)
        low, high = rows(h, c, y, 0, QUARTER), rows(h, c, y, QUARTER, QUARTER)
        gbuf[own, :] = block
        low_n = push(gbuf.at[low], gbuf.at[low], nxt)
        high_p = push(gbuf.at[high], gbuf.at[high], prv)
        own_s = push(gbuf.at[own], gbuf.at[own], sib)
        high_n = push(gbuf.at[high], gbuf.at[high], nxt)
        low_p = push(gbuf.at[low], gbuf.at[low], prv)
        yield 0
        low_n.wait_recv()
        part = gbuf.at[rows(h, c, down, 0, QUARTER)]
        fwd_n = push(part, part, nxt)
        high_p.wait_recv()
        part = gbuf.at[rows(h, c, up, QUARTER, QUARTER)]
        fwd_p = push(part, part, prv)
        yield 0
        high_n.wait_recv()
        part = gbuf.at[rows(h, c, down)]
        sib_a = push(part, part, sib)
        low_p.wait_recv()
        part = gbuf.at[rows(h, c, up)]
        sib_b = push(part, part, sib)
        yield 0
        fwd_n.wait_recv()
        fwd_p.wait_recv()
        part = gbuf.at[rows(h, c, far)]
        sib_c = push(part, part, sib)
        own_s.wait_recv()
        sib_a.wait_recv()
        sib_b.wait_recv()
        yield 0
        sib_c.wait_recv()

    order = [far, up, down, y]

    def swap_in(src, dst, h):
        copies = [push(src.at[places(h, ox, q)], dst.at[rows(h, xl, q)], xnb, False) for q in order]
        for q in range(RING):
            dst[rows(h, xl, q), :] = src[places(h, xl, q), :]
        return copies

    swaps = []

    def swap_out(src, dst, h):
        for q in order:
            swaps.append(push(src.at[rows(h, ox, q)], dst.at[places(h, xl, q)], xnb, False))
        for q in range(RING):
            dst[places(h, xl, q), :] = src[rows(h, xl, q), :]

    def swap_done():
        for copy in swaps:
            copy.wait()
        swaps.clear()

    turn = [0, 0]
    leaving = [[], []]
    sums = [None, None]

    def scatter(h, lhs, weight, dims, chunks=()):
        for copy in leaving[h]:
            copy.wait_send()
        leaving[h].clear()
        which = turn[h] % 2
        turn[h] += 1
        own, sib_out, stage = ref.own.at[h], ref.sib_out.at[h], ref.stage.at[h]
        sib_in = ref.sib_in.at[which, h]
        near_n, near_p = ref.near_n.at[which, h], ref.near_p.at[which, h]
        far_n, far_p = ref.far_n.at[which, h], ref.far_p.at[which, h]
        low, high = pl.ds(0, QUARTER), pl.ds(QUARTER, QUARTER)

        def leave(src, dst, target):
            copy = push(src, dst, target, False)
            leaving[h].append(copy)
            return copy

        def block(q, offset=0, size=HALF):
            return pl.ds(pl.multiple_of(q * HALF + offset, QUARTER), size)

        for copy in chunks:
            copy.wait_recv()
        sib_out[...] = lax.dot_general(
            lhs[span(h, oc), :], weight(), dims, preferred_element_type=F32
        ).astype(BF)
        passed = leave(sib_out, sib_in, sib)
        own[...] = lax.dot_general(lhs[span(h, c), :], weight(), dims, preferred_element_type=F32)
        yield 0
        passed.wait_recv()
        stage[0] = (own[block(far), :] + sib_in[block(far), :].astype(F32)).astype(BF)
        fn = leave(stage.at[0, low], far_n, nxt)
        fp = leave(stage.at[0, high], far_p, prv)
        total = own[block(up), :] + sib_in[block(up), :].astype(F32)
        stage[1, high, :] = total[QUARTER:].astype(BF)
        nh = leave(stage.at[1, high], near_n.at[high], nxt)
        own[block(up, 0, QUARTER), :] = total[:QUARTER]
        total = own[block(down), :] + sib_in[block(down), :].astype(F32)
        stage[2, low, :] = total[:QUARTER].astype(BF)
        pl_ = leave(stage.at[2, low], near_p.at[low], prv)
        own[block(down, QUARTER, QUARTER), :] = total[QUARTER:]
        own[block(y), :] = own[block(y), :] + sib_in[block(y), :].astype(F32)
        yield 0
        fn.wait_recv()
        stage[1, low, :] = (own[block(up, 0, QUARTER), :] + far_n[...].astype(F32)).astype(BF)
        nl = leave(stage.at[1, low], near_n.at[low], nxt)
        fp.wait_recv()
        stage[2, high, :] = (
            own[block(down, QUARTER, QUARTER), :] + far_p[...].astype(F32)
        ).astype(BF)
        ph = leave(stage.at[2, high], near_p.at[high], prv)
        yield 0
        for copy in (nh, pl_, nl, ph):
            copy.wait_recv()
        for copy in chunks:
            copy.wait_send()
        sums[h] = own[block(y), :] + near_n[...].astype(F32) + near_p[...].astype(F32)

    def norm_back(dy, values, stream, layer, h, row, gain):
        xhat, r = norm_parts(values)
        kept = ref.norms.at[layer, h]
        kept[row : row + 1, :] = jnp.sum(dy * xhat, axis=0, keepdims=True)
        kept[row + 1 : row + 2, :] = jnp.sum(dy, axis=0, keepdims=True)
        scaled = dy * gain
        return stream + r * (
            scaled
            - jnp.mean(scaled, axis=-1, keepdims=True)
            - xhat * jnp.mean(scaled * xhat, axis=-1, keepdims=True)
        )

    def product(left, right):
        return lax.dot_general(left, right, TN, preferred_element_type=F32).astype(BF)

    def column_sums(values):
        return jnp.sum(values.astype(F32), axis=0, keepdims=True)

    def fill_up(layer, t):
        g_up = product(ref.gather_b[layer, :, t * BLK : (t + 1) * BLK], ref.grad_pre[layer])
        for i in range(8):
            x, zr, part = i // 2, i % 2, slice(i * 16, i * 16 + 16)
            for zc in range(2):
                ref.grads_m[layer, x, zr * 2 + zc, t * 16 : t * 16 + 16, :] = g_up[
                    part, zc * 256 : zc * 256 + 256
                ]

    def fill_qkv(layer, t):
        g_qkv = product(ref.gather_a[layer, :, t * BLK : (t + 1) * BLK], ref.dproj[layer])
        for i in range(8):
            x, zr, part = i // 2, i % 2, slice(i * 16, i * 16 + 16)
            ref.grads_a[layer, x, zr * 2, t * 16 : t * 16 + 16, :] = g_qkv[part, 0:256]
            ref.grads_a[layer, x, zr * 2 + 1, t * 16 : t * 16 + 16, 0:128] = g_qkv[part, 256:384]

    def fill_down(layer, t):
        g_down = product(ref.active[layer, :, t * BLK : (t + 1) * BLK], ref.gather_m[layer])
        for zr in range(2):
            for i in range(4):
                at = 128 + (i % 2) * 64
                ref.grads_m[layer, t, zr * 2 + i // 2, at : at + 64, :] = g_down[
                    zr * 64 : zr * 64 + 64, i * 256 : i * 256 + 256
                ]

    def fill_dense(layer):
        g_dense = product(ref.ctx_rows[layer], ref.gather_t[layer])
        for part in range(8):
            x, zr = part // 2, part % 2
            for i in range(4):
                at = 128 + (i % 2) * 16
                ref.grads_a[layer, x, zr * 2 + i // 2, at : at + 16, :] = g_dense[
                    part * 16 : part * 16 + 16, i * 256 : i * 256 + 256
                ]

    def fill_spare(layer):
        here = pl.ds(pl.multiple_of(rank * BLK, BLK), BLK)
        sums_p, sums_u = column_sums(ref.dproj[layer]), column_sums(ref.grad_pre[layer])
        parts = [sums_p[:, :BLK], sums_p[:, 2 * BLK :]]
        parts += [column_sums(ref.gather_t[layer, :, here]), column_sums(ref.gather_m[layer, :, here])]
        parts += [sums_u[:, i * BLK : (i + 1) * BLK] for i in range(4)]
        vectors = jnp.concatenate(parts, axis=0)
        empty = jnp.zeros((16, BLK), BF)
        for t in range(2 * RING):
            spare = jnp.concatenate(
                [jnp.where(rank == t, vectors, jnp.zeros_like(vectors)),
                 ref.norms[layer, 0, 0:4, t * BLK : (t + 1) * BLK]
                 + ref.norms[layer, 1, 0:4, t * BLK : (t + 1) * BLK],
                 jnp.zeros((4, BLK), F32)],
                axis=0,
            ).astype(BF)
            for i in range(8):
                x, zr = i // 2, i % 2
                ref.grads_a[layer, x, zr * 2 + 1, t * 16 : t * 16 + 16, 128:256] = (
                    spare if i == 0 else empty
                )

    vec = ref.vec
    pack_copies = [push(ref.pack, vec.at[shard], peer) for peer in peers]
    first_weights = ship_columns(ref.raw_qkv, 0, ref.w_qkv.at[0], 3)
    vec[shard] = ref.pack[...]
    wait_all(pack_copies)

    def vector(number, layer):
        row = number * 2 + layer
        return jnp.concatenate([vec[s, row : row + 1, :] for s in range(2 * RING)], axis=1).astype(F32)

    def rank_vector(row):
        return vec[rank, row : row + 1, :].astype(F32)

    def normed(values, number, layer):
        xhat, _ = norm_parts(values)
        return (xhat * vector(number, layer) + vector(number + 1, layer)).astype(BF)

    def project(layer, h):
        bias = jnp.concatenate(
            [rank_vector(12 + layer), jnp.zeros((1, BLK), F32), rank_vector(14 + layer)], axis=1
        )
        for group in range(2):
            where = span(h, group)
            value = jnp.dot(
                ref.gather_a[layer, where, :], tall(ref.w_qkv.at[layer]), preferred_element_type=F32
            )
            ref.pbuf[where, :] = (value + bias).astype(BF)
        swap_out(ref.pbuf, ref.qkv.at[layer], h)

    def lift(layer, h):
        bias = jnp.concatenate([rank_vector(16 + 4 * layer + i) for i in range(4)], axis=1)
        for group in range(4):
            where = pl.ds(h * 512 + group * BLK, BLK)
            pre = jnp.dot(
                ref.gather_b[layer, where, :], tall(ref.w_up.at[layer]), preferred_element_type=F32
            ) + bias
            sq = pre * pre
            t = jnp.tanh(0.7978845608028654 * (pre + 0.044715 * sq * pre))
            ref.active[layer, where, :] = (0.5 * pre * (1.0 + t)).astype(BF)
            ref.slope[layer, where, :] = (
                0.5 * (1.0 + t)
                + 0.5 * pre * (1.0 - t * t) * (0.7978845608028654 * (1.0 + 3.0 * 0.044715 * sq))
            ).astype(BF)

    def lower(layer, h):
        for group in range(2):
            where = span(h, group)
            value = lax.dot_general(
                ref.gather_m[layer, where, :], ref.w_down[layer], NT, preferred_element_type=F32
            )
            ref.grad_pre[layer, where, :] = (value * ref.slope[layer, where, :].astype(F32)).astype(BF)

    def spread_context(layer, h):
        for group in range(2):
            where = span(h, group)
            value = lax.dot_general(
                ref.gather_t[layer, where, :], ref.w_dense[layer], NT, preferred_element_type=F32
            )
            ref.ctx[where, :] = value.astype(BF)
        swap_out(ref.ctx, ref.gctx, h)

    shipping = SimpleNamespace()

    def ship_a():
        shipping.quarters = ship_quarters(first_weights)
        shipping.up0 = ship_columns(ref.raw_up, 0, ref.w_up.at[0], 1)
        shipping.dense0 = ship_rows(ref.raw_dense, 0, ref.w_dense.at[0])

    def ship_b():
        shipping.quarters = ship_quarters(shipping.up0)
        shipping.qkv1 = ship_columns(ref.raw_qkv, 1, ref.w_qkv.at[1], 3)

    def ship_c():
        shipping.down0 = ship_rows(ref.raw_down, 0, ref.w_down.at[0])

    def ship_d():
        wait_all(shipping.quarters)
        shipping.quarters = ship_quarters(shipping.qkv1)
        shipping.up1 = ship_columns(ref.raw_up, 1, ref.w_up.at[1], 1)
        shipping.dense1 = ship_rows(ref.raw_dense, 1, ref.w_dense.at[1])

    def ship_e():
        wait_all(shipping.quarters)
        shipping.quarters = ship_quarters(shipping.up1)
        shipping.down1 = ship_rows(ref.raw_down, 1, ref.w_down.at[1])

    used = [[], []]
    reduced = [[], []]
    through = []

    def reduce_unit(kind, layer):
        if layer == 0:
            while kind not in through:
                yield 0
            for copy in used[kind]:
                copy.wait_send()
            for copy in reduced[kind]:
                copy.wait()
            used[kind].clear()
            reduced[kind].clear()
            for partner in env.reduce_partners:
                pl.semaphore_signal(
                    ref.again.at[kind], inc=1, device_id=partner, device_id_type=MESH
                )
            yield 0
            pl.semaphore_wait(ref.again.at[kind], len(env.reduce_partners))
        grads = (ref.grads_a if kind else ref.grads_m).at[layer]
        out = (ref.totals_a if kind else ref.totals_m).at[layer]
        per = len(REDUCE_NAMES) // 4
        parts = []
        for one in range(2):
            at = (kind * 2 + one) * per
            bufs = [getattr(ref, name) for name in REDUCE_NAMES[at : at + per]]
            parts.append(
                reduce_job(env, one == 0, one, grads, out, bufs, used[kind], reduced[kind])
            )
        while parts:
            advance(parts, 1)
            yield 0
        through.append(kind)

    reached = {}

    def both(key, action):
        reached[key] = reached.get(key, 0) + 1
        if reached[key] == 2:
            action()

    def later(function, layer, amount):
        for t in range(amount):
            fillers.append(functools.partial(function, layer, t))

    def half(h):
        return pl.ds(h * HALF, HALF)

    def start_unit(kind, layer):
        def go():
            jobs.append(reduce_unit(kind, layer))

        return go

    def feed_gradients(layer):
        later(fill_up, layer, 8)
        later(fill_down, layer, 4)
        fillers.append(start_unit(0, layer))

    def first_phase(h):
        yield from gather(
            ref.gather_a.at[0], h, normed(ref.tokens[half(h), :].astype(F32), 0, 0)
        )
        if h == 0:
            wait_all(shipping.quarters)
        project(0, h)

    def forward_phase(layer, h, chunks):
        if h == 0:
            (shipping.dense1 if layer else shipping.dense0)()
        yield from scatter(h, ref.ctx_rows.at[layer], lambda: ref.w_dense[layer], NN, chunks)
        stream = ref.stream1[half(h), :] if layer else ref.tokens[half(h), :].astype(F32)
        middle = stream + (sums[h] + vector(2, layer))
        ref.middle[layer, half(h), :] = middle
        if layer == 0 and h == 0:
            ship_c()
        yield from gather(ref.gather_b.at[layer], h, normed(middle, 3, layer))
        if layer == 0 and h == 0:
            ship_d()
        lift(layer, h)
        if h == 0:
            (shipping.down1 if layer else shipping.down0)()
        yield from scatter(h, ref.active.at[layer], lambda: ref.w_down[layer], NN)
        result = ref.middle[layer, half(h), :] + (sums[h] + vector(5, layer))
        if layer == 0:
            ref.stream1[half(h), :] = result
            if h == 0:
                ship_e()
            yield from gather(ref.gather_a.at[1], h, normed(result, 0, 1))
            project(1, h)
        else:
            ref.output[half(h), :] = result
            lower(1, h)
            both(0, lambda: feed_gradients(1))
            yield from feed_back(1, h, ref.grad_out[half(h), :].astype(F32))

    def feed_back(layer, h, grad):
        yield from scatter(h, ref.grad_pre.at[layer], lambda: tall(ref.w_up.at[layer]), NT)
        grad = norm_back(
            sums[h], ref.middle[layer, half(h), :], grad, layer, h, 2, vector(3, layer)
        )
        ref.kept[half(h), :] = grad
        yield from gather(ref.gather_t.at[layer], h, grad.astype(BF))
        spread_context(layer, h)

    def backward_phase(layer, h, chunks):
        yield from scatter(
            h, ref.dproj.at[layer], lambda: tall(ref.w_qkv.at[layer]), NT, chunks
        )
        values = ref.stream1[half(h), :] if layer else ref.tokens[half(h), :].astype(F32)
        grad = norm_back(sums[h], values, ref.kept[half(h), :], layer, h, 0, vector(0, layer))

        def attention_gradients():
            later(fill_qkv, layer, 8)
            fillers.append(functools.partial(fill_spare, layer))
            fillers.append(start_unit(1, layer))

        both((1, layer), attention_gradients)
        if layer:
            yield from gather(ref.gather_m.at[0], h, grad.astype(BF))
            lower(0, h)
            both(2, lambda: feed_gradients(0))
            yield from feed_back(0, h, grad)
        else:
            ref.grad_tokens[half(h), :] = grad

    starts = [first_phase(h) for h in range(2)]
    advance(starts, 1)
    ship_a()
    run(*starts)
    ship_b()
    for h in range(2):
        jobs.append(gather(ref.gather_m.at[1], h, ref.grad_out[half(h), :]))
    advance(jobs, 1)
    for layer in range(2):
        swap_done()
        attention_forward(ref.slopes, ref.qkv.at[layer], ref.ctx)
        chunks = [swap_in(ref.ctx, ref.ctx_rows.at[layer], h) for h in range(2)]
        if layer:
            run_jobs(jobs)
        run(*[forward_phase(layer, h, chunks[h]) for h in range(2)])
        if layer == 0:
            wait_all(shipping.quarters)
    for layer in (1, 0):
        tick(2)
        swap_done()
        fillers.insert(0, functools.partial(fill_dense, layer))
        attention_backward(ref.slopes, ref.qkv.at[layer], ref.gctx, ref.pbuf, ref.dk, ref.dv)
        chunks = [swap_in(ref.pbuf, ref.dproj.at[layer], h) for h in range(2)]
        tick(2)
        run(*[backward_phase(layer, h, chunks[h]) for h in range(2)])
    work(len(fillers))
    run_jobs(jobs)
    for copy in sent + leaving[0] + leaving[1] + used[0] + used[1]:
        copy.wait_send()
    for copy in reduced[0] + reduced[1]:
        copy.wait()


NN = (((1,), (0,)), ((), ()))
NT = (((1,), (1,)), ((), ()))
TN = (((0,), (0,)), ((), ()))


def chain_call(cid, **operands):
    full = 2 * RING * BLK
    packed_m, packed_a = [(2, RING, RING, count, 256) for count in (PIECE_M, PIECE_A)]
    vmem = pltpu.VMEM
    outs = dict(
        output=((BLK, WIDTH), F32, vmem),
        grad_tokens=((BLK, WIDTH), F32, vmem),
        totals_m=(packed_m, BF, pl.ANY),
        totals_a=(packed_a, BF, pl.ANY),
    )
    scratch = dict(
        vec=vmem((2 * RING,) + operands["pack"].shape, BF),
        w_qkv=vmem((2, 8, 4, 32, 384), BF),
        w_up=vmem((2, 8, 4, 32, 512), BF),
        w_dense=vmem((2, BLK, WIDTH), BF),
        w_down=vmem((2, 512, WIDTH), BF),
        gather_a=vmem((2, full, WIDTH), BF),
        gather_b=vmem((2, full, WIDTH), BF),
        gather_m=vmem((2, full, WIDTH), BF),
        gather_t=vmem((2, full, WIDTH), BF),
        pbuf=vmem((full, 384), BF),
        qkv=vmem((2, full, 384), BF),
        ctx=vmem((full, BLK), BF),
        ctx_rows=vmem((2, full, BLK), BF),
        active=vmem((2, full, 512), BF),
        slope=vmem((2, full, 512), BF),
        grad_pre=vmem((2, full, 512), BF),
        gctx=vmem((full, BLK), BF),
        dproj=vmem((2, full, 384), BF),
        dk=vmem((full, BLK), F32),
        dv=vmem((full, BLK), F32),
        stream1=vmem((BLK, WIDTH), F32),
        middle=vmem((2, BLK, WIDTH), F32),
        kept=vmem((BLK, WIDTH), F32),
        norms=vmem((2, 2, 8, WIDTH), F32),
        own=vmem((2, RING * HALF, WIDTH), F32),
        sib_out=vmem((2, RING * HALF, WIDTH), BF),
        sib_in=vmem((2, 2, RING * HALF, WIDTH), BF),
        stage=vmem((2, 3, HALF, WIDTH), BF),
        near_n=vmem((2, 2, HALF, WIDTH), BF),
        near_p=vmem((2, 2, HALF, WIDTH), BF),
        far_n=vmem((2, 2, QUARTER, WIDTH), BF),
        far_p=vmem((2, 2, QUARTER, WIDTH), BF),
        grads_m=vmem(packed_m, BF),
        grads_a=vmem(packed_a, BF),
        again=pltpu.SemaphoreType.REGULAR((2,)),
        send=pltpu.SemaphoreType.DMA((450,)),
        recv=pltpu.SemaphoreType.DMA((450,)),
        local=pltpu.SemaphoreType.DMA((24,)),
    )
    scratch.update(zip(REDUCE_NAMES, reduce_scratch(PIECE_M) * 2 + reduce_scratch(PIECE_A) * 2))

    def space(name):
        if name.startswith("raw_"):
            return pl.ANY
        return pltpu.SMEM if name == "slopes" else vmem

    results = pl.pallas_call(
        functools.partial(chain_kernel, list(operands) + list(outs) + list(scratch)),
        out_shape=[jax.ShapeDtypeStruct(shape, dtype) for shape, dtype, _ in outs.values()],
        in_specs=[pl.BlockSpec(memory_space=space(name)) for name in operands],
        out_specs=[pl.BlockSpec(memory_space=where) for _, _, where in outs.values()],
        scratch_shapes=list(scratch.values()),
        compiler_params=pltpu.CompilerParams(
            collective_id=cid, has_side_effects=True, vmem_limit_bytes=CALL_VMEM
        ),
    )(*operands.values())
    return results


def unpack_kernel(feed, attend, qkv, up, dense, down, spare):
    for zr in range(2):
        rows = slice(zr * 16, zr * 16 + 16)
        for zc in range(2):
            z = zr * 2 + zc
            for k in range(2 * RING):
                slot = slice(k * 16, k * 16 + 16)
                at = k * 512 + zc * 256
                up[0, rows, at : at + 256] = feed[0, 0, z, slot, :].astype(F32)
                part = attend[0, 0, z, slot, :].astype(F32)
                for j in range(2 - zc):
                    at = (zc * 2 + j) * WIDTH + k * BLK
                    qkv[0, rows, at : at + BLK] = part[:, j * BLK : (j + 1) * BLK]
            for i in range(2):
                at = zc * 512 + i * 256
                lanes = slice(at, at + 256)
                dense[0, rows, lanes] = attend[0, 0, z, 128 + i * 16 : 144 + i * 16, :].astype(F32)
                down[0, zr * 64 : zr * 64 + 64, lanes] = feed[
                    0, 0, z, 128 + i * 64 : 192 + i * 64, :
                ].astype(F32)

    @pl.when(pl.program_id(1) == 0)
    def _():
        total = attend[0, 0, 1, 0:16, 128:256].astype(F32)
        for k in range(1, 2 * RING):
            total = total + attend[0, 0, 1, k * 16 : k * 16 + 16, 128:256].astype(F32)
        spare[0] = total


def unpack_call(feed, attend):
    layers = 2

    def pieces(count):
        return pl.BlockSpec((1, 1, RING, count, 256), lambda layer, x: (layer, x, 0, 0, 0))

    def rows(count, width):
        return pl.BlockSpec((1, count, width), lambda layer, x: (layer, x, 0))

    return pl.pallas_call(
        unpack_kernel,
        grid=(layers, RING),
        out_shape=[
            jax.ShapeDtypeStruct((layers, BLK, 3 * WIDTH), F32),
            jax.ShapeDtypeStruct((layers, BLK, 4 * WIDTH), F32),
            jax.ShapeDtypeStruct((layers, BLK, WIDTH), F32),
            jax.ShapeDtypeStruct((layers, 4 * BLK, WIDTH), F32),
            jax.ShapeDtypeStruct((layers, 16, BLK), F32),
        ],
        in_specs=[pieces(PIECE_M), pieces(PIECE_A)],
        out_specs=[
            rows(32, 3 * WIDTH), rows(32, 4 * WIDTH), rows(32, WIDTH), rows(128, WIDTH),
            pl.BlockSpec((1, 16, BLK), lambda layer, x: (layer, 0, 0)),
        ],
        compiler_params=pltpu.CompilerParams(vmem_limit_bytes=CALL_VMEM),
    )(feed, attend)


def on_device(
    tokens,
    grad_out,
    slope_index,
    ln1_gain,
    ln1_bias,
    qkv_weight,
    q_bias,
    v_bias,
    dense_weight,
    dense_bias,
    ln2_gain,
    ln2_bias,
    up_weight,
    up_bias,
    down_weight,
    down_bias,
):
    layers = qkv_weight.shape[0]
    heads = slope_index.shape[0]
    rank = lax.axis_index("c") * RING + lax.axis_index("y")
    slopes_all = jnp.exp2(-8.0 * (slope_index.astype(F32) + 1.0) / heads)
    slopes = lax.dynamic_slice(slopes_all, (rank * 2,), (2,))

    pack = jnp.concatenate(
        [ln1_gain, ln1_bias, dense_bias, ln2_gain, ln2_bias, down_bias, q_bias, v_bias]
        + [up_bias.reshape(8, BLK), jnp.zeros((8, BLK), BF)]
    )
    output, grad_stream, feed, attend = chain_call(
        1, slopes=slopes, tokens=tokens, grad_out=grad_out, pack=pack, raw_qkv=qkv_weight,
        raw_up=up_weight, raw_dense=dense_weight, raw_down=down_weight,
    )
    g_qkv, g_up, g_dense, g_down, spare = unpack_call(feed, attend)
    return (
        output,
        grad_stream,
        spare[:, 8],
        spare[:, 9],
        g_qkv,
        spare[:, 0],
        spare[:, 1],
        g_dense,
        spare[:, 2],
        spare[:, 10],
        spare[:, 11],
        g_up,
        spare[:, 4:8].reshape(layers, -1),
        g_down,
        spare[:, 3],
    )


def solution(mesh):
    replica, shard = mesh.devices.shape
    fine = Mesh(mesh.devices.reshape(replica // 4, 2, 2, shard // RING, RING), AXES)
    rows = P(AXES, None)
    flat = P(None, ("xl", "y"))
    wide = P(None, ("xl", "y"), None)
    return jax.shard_map(
        on_device,
        mesh=fine,
        in_specs=(
            rows, rows, P(), flat, flat, wide, flat, flat, wide, flat, flat, flat, wide, flat,
            wide, flat,
        ),
        out_specs=(
            rows, rows, flat, flat, wide, flat, flat, wide, flat, flat, flat, wide, flat, wide,
            flat,
        ),
        check_vma=False,
    )
```

```python
import functools
from types import SimpleNamespace

import jax
import jax.numpy as jnp
from jax import lax
from jax.experimental import pallas as pl
from jax.experimental.pallas import tpu as pltpu
from jax.sharding import Mesh
from jax.sharding import PartitionSpec as P

eps = 1e-05
MESH = pl.DeviceIdType.MESH
AXES = ("z", "xh", "c", "xl", "y")
BF = jnp.bfloat16
F32 = jnp.float32
BLK = 128
HALF = 64
WIDTH = 1024
RING = 4
CALL_VMEM = 63 * 1024 * 1024


def norm_parts(values):
    average = jnp.mean(values, axis=-1, keepdims=True)
    centred = values - average
    variance = jnp.mean(centred * centred, axis=-1, keepdims=True)
    r = lax.rsqrt(variance + eps)
    return centred * r, r


PIECE = 208
COLS = 512
LANES = 256


def neighbours():
    z, xh, c, xl, y = (lax.axis_index(name) for name in AXES)
    x = xh * 2 + xl

    def at_x(value):
        value = lax.rem(value, RING)
        return {"xh": value // 2, "xl": lax.rem(value, 2)}

    env = SimpleNamespace(z=z, xh=xh, c=c, xl=xl, y=y, x=x)
    env.x_next, env.x_prev = at_x(x + 1), at_x(x + 3)
    env.z_next, env.z_prev = {"z": lax.rem(z + 1, RING)}, {"z": lax.rem(z + 3, RING)}
    env.z_far = {"z": lax.rem(z + 2, RING)}
    env.across, env.diagonal, env.sib = {"xh": 1 - xh}, {"xl": 1 - xl, "c": 1 - c}, {"c": 1 - c}
    env.mates = [(1 - c, y)]
    for dy in (2, 1, 3):
        env.mates += [(c, lax.rem(y + dy, RING)), (1 - c, lax.rem(y + dy, RING))]
    env.reduce_partners = [env.x_next, env.x_prev, env.z_next, env.z_prev, env.z_far]
    env.reduce_partners += [env.across, env.diagonal]
    env.reduce_partners += [{"c": core, "y": other} for core, other in env.mates]
    return env


def enter(partners):
    barrier = pltpu.get_barrier_semaphore()
    for partner in partners:
        pl.semaphore_signal(barrier, inc=1, device_id=partner, device_id_type=MESH)
    pl.semaphore_wait(barrier, len(partners))


def advance(jobs, steps):
    for _ in range(steps):
        for one in list(jobs):
            if next(one, 1) == 1:
                jobs.remove(one)


def run_jobs(jobs):
    while jobs:
        advance(jobs, 1)


def reduce_job(env, x_first, half, grads, out, bufs, sent, local):
    (far_n, far_p, near_n, near_p, total, far2_n, far2_p, near2_n, near2_p,
     summed, final_piece, final, send, recv, keep) = bufs
    c, xl, x, z = env.c, env.xl, env.x, env.z
    rank = c * RING + env.y
    lanes = pl.ds(half * LANES, LANES)
    count = [0]

    def push(src, dst, target):
        i = count[0]
        count[0] += 1
        copy = pltpu.make_async_remote_copy(
            src_ref=src, dst_ref=dst, send_sem=send.at[i], recv_sem=recv.at[i],
            device_id=target, device_id_type=MESH,
        )
        copy.start()
        sent.append(copy)
        return copy

    a, b = (x, z) if x_first else (z, x)
    a_next, a_prev = (env.x_next, env.x_prev) if x_first else (env.z_next, env.z_prev)
    b_next, b_prev = (env.z_next, env.z_prev) if x_first else (env.x_next, env.x_prev)

    def piece(index, start, size):
        if x_first:
            return grads.at[index, pl.ds(start, size), :, lanes]
        return grads.at[pl.ds(start, size), index, :, lanes]

    def load(view):
        return view[...].astype(F32)

    far, up, down = (lax.rem(a + d, RING) for d in (2, 1, 3))
    lo, hi = pl.ds(0, 2), pl.ds(2, 2)
    fn = push(piece(far, 0, 2), far_n, a_next)
    fp = push(piece(far, 2, 2), far_p, a_prev)
    nh = push(piece(up, 2, 2), near_n.at[hi], a_next)
    pl_ = push(piece(down, 0, 2), near_p.at[lo], a_prev)
    yield 0
    fn.wait_recv()
    far_n[...] = (load(piece(up, 0, 2)) + far_n[...].astype(F32)).astype(BF)
    nl = push(far_n, near_n.at[lo], a_next)
    fp.wait_recv()
    far_p[...] = (load(piece(down, 2, 2)) + far_p[...].astype(F32)).astype(BF)
    ph = push(far_p, near_p.at[hi], a_prev)
    yield 0
    yield 0
    for copy in (nh, pl_, nl, ph):
        copy.wait_recv()
    for q in range(RING):
        own = load(piece(a, q, 1))
        total[q] = (
            own.reshape(PIECE, LANES) + near_n[q].astype(F32) + near_p[q].astype(F32)
        ).astype(BF)

    far, up, down = (lax.rem(b + d, RING) for d in (2, 1, 3))
    cut = 96
    lo, hi = pl.ds(0, cut), pl.ds(cut, PIECE - cut)
    fn = push(total.at[far, lo], far2_n, b_next)
    fp = push(total.at[far, hi], far2_p, b_prev)
    nh = push(total.at[up, hi], near2_n.at[hi], b_next)
    pl_ = push(total.at[down, lo], near2_p.at[lo], b_prev)
    yield 0
    fn.wait_recv()
    far2_n[...] = (total[up, lo, :].astype(F32) + far2_n[...].astype(F32)).astype(BF)
    nl = push(far2_n, near2_n.at[lo], b_next)
    fp.wait_recv()
    far2_p[...] = (total[down, hi, :].astype(F32) + far2_p[...].astype(F32)).astype(BF)
    ph = push(far2_p, near2_p.at[hi], b_prev)
    yield 0
    for copy in (nh, pl_, nl, ph):
        copy.wait_recv()
    summed[...] = (
        total[b].astype(F32) + near2_n[...].astype(F32) + near2_p[...].astype(F32)
    ).astype(BF)

    def slot(number):
        return pl.ds(pl.multiple_of(number * 16, 16), 16)

    copies = [
        push(
            summed.at[slot(core * RING + other)], final_piece.at[slot(rank)],
            {"c": core, "y": other},
        )
        for core, other in env.mates
    ]
    final_piece[slot(rank), :] = summed[slot(rank), :]
    final_piece[2 * RING * 16 :, :] = summed[2 * RING * 16 :, :]
    yield 0
    for copy in copies:
        copy.wait_recv()

    trade = pltpu.make_async_remote_copy(
        src_ref=final_piece, dst_ref=final.at[x, z], send_sem=keep.at[0],
        recv_sem=keep.at[1], device_id=env.diagonal, device_id_type=MESH,
    )

    @pl.when(c != xl)
    def _():
        trade.start()

    @pl.when(c == xl)
    def _():
        final[x, z] = final_piece[...]

    yield 0

    @pl.when(c != xl)
    def _():
        trade.wait()

    mine, other = env.xh * 2 + c, (1 - env.xh) * 2 + c
    zn, zp, zf = (lax.rem(z + d, RING) for d in (1, 3, 2))

    def spread(first, second, target):
        view = final.at[first, second]
        return push(view, view, target)

    if not x_first:
        along = [spread(mine, z, target) for target in (env.z_far, env.z_next, env.z_prev)]
        yield 0
        yield 0
        for copy in along:
            copy.wait_recv()
        cross = push(final.at[mine], final.at[mine], env.across)
        siblings = [push(final.at[mine], final.at[mine], env.sib)]
        yield 0
        yield 0
        cross.wait_recv()
        siblings.append(push(final.at[other], final.at[other], env.sib))
        yield 0
        for copy in siblings:
            copy.wait_recv()
        back = pltpu.make_async_copy(final, out.at[:, :, :, lanes], keep.at[2])
        back.start()
        local.append(back)
        return

    one_n = spread(mine, z, env.z_next)
    cross = spread(mine, z, env.across)
    one_p = spread(mine, z, env.z_prev)
    siblings = [spread(mine, z, env.sib)]
    yield 0
    cross.wait_recv()
    two_p = spread(other, z, env.z_prev)
    two_n = spread(other, z, env.z_next)
    siblings.append(spread(other, z, env.sib))
    yield 0
    one_n.wait_recv()
    fwd_n = spread(mine, zp, env.z_next)
    siblings.append(spread(mine, zp, env.sib))
    two_p.wait_recv()
    fwd_p = spread(other, zn, env.z_prev)
    siblings.append(spread(other, zn, env.sib))
    yield 0
    one_p.wait_recv()
    siblings.append(spread(mine, zn, env.sib))
    two_n.wait_recv()
    siblings.append(spread(other, zp, env.sib))
    yield 0
    fwd_n.wait_recv()
    siblings.append(spread(mine, zf, env.sib))
    fwd_p.wait_recv()
    siblings.append(spread(other, zf, env.sib))
    yield 0
    for copy in siblings:
        copy.wait_recv()
    back = pltpu.make_async_copy(final, out.at[:, :, :, lanes], keep.at[2])
    back.start()
    local.append(back)


def reduce_scratch():
    two, four = (2, PIECE, LANES), (4, PIECE, LANES)
    one, low, high = (PIECE, LANES), (96, LANES), (PIECE - 96, LANES)
    shapes = [two, two, four, four, four, low, high, one, one, one, one]
    return [pltpu.VMEM(shape, BF) for shape in shapes] + [
        pltpu.VMEM((RING, RING, PIECE, LANES), BF),
        pltpu.SemaphoreType.DMA((40,)),
        pltpu.SemaphoreType.DMA((40,)),
        pltpu.SemaphoreType.DMA((3,)),
    ]


REDUCE_NAMES = ["job%d" % i for i in range(30)]


QB = 256


def head_only(values, head):
    lane = lax.broadcasted_iota(jnp.int32, values.shape, 1)
    keep = (lane // 64) == head
    return jnp.where(keep, values, jnp.zeros_like(values))


def probs_of(q_pad, keys, slope, start):
    count = keys.shape[0]
    scores = lax.dot_general(keys, q_pad, NT, preferred_element_type=F32)
    key_pos = lax.broadcasted_iota(jnp.int32, (count, QB), 0)
    query_pos = lax.broadcasted_iota(jnp.int32, (count, QB), 1) + start
    scores = scores + slope * key_pos.astype(F32)
    scores = jnp.where(key_pos <= query_pos, scores, -1000000000.0)
    top = jnp.max(scores, axis=0, keepdims=True)
    exponent = jnp.exp(scores - top)
    total = jnp.sum(exponent, axis=0, keepdims=True)
    return exponent * (1.0 / total)


def attention_forward(slopes, qkv, ctx):
    value_t = qkv[:, 2 * BLK : 3 * BLK].astype(F32).T.astype(BF)
    for start in range(0, qkv.shape[0], QB):
        count = start + QB
        queries = qkv[start : start + QB, 0:BLK] * jnp.asarray(0.125, BF)
        keys = qkv[0:count, BLK : 2 * BLK]
        parts = []
        for head in range(2):
            probs = probs_of(head_only(queries, head), keys, slopes[head], start).astype(BF)
            ctx_t = jnp.dot(value_t[:, 0:count], probs, preferred_element_type=F32)
            parts.append(ctx_t[head * 64 : head * 64 + 64])
        ctx[start : start + QB, :] = jnp.concatenate(parts, axis=0).T.astype(BF)


def attention_backward(slopes, qkv, gctx, dqkv, dk, dv):
    key_t = qkv[:, BLK : 2 * BLK].astype(F32).T.astype(BF)
    dk[...] = jnp.zeros_like(dk)
    dv[...] = jnp.zeros_like(dv)
    for start in range(0, qkv.shape[0], QB):
        count = start + QB
        queries = qkv[start : start + QB, 0:BLK] * jnp.asarray(0.125, BF)
        keys = qkv[0:count, BLK : 2 * BLK]
        values = qkv[0:count, 2 * BLK : 3 * BLK]
        grads = gctx[start : start + QB, :]
        parts = []
        for head in range(2):
            q_pad = head_only(queries, head)
            g_pad = head_only(grads, head)
            probs = probs_of(q_pad, keys, slopes[head], start)
            grad_probs = lax.dot_general(values, g_pad, NT, preferred_element_type=F32)
            inner = jnp.sum(probs * grad_probs, axis=0, keepdims=True)
            grad_scores = (probs * (grad_probs - inner)).astype(BF)
            dk[0:count, :] += jnp.dot(grad_scores, q_pad, preferred_element_type=F32)
            dv[0:count, :] += jnp.dot(probs.astype(BF), g_pad, preferred_element_type=F32)
            dq_t = jnp.dot(key_t[:, 0:count], grad_scores, preferred_element_type=F32)
            parts.append(dq_t[head * 64 : head * 64 + 64] * 0.125)
        dqkv[start : start + QB, 0:BLK] = jnp.concatenate(parts, axis=0).T.astype(BF)
    dqkv[:, BLK : 2 * BLK] = dk[...].astype(BF)
    dqkv[:, 2 * BLK : 3 * BLK] = dv[...].astype(BF)


VECTORS = (
    "ln1_gain", "ln1_bias", "dense_bias", "ln2_gain", "ln2_bias", "down_bias", "q_bias", "v_bias",
)


def chain_kernel(names, *refs):
    ref = SimpleNamespace(**dict(zip(names, refs)))
    env = neighbours()
    z, c, xl, y = env.z, env.c, env.xl, env.y
    shard, rank = xl * RING + y, c * RING + y
    up, down, far = lax.rem(y + 1, RING), lax.rem(y + 3, RING), lax.rem(y + 2, RING)
    oc, ox = 1 - c, 1 - xl
    sib, nxt, prv, xnb = env.sib, {"y": up}, {"y": down}, {"xl": ox}
    plane = [
        (lax.rem(xl + dx, 2), lax.rem(y + dy, RING))
        for dx, dy in ((0, 2), (1, 2), (1, 1), (1, 3), (0, 1), (0, 3), (1, 0))
    ]
    peers = [{"xl": px, "y": py} for px, py in plane]
    z_far = env.z_far
    enter(peers + env.reduce_partners)

    sent, jobs, job_sent, reduced, fillers = [], [], [], [], []
    counts = SimpleNamespace(push=0, store=0)

    def push(src, dst, target, track=True):
        i = counts.push
        counts.push += 1
        copy = pltpu.make_async_remote_copy(
            src_ref=src, dst_ref=dst, send_sem=ref.send.at[i], recv_sem=ref.recv.at[i],
            device_id=target, device_id_type=MESH,
        )
        copy.start()
        if track:
            sent.append(copy)
        return copy

    def store(src, dst):
        copy = pltpu.make_async_copy(src, dst, ref.local.at[counts.store])
        counts.store += 1
        copy.start()
        return copy

    def work(amount):
        for _ in range(min(amount, len(fillers))):
            fillers.pop(0)()

    def rows(group, q, offset=0, size=BLK):
        return pl.ds(pl.multiple_of((group * RING + q) * BLK + offset, HALF), size)

    def ship_columns(raw, layer, dst, parts):
        per = dst.shape[3] // parts
        quarter = pl.ds(pl.multiple_of(z * dst.shape[2], dst.shape[2]), dst.shape[2])
        copies, keeps = [], []
        for j in range(parts):
            for (_, py), peer in zip(plane, peers):
                cols = pl.ds(pl.multiple_of((j * 2 * RING + c * RING + py) * per, per), per)
                copies.append(
                    push(raw.at[layer, quarter, cols], dst.at[shard, z, :, pl.ds(j * per, per)], peer)
                )
            cols = pl.ds(pl.multiple_of((j * 2 * RING + rank) * per, per), per)
            keeps.append(store(raw.at[layer, quarter, cols], dst.at[shard, z, :, pl.ds(j * per, per)]))
        return dst, copies, keeps

    def ship_quarters(step):
        dst, copies, keeps = step
        for copy in copies:
            copy.wait_recv()
        for copy in keeps:
            copy.wait()
        view = dst.at[:, z]
        return [push(view, view, target) for target in (env.z_next, env.z_prev, z_far)]

    def ship_rows(raw, layer, dst):
        i = counts.push
        counts.push += 1
        copy = pltpu.make_async_remote_copy(
            src_ref=raw.at[layer], dst_ref=dst, send_sem=ref.send.at[i], recv_sem=ref.recv.at[i],
            device_id=xnb, device_id_type=MESH,
        )
        keep = pltpu.make_async_copy(raw.at[layer], dst, ref.local.at[counts.store])
        counts.store += 1

        @pl.when(c == xl)
        def _():
            copy.start()
            keep.start()

        def finish():
            @pl.when(c == xl)
            def _():
                copy.wait_send()
                keep.wait()

            @pl.when(c != xl)
            def _():
                copy.wait_recv()

        return finish

    def wait_all(copies):
        for copy in copies:
            copy.wait_recv()

    def tall(weight):
        return weight[...].reshape(WIDTH, weight.shape[3])

    def gather_start(gbuf, block):
        own = rows(c, y)
        low, high = rows(c, y, 0, HALF), rows(c, y, HALF, HALF)
        gbuf[own, :] = block
        return [
            push(gbuf.at[low], gbuf.at[low], nxt),
            push(gbuf.at[high], gbuf.at[high], prv),
            push(gbuf.at[own], gbuf.at[own], sib),
            push(gbuf.at[high], gbuf.at[high], nxt),
            push(gbuf.at[low], gbuf.at[low], prv),
        ]

    def gather_rest(gbuf, first, consume):
        low_n, high_p, own_s, high_n, low_p = first
        if consume:
            consume(c, y)
        yield 0
        low_n.wait_recv()
        part = gbuf.at[rows(c, down, 0, HALF)]
        fwd_n = push(part, part, nxt)
        high_p.wait_recv()
        part = gbuf.at[rows(c, up, HALF, HALF)]
        fwd_p = push(part, part, prv)
        own_s.wait_recv()
        if consume:
            consume(oc, y)
        yield 0
        high_n.wait_recv()
        part = gbuf.at[rows(c, down)]
        sib_a = push(part, part, sib)
        low_p.wait_recv()
        part = gbuf.at[rows(c, up)]
        sib_b = push(part, part, sib)
        if consume:
            consume(c, down)
            consume(c, up)
            sib_a.wait_recv()
            consume(oc, down)
            sib_b.wait_recv()
            consume(oc, up)
        yield 0
        fwd_n.wait_recv()
        fwd_p.wait_recv()
        part = gbuf.at[rows(c, far)]
        sib_c = push(part, part, sib)
        if consume:
            consume(c, far)
        else:
            yield 0
            sib_a.wait_recv()
            sib_b.wait_recv()
        sib_c.wait_recv()
        if consume:
            consume(oc, far)

    def gather(gbuf, block, consume, between=None, fill=1):
        steps = gather_rest(gbuf, gather_start(gbuf, block), consume)
        if between:
            between()
        while next(steps, 1) == 0:
            advance(jobs, 1)
            work(fill)

    def swap_in(src, dst):
        copies = [push(src.at[rows(ox, q)], dst.at[rows(xl, q)], xnb, False) for q in order]
        mine = pl.ds(pl.multiple_of(xl * RING * BLK, BLK), RING * BLK)
        dst[mine, :] = src[mine, :]
        return copies

    def swap_out(src, dst, q):
        copy = push(src.at[rows(ox, q)], dst.at[rows(xl, q)], xnb, False)
        dst[rows(xl, q), :] = src[rows(xl, q), :]
        return copy

    def swap_done(copies):
        for copy in copies:
            copy.wait()

    order = [far, up, down, y]
    turn = [0]
    leaving = []

    def scatter(lhs, weight, dims, chunks=None, hook=None, fill=5):
        for copy in leaving:
            copy.wait_send()
        leaving.clear()
        which = turn[0] % 2
        turn[0] += 1
        own, sib_out, sib_in, stage = ref.own, ref.sib_out, ref.sib_in.at[which], ref.stage
        near_n, near_p = ref.near_n.at[which], ref.near_p.at[which]
        far_n, far_p = ref.far_n.at[which], ref.far_p.at[which]
        low, high = pl.ds(0, HALF), pl.ds(HALF, HALF)
        ring = SimpleNamespace()
        passed = []

        def leave(src, dst, target):
            copy = push(src, dst, target, False)
            leaving.append(copy)
            return copy

        def partial(group, q):
            return lax.dot_general(
                lhs[rows(group, q), :], weight(), dims, preferred_element_type=F32
            )

        def begin(slot):
            if chunks:
                chunks[slot].wait_recv()
            sib_out[slot] = partial(oc, order[slot]).astype(BF)
            passed.append(leave(sib_out.at[slot], sib_in.at[slot], sib))
            own[slot] = partial(c, order[slot])

        def finish(slot):
            passed[slot].wait_recv()
            total = own[slot] + sib_in[slot].astype(F32)
            if slot == 0:
                stage[0] = total.astype(BF)
                ring.fn = leave(stage.at[0, low], far_n, nxt)
                ring.fp = leave(stage.at[0, high], far_p, prv)
            elif slot == 1:
                stage[1, high, :] = total[HALF:].astype(BF)
                ring.nh = leave(stage.at[1, high], near_n.at[high], nxt)
                own[1, low, :] = total[:HALF]
            elif slot == 2:
                stage[2, low, :] = total[:HALF].astype(BF)
                ring.pl = leave(stage.at[2, low], near_p.at[low], prv)
                own[2, high, :] = total[HALF:]
            else:
                own[3] = total

        begin(0)
        begin(1)
        finish(0)
        begin(2)
        finish(1)
        begin(3)
        finish(2)
        finish(3)
        if hook:
            hook()
        ring.fn.wait_recv()
        stage[1, low, :] = (own[1, low, :] + far_n[...].astype(F32)).astype(BF)
        ring.nl = leave(stage.at[1, low], near_n.at[low], nxt)
        ring.fp.wait_recv()
        stage[2, high, :] = (own[2, high, :] + far_p[...].astype(F32)).astype(BF)
        ring.ph = leave(stage.at[2, high], near_p.at[high], prv)
        advance(jobs, 1)
        work(fill)
        for copy in (ring.nh, ring.pl, ring.nl, ring.ph):
            copy.wait_recv()
        if chunks:
            for copy in chunks:
                copy.wait_send()
        return own[3] + near_n[...].astype(F32) + near_p[...].astype(F32)

    def norm_back(dy, values, stream, layer, row, gain):
        xhat, r = norm_parts(values)
        sums = ref.norms.at[layer]
        sums[row : row + 1, :] = jnp.sum(dy * xhat, axis=0, keepdims=True)
        sums[row + 1 : row + 2, :] = jnp.sum(dy, axis=0, keepdims=True)
        scaled = dy * gain
        return stream + r * (
            scaled
            - jnp.mean(scaled, axis=-1, keepdims=True)
            - xhat * jnp.mean(scaled * xhat, axis=-1, keepdims=True)
        )

    def product(left, right):
        return lax.dot_general(left, right, TN, preferred_element_type=F32).astype(BF)

    def column_sums(values):
        return jnp.sum(values.astype(F32), axis=0, keepdims=True)

    def grads_of(layer):
        return ref.grads1 if layer else ref.grads0

    def fill_up(layer, t):
        out, g_up = grads_of(layer), product(
            ref.gather_b[layer, :, t * BLK : (t + 1) * BLK], ref.grad_pre[layer]
        )
        for i in range(8):
            x, zr, part = i // 2, i % 2, slice(i * 16, i * 16 + 16)
            out[x, zr * 2, t * 16 : t * 16 + 16, 384:512] = g_up[part, 0:128]
            out[x, zr * 2 + 1, t * 16 : t * 16 + 16, 0:384] = g_up[part, 128:512]

    def fill_qkv(layer, t):
        out, g_qkv = grads_of(layer), product(
            ref.gather_a[layer, :, t * BLK : (t + 1) * BLK], ref.dproj[layer]
        )
        for i in range(8):
            x, zr, part = i // 2, i % 2, slice(i * 16, i * 16 + 16)
            out[x, zr * 2, t * 16 : t * 16 + 16, 0:384] = g_qkv[part]

    def fill_down(layer, t):
        out = grads_of(layer)
        g_down = product(ref.active[layer, :, t * BLK : (t + 1) * BLK], ref.gather_m[layer])
        for half in range(2):
            i = t * 2 + half
            x, zr = i // 2, i % 2
            for zc in range(2):
                lanes = slice(zc * COLS, zc * COLS + COLS)
                out[x, zr * 2 + zc, 144:208, :] = g_down[half * 64 : half * 64 + 64, lanes]

    def fill_dense(layer):
        out = grads_of(layer)
        g_dense = product(ref.ctx_rows[layer], ref.gather_t[layer])
        for i in range(8):
            x, zr = i // 2, i % 2
            for zc in range(2):
                lanes = slice(zc * COLS, zc * COLS + COLS)
                out[x, zr * 2 + zc, 128:144, :] = g_dense[i * 16 : i * 16 + 16, lanes]

    def fill_spare(layer):
        out = grads_of(layer)
        here = pl.ds(pl.multiple_of(rank * BLK, BLK), BLK)
        sums_p, sums_u = column_sums(ref.dproj[layer]), column_sums(ref.grad_pre[layer])
        parts = [sums_p[:, :BLK], sums_p[:, 2 * BLK :]]
        parts += [column_sums(ref.gather_t[layer, :, here]), column_sums(ref.gather_m[layer, :, here])]
        parts += [sums_u[:, i * BLK : (i + 1) * BLK] for i in range(4)]
        vectors = jnp.concatenate(parts, axis=0)
        empty = jnp.zeros((16, BLK), BF)
        for t in range(2 * RING):
            spare = jnp.concatenate(
                [jnp.where(rank == t, vectors, jnp.zeros_like(vectors)),
                 ref.norms[layer, 0:4, t * BLK : (t + 1) * BLK], jnp.zeros((4, BLK), F32)],
                axis=0,
            ).astype(BF)
            for i in range(8):
                x, zr = i // 2, i % 2
                out[x, zr * 2 + 1, t * 16 : t * 16 + 16, 384:512] = spare if i == 0 else empty

    def queue(function, layer, amount):
        for t in range(amount):
            fillers.append(functools.partial(function, layer, t))

    vec = ref.vec
    pack = ref.pack
    for i, name in enumerate(VECTORS):
        pack[2 * i : 2 * i + 2, :] = getattr(ref, name)[...].astype(F32)
    for i in range(8):
        part = slice((i % 4) * BLK, (i % 4 + 1) * BLK)
        pack[16 + i : 17 + i, :] = ref.up_bias[i // 4 : i // 4 + 1, part].astype(F32)
    pack_copies = [push(ref.pack, vec.at[shard], peer) for peer in peers]
    first_weights = ship_columns(ref.raw_qkv, 0, ref.w_qkv.at[0], 3)
    vec[shard] = ref.pack[...]
    wait_all(pack_copies)

    def vector(number, layer):
        row = number * 2 + layer
        return jnp.concatenate([vec[s, row : row + 1, :] for s in range(2 * RING)], axis=1)

    def rank_vector(row):
        return vec[rank, row : row + 1, :]

    def normed(values, number, layer):
        xhat, _ = norm_parts(values)
        return (xhat * vector(number, layer) + vector(number + 1, layer)).astype(BF)

    swaps = []

    def project(layer):
        done = []
        bias = jnp.concatenate(
            [rank_vector(12 + layer), jnp.zeros((1, BLK), F32), rank_vector(14 + layer)], axis=1
        )

        def consume(group, q):
            where = rows(group, q)
            value = jnp.dot(
                ref.gather_a[layer, where, :], tall(ref.w_qkv.at[layer]), preferred_element_type=F32
            )
            ref.pbuf[where, :] = (value + bias).astype(BF)
            if any(q is other for other in done):
                swaps.append(swap_out(ref.pbuf, ref.qkv.at[layer], q))
            done.append(q)

        return consume

    def lift(layer):
        bias = jnp.concatenate([rank_vector(16 + 4 * layer + i) for i in range(4)], axis=1)

        def consume(group, q):
            where = rows(group, q)
            pre = jnp.dot(
                ref.gather_b[layer, where, :], tall(ref.w_up.at[layer]), preferred_element_type=F32
            ) + bias
            sq = pre * pre
            t = jnp.tanh(0.7978845608028654 * (pre + 0.044715 * sq * pre))
            ref.active[layer, where, :] = (0.5 * pre * (1.0 + t)).astype(BF)
            ref.slope[layer, where, :] = (
                0.5 * (1.0 + t)
                + 0.5 * pre * (1.0 - t * t) * (0.7978845608028654 * (1.0 + 3.0 * 0.044715 * sq))
            ).astype(BF)

        return consume

    def lower(layer):
        def consume(group, q):
            where = rows(group, q)
            value = lax.dot_general(
                ref.gather_m[layer, where, :], ref.w_down[layer], NT, preferred_element_type=F32
            )
            ref.grad_pre[layer, where, :] = (value * ref.slope[layer, where, :].astype(F32)).astype(BF)

        return consume

    def spread_context(layer):
        done = []

        def consume(group, q):
            where = rows(group, q)
            value = lax.dot_general(
                ref.gather_t[layer, where, :], ref.w_dense[layer], NT, preferred_element_type=F32
            )
            ref.ctx[where, :] = value.astype(BF)
            if any(q is other for other in done):
                swaps.append(swap_out(ref.ctx, ref.gctx, q))
            done.append(q)

        return consume

    shipping = SimpleNamespace()

    def ship_a():
        shipping.quarters = ship_quarters(first_weights)
        shipping.up0 = ship_columns(ref.raw_up, 0, ref.w_up.at[0], 1)
        shipping.dense0 = ship_rows(ref.raw_dense, 0, ref.w_dense.at[0])
        wait_all(shipping.quarters)

    def ship_b():
        shipping.quarters = ship_quarters(shipping.up0)
        shipping.qkv1 = ship_columns(ref.raw_qkv, 1, ref.w_qkv.at[1], 3)

    def ship_c():
        shipping.down0 = ship_rows(ref.raw_down, 0, ref.w_down.at[0])

    def ship_d():
        wait_all(shipping.quarters)
        shipping.quarters = ship_quarters(shipping.qkv1)
        shipping.up1 = ship_columns(ref.raw_up, 1, ref.w_up.at[1], 1)
        shipping.dense1 = ship_rows(ref.raw_dense, 1, ref.w_dense.at[1])

    def ship_e():
        wait_all(shipping.quarters)
        shipping.quarters = ship_quarters(shipping.up1)
        shipping.down1 = ship_rows(ref.raw_down, 1, ref.w_down.at[1])

    gather(ref.gather_a.at[0], normed(ref.tokens[...].astype(F32), 0, 0), project(0), ship_a)
    ship_b()
    jobs.append(gather_rest(ref.gather_m.at[1], gather_start(ref.gather_m.at[1], ref.grad_out[...]), None))
    advance(jobs, 1)
    for layer in range(2):
        swap_done(swaps)
        swaps.clear()
        attention_forward(ref.slopes, ref.qkv.at[layer], ref.ctx)
        chunks = swap_in(ref.ctx, ref.ctx_rows.at[layer])
        if layer == 0:
            advance(jobs, 1)
            shipping.dense0()
        else:
            shipping.dense1()
        acc = scatter(
            ref.ctx_rows.at[layer], lambda: ref.w_dense[layer], NN, chunks,
            ship_c if layer == 0 else None,
        )
        stream = ref.tokens[...].astype(F32) if layer == 0 else ref.stream1[...]
        middle = stream + (acc + vector(2, layer))
        ref.middle[layer] = middle
        if layer == 0:
            wait_all(shipping.quarters)
            shipping.quarters = []
        gather(ref.gather_b.at[layer], normed(middle, 3, layer), lift(layer), ship_d if layer == 0 else None)
        if layer == 0:
            shipping.down0()
        else:
            run_jobs(jobs)
            shipping.down1()
            lower_rows = lower(1)
            for core in range(2):
                for q in range(RING):
                    fillers.append(functools.partial(lower_rows, core, q))
        acc = scatter(ref.active.at[layer], lambda: ref.w_down[layer], NN, None, None, 8)
        result = ref.middle[layer] + (acc + vector(5, layer))
        if layer == 0:
            ref.stream1[...] = result
            wait_all(shipping.quarters)
            shipping.quarters = []
            gather(ref.gather_a.at[1], normed(result, 0, 1), project(1), ship_e)
            wait_all(shipping.quarters)
        else:
            ref.output[...] = result

    def start_reduction(grads, out):
        bufs = [getattr(ref, name) for name in REDUCE_NAMES]
        per = len(bufs) // 2
        for one in range(2):
            mine = bufs[one * per : one * per + per]
            jobs.append(reduce_job(env, one == 0, one, grads, out, mine, job_sent, reduced))

    grad = ref.grad_out[...].astype(F32)
    for layer in (1, 0):
        work(len(fillers))
        queue(fill_up, layer, 8)
        queue(fill_down, layer, 4)
        if layer:
            ref.kept[...] = grad
        acc = scatter(ref.grad_pre.at[layer], lambda: tall(ref.w_up.at[layer]), NT)
        grad = norm_back(acc, ref.middle[layer], ref.kept[...], layer, 2, vector(3, layer))
        ref.kept[...] = grad
        gather(ref.gather_t.at[layer], grad.astype(BF), spread_context(layer), None, 2)
        fillers.insert(0, functools.partial(fill_dense, layer))
        advance(jobs, 1)
        swap_done(swaps)
        swaps.clear()
        attention_backward(ref.slopes, ref.qkv.at[layer], ref.gctx, ref.pbuf, ref.dk, ref.dv)
        advance(jobs, 1)
        chunks = swap_in(ref.pbuf, ref.dproj.at[layer])
        queue(fill_qkv, layer, 8)
        acc = scatter(ref.dproj.at[layer], lambda: tall(ref.w_qkv.at[layer]), NT, chunks)
        values = ref.stream1[...] if layer else ref.tokens[...].astype(F32)
        grad = norm_back(acc, values, ref.kept[...], layer, 0, vector(0, layer))
        fillers.append(functools.partial(fill_spare, layer))
        if layer:
            ref.kept[...] = grad
            gather(ref.gather_m.at[0], grad.astype(BF), lower(0), None, 3)
            work(len(fillers))
            start_reduction(ref.grads1, ref.totals1)
            advance(jobs, 1)
        else:
            ref.grad_tokens[...] = grad
    run_jobs(jobs)
    for copy in job_sent:
        copy.wait_send()
    for copy in reduced:
        copy.wait()
    job_sent.clear()
    reduced.clear()
    for partner in env.reduce_partners:
        pl.semaphore_signal(ref.again.at[0], inc=1, device_id=partner, device_id_type=MESH)
    work(len(fillers))
    pl.semaphore_wait(ref.again.at[0], len(env.reduce_partners))
    start_reduction(ref.grads0, ref.totals0)
    run_jobs(jobs)
    for copy in sent + leaving + job_sent:
        copy.wait_send()
    for copy in reduced:
        copy.wait()


NN = (((1,), (0,)), ((), ()))
NT = (((1,), (1,)), ((), ()))
TN = (((0,), (0,)), ((), ()))


def chain_call(cid, **operands):
    full, packed = 2 * RING * BLK, (RING, RING, PIECE, COLS)
    vmem = pltpu.VMEM
    outs = dict(
        output=((BLK, WIDTH), F32, vmem),
        grad_tokens=((BLK, WIDTH), F32, vmem),
        totals1=(packed, BF, pl.ANY),
        totals0=(packed, BF, pl.ANY),
    )
    scratch = dict(
        pack=vmem((24, BLK), F32),
        vec=vmem((2 * RING, 24, BLK), F32),
        w_qkv=vmem((2, 8, 4, 32, 384), BF),
        w_up=vmem((2, 8, 4, 32, 512), BF),
        w_dense=vmem((2, BLK, WIDTH), BF),
        w_down=vmem((2, 512, WIDTH), BF),
        gather_a=vmem((2, full, WIDTH), BF),
        gather_b=vmem((2, full, WIDTH), BF),
        gather_m=vmem((2, full, WIDTH), BF),
        gather_t=vmem((2, full, WIDTH), BF),
        pbuf=vmem((full, 384), BF),
        qkv=vmem((2, full, 384), BF),
        ctx=vmem((full, BLK), BF),
        ctx_rows=vmem((2, full, BLK), BF),
        active=vmem((2, full, 512), BF),
        slope=vmem((2, full, 512), BF),
        grad_pre=vmem((2, full, 512), BF),
        gctx=vmem((full, BLK), BF),
        dproj=vmem((2, full, 384), BF),
        dk=vmem((full, BLK), F32),
        dv=vmem((full, BLK), F32),
        stream1=vmem((BLK, WIDTH), F32),
        middle=vmem((2, BLK, WIDTH), F32),
        kept=vmem((BLK, WIDTH), F32),
        norms=vmem((2, 8, WIDTH), F32),
        own=vmem((RING, BLK, WIDTH), F32),
        sib_out=vmem((RING, BLK, WIDTH), BF),
        sib_in=vmem((2, RING, BLK, WIDTH), BF),
        stage=vmem((3, BLK, WIDTH), BF),
        near_n=vmem((2, BLK, WIDTH), BF),
        near_p=vmem((2, BLK, WIDTH), BF),
        far_n=vmem((2, HALF, WIDTH), BF),
        far_p=vmem((2, HALF, WIDTH), BF),
        grads1=vmem(packed, BF),
        grads0=vmem(packed, BF),
        again=pltpu.SemaphoreType.REGULAR((1,)),
        send=pltpu.SemaphoreType.DMA((320,)),
        recv=pltpu.SemaphoreType.DMA((320,)),
        local=pltpu.SemaphoreType.DMA((24,)),
    )
    scratch.update(zip(REDUCE_NAMES, reduce_scratch() * 2))

    def space(name):
        if name.startswith("raw_"):
            return pl.ANY
        return pltpu.SMEM if name == "slopes" else vmem

    results = pl.pallas_call(
        functools.partial(chain_kernel, list(operands) + list(outs) + list(scratch)),
        out_shape=[jax.ShapeDtypeStruct(shape, dtype) for shape, dtype, _ in outs.values()],
        in_specs=[pl.BlockSpec(memory_space=space(name)) for name in operands],
        out_specs=[pl.BlockSpec(memory_space=where) for _, _, where in outs.values()],
        scratch_shapes=list(scratch.values()),
        compiler_params=pltpu.CompilerParams(
            collective_id=cid, has_side_effects=True, vmem_limit_bytes=CALL_VMEM
        ),
    )(*operands.values())
    return results


def unpack_kernel(final0, final1, qkv, up, dense, down, spare):
    layer, x = pl.program_id(0), pl.program_id(1)

    def write(final):
        for zr in range(2):
            rows = slice(zr * 16, zr * 16 + 16)
            for k in range(2 * RING):
                slot = slice(k * 16, k * 16 + 16)
                left = final[0, zr * 2, slot, :].astype(F32)
                right = final[0, zr * 2 + 1, slot, :].astype(F32)
                for j in range(3):
                    at = j * WIDTH + k * BLK
                    qkv[0, rows, at : at + BLK] = left[:, j * BLK : (j + 1) * BLK]
                up[0, rows, k * 512 : k * 512 + 128] = left[:, 384:512]
                up[0, rows, k * 512 + 128 : k * 512 + 512] = right[:, 0:384]
            for zc in range(2):
                lanes = slice(zc * COLS, zc * COLS + COLS)
                dense[0, rows, lanes] = final[0, zr * 2 + zc, 128:144, :].astype(F32)
                down[0, zr * 64 : zr * 64 + 64, lanes] = final[0, zr * 2 + zc, 144:208, :].astype(F32)

        @pl.when(x == 0)
        def _():
            total = final[0, 1, 0:16, 384:512].astype(F32)
            for k in range(1, 2 * RING):
                total = total + final[0, 1, k * 16 : k * 16 + 16, 384:512].astype(F32)
            spare[0] = total

    @pl.when(layer == 0)
    def _():
        write(final0)

    @pl.when(layer == 1)
    def _():
        write(final1)


def unpack_call(final0, final1):
    layers = 2

    def block(index):
        def at(layer, x):
            return (jnp.where(layer == index, x, (RING - 1) * (1 - index)), 0, 0, 0)

        return pl.BlockSpec((1, RING, PIECE, COLS), at)

    def rows(count, width):
        return pl.BlockSpec((1, count, width), lambda layer, x: (layer, x, 0))

    return pl.pallas_call(
        unpack_kernel,
        grid=(layers, RING),
        out_shape=[
            jax.ShapeDtypeStruct((layers, BLK, 3 * WIDTH), F32),
            jax.ShapeDtypeStruct((layers, BLK, 4 * WIDTH), F32),
            jax.ShapeDtypeStruct((layers, BLK, WIDTH), F32),
            jax.ShapeDtypeStruct((layers, 4 * BLK, WIDTH), F32),
            jax.ShapeDtypeStruct((layers, 16, BLK), F32),
        ],
        in_specs=[block(0), block(1)],
        out_specs=[
            rows(32, 3 * WIDTH), rows(32, 4 * WIDTH), rows(32, WIDTH), rows(128, WIDTH),
            pl.BlockSpec((1, 16, BLK), lambda layer, x: (layer, 0, 0)),
        ],
        compiler_params=pltpu.CompilerParams(vmem_limit_bytes=CALL_VMEM),
    )(final0, final1)


def on_device(
    tokens,
    grad_out,
    slope_index,
    ln1_gain,
    ln1_bias,
    qkv_weight,
    q_bias,
    v_bias,
    dense_weight,
    dense_bias,
    ln2_gain,
    ln2_bias,
    up_weight,
    up_bias,
    down_weight,
    down_bias,
):
    layers = qkv_weight.shape[0]
    heads = slope_index.shape[0]
    rank = lax.axis_index("c") * RING + lax.axis_index("y")
    slopes_all = jnp.exp2(-8.0 * (slope_index.astype(F32) + 1.0) / heads)
    slopes = lax.dynamic_slice(slopes_all, (rank * 2,), (2,))

    output, grad_stream, final1, final0 = chain_call(
        1, slopes=slopes, tokens=tokens, grad_out=grad_out, ln1_gain=ln1_gain, ln1_bias=ln1_bias,
        dense_bias=dense_bias, ln2_gain=ln2_gain, ln2_bias=ln2_bias, down_bias=down_bias,
        q_bias=q_bias, v_bias=v_bias, up_bias=up_bias, raw_qkv=qkv_weight,
        raw_up=up_weight, raw_dense=dense_weight, raw_down=down_weight,
    )
    g_qkv, g_up, g_dense, g_down, spare = unpack_call(final0, final1)
    return (
        output,
        grad_stream,
        spare[:, 8],
        spare[:, 9],
        g_qkv,
        spare[:, 0],
        spare[:, 1],
        g_dense,
        spare[:, 2],
        spare[:, 10],
        spare[:, 11],
        g_up,
        spare[:, 4:8].reshape(layers, -1),
        g_down,
        spare[:, 3],
    )


def solution(mesh):
    replica, shard = mesh.devices.shape
    fine = Mesh(mesh.devices.reshape(replica // 4, 2, 2, shard // RING, RING), AXES)
    rows = P(AXES, None)
    flat = P(None, ("xl", "y"))
    wide = P(None, ("xl", "y"), None)
    return jax.shard_map(
        on_device,
        mesh=fine,
        in_specs=(
            rows, rows, P(), flat, flat, wide, flat, flat, wide, flat, flat, flat, wide, flat,
            wide, flat,
        ),
        out_specs=(
            rows, rows, flat, flat, wide, flat, flat, wide, flat, flat, flat, wide, flat, wide,
            flat,
        ),
        check_vma=False,
    )
```

```python
import functools
from types import SimpleNamespace

import jax
import jax.numpy as jnp
from jax import lax
from jax.experimental import pallas as pl
from jax.experimental.pallas import tpu as pltpu
from jax.sharding import Mesh
from jax.sharding import PartitionSpec as P

eps = 1e-05
MESH = pl.DeviceIdType.MESH
AXES = ("z", "xh", "c", "xl", "y")
BF = jnp.bfloat16
F32 = jnp.float32
BLK = 128
HALF = 64
WIDTH = 1024
RING = 4
CALL_VMEM = 62 * 1024 * 1024


def norm_parts(values):
    average = jnp.mean(values, axis=-1, keepdims=True)
    centred = values - average
    variance = jnp.mean(centred * centred, axis=-1, keepdims=True)
    r = lax.rsqrt(variance + eps)
    return centred * r, r


PIECE = 208
COLS = 512
LANES = 256


def neighbours():
    z, xh, c, xl, y = (lax.axis_index(name) for name in AXES)
    x = xh * 2 + xl

    def at_x(value):
        value = lax.rem(value, RING)
        return {"xh": value // 2, "xl": lax.rem(value, 2)}

    env = SimpleNamespace(z=z, xh=xh, c=c, xl=xl, y=y, x=x)
    env.x_next, env.x_prev = at_x(x + 1), at_x(x + 3)
    env.z_next, env.z_prev = {"z": lax.rem(z + 1, RING)}, {"z": lax.rem(z + 3, RING)}
    env.across, env.diagonal, env.sib = {"xh": 1 - xh}, {"xl": 1 - xl, "c": 1 - c}, {"c": 1 - c}
    env.mates = [(1 - c, y)]
    for dy in (2, 1, 3):
        env.mates += [(c, lax.rem(y + dy, RING)), (1 - c, lax.rem(y + dy, RING))]
    env.reduce_partners = [env.x_next, env.x_prev, env.z_next, env.z_prev, env.across, env.diagonal]
    env.reduce_partners += [{"c": core, "y": other} for core, other in env.mates]
    return env


def enter(partners):
    barrier = pltpu.get_barrier_semaphore()
    for partner in partners:
        pl.semaphore_signal(barrier, inc=1, device_id=partner, device_id_type=MESH)
    pl.semaphore_wait(barrier, len(partners))


def advance(jobs, steps):
    for _ in range(steps):
        for one in list(jobs):
            if next(one, 1) == 1:
                jobs.remove(one)


def run_jobs(jobs):
    while jobs:
        advance(jobs, 1)


def reduce_job(env, x_first, half, grads, out, bufs, sent, local):
    (far_n, far_p, near_n, near_p, total, far2_n, far2_p, near2_n, near2_p,
     summed, final_piece, final, send, recv, keep) = bufs
    c, xl, x, z = env.c, env.xl, env.x, env.z
    rank = c * RING + env.y
    lanes = pl.ds(half * LANES, LANES)
    count = [0]

    def push(src, dst, target):
        i = count[0]
        count[0] += 1
        copy = pltpu.make_async_remote_copy(
            src_ref=src, dst_ref=dst, send_sem=send.at[i], recv_sem=recv.at[i],
            device_id=target, device_id_type=MESH,
        )
        copy.start()
        sent.append(copy)
        return copy

    a, b = (x, z) if x_first else (z, x)
    a_next, a_prev = (env.x_next, env.x_prev) if x_first else (env.z_next, env.z_prev)
    b_next, b_prev = (env.z_next, env.z_prev) if x_first else (env.x_next, env.x_prev)

    def piece(index, start, size):
        if x_first:
            return grads.at[index, pl.ds(start, size), :, lanes]
        return grads.at[pl.ds(start, size), index, :, lanes]

    def load(view):
        return view[...].astype(F32)

    far, up, down = (lax.rem(a + d, RING) for d in (2, 1, 3))
    lo, hi = pl.ds(0, 2), pl.ds(2, 2)
    fn = push(piece(far, 0, 2), far_n, a_next)
    fp = push(piece(far, 2, 2), far_p, a_prev)
    nh = push(piece(up, 2, 2), near_n.at[hi], a_next)
    pl_ = push(piece(down, 0, 2), near_p.at[lo], a_prev)
    yield 0
    fn.wait_recv()
    far_n[...] = (load(piece(up, 0, 2)) + far_n[...].astype(F32)).astype(BF)
    nl = push(far_n, near_n.at[lo], a_next)
    fp.wait_recv()
    far_p[...] = (load(piece(down, 2, 2)) + far_p[...].astype(F32)).astype(BF)
    ph = push(far_p, near_p.at[hi], a_prev)
    yield 0
    yield 0
    for copy in (nh, pl_, nl, ph):
        copy.wait_recv()
    for q in range(RING):
        own = load(piece(a, q, 1))
        total[q] = (
            own.reshape(PIECE, LANES) + near_n[q].astype(F32) + near_p[q].astype(F32)
        ).astype(BF)

    far, up, down = (lax.rem(b + d, RING) for d in (2, 1, 3))
    cut = 96
    lo, hi = pl.ds(0, cut), pl.ds(cut, PIECE - cut)
    fn = push(total.at[far, lo], far2_n, b_next)
    fp = push(total.at[far, hi], far2_p, b_prev)
    nh = push(total.at[up, hi], near2_n.at[hi], b_next)
    pl_ = push(total.at[down, lo], near2_p.at[lo], b_prev)
    yield 0
    fn.wait_recv()
    far2_n[...] = (total[up, lo, :].astype(F32) + far2_n[...].astype(F32)).astype(BF)
    nl = push(far2_n, near2_n.at[lo], b_next)
    fp.wait_recv()
    far2_p[...] = (total[down, hi, :].astype(F32) + far2_p[...].astype(F32)).astype(BF)
    ph = push(far2_p, near2_p.at[hi], b_prev)
    yield 0
    for copy in (nh, pl_, nl, ph):
        copy.wait_recv()
    summed[...] = (
        total[b].astype(F32) + near2_n[...].astype(F32) + near2_p[...].astype(F32)
    ).astype(BF)

    def slot(number):
        return pl.ds(pl.multiple_of(number * 16, 16), 16)

    copies = [
        push(
            summed.at[slot(core * RING + other)], final_piece.at[slot(rank)],
            {"c": core, "y": other},
        )
        for core, other in env.mates
    ]
    final_piece[slot(rank), :] = summed[slot(rank), :]
    final_piece[2 * RING * 16 :, :] = summed[2 * RING * 16 :, :]
    yield 0
    for copy in copies:
        copy.wait_recv()

    trade = pltpu.make_async_remote_copy(
        src_ref=final_piece, dst_ref=final.at[x, z], send_sem=keep.at[0],
        recv_sem=keep.at[1], device_id=env.diagonal, device_id_type=MESH,
    )

    @pl.when(c != xl)
    def _():
        trade.start()

    @pl.when(c == xl)
    def _():
        final[x, z] = final_piece[...]

    yield 0

    @pl.when(c != xl)
    def _():
        trade.wait()

    mine, other = env.xh * 2 + c, (1 - env.xh) * 2 + c
    zn, zp, zf = (lax.rem(z + d, RING) for d in (1, 3, 2))

    def spread(first, second, target):
        view = final.at[first, second]
        return push(view, view, target)

    one_n = spread(mine, z, env.z_next)
    cross = spread(mine, z, env.across)
    one_p = spread(mine, z, env.z_prev)
    siblings = [spread(mine, z, env.sib)]
    yield 0
    cross.wait_recv()
    two_p = spread(other, z, env.z_prev)
    two_n = spread(other, z, env.z_next)
    siblings.append(spread(other, z, env.sib))
    yield 0
    one_n.wait_recv()
    fwd_n = spread(mine, zp, env.z_next)
    siblings.append(spread(mine, zp, env.sib))
    two_p.wait_recv()
    fwd_p = spread(other, zn, env.z_prev)
    siblings.append(spread(other, zn, env.sib))
    yield 0
    one_p.wait_recv()
    siblings.append(spread(mine, zn, env.sib))
    two_n.wait_recv()
    siblings.append(spread(other, zp, env.sib))
    yield 0
    fwd_n.wait_recv()
    siblings.append(spread(mine, zf, env.sib))
    fwd_p.wait_recv()
    siblings.append(spread(other, zf, env.sib))
    yield 0
    for copy in siblings:
        copy.wait_recv()
    back = pltpu.make_async_copy(final, out.at[:, :, :, lanes], keep.at[2])
    back.start()
    local.append(back)


def reduce_scratch():
    two, four = (2, PIECE, LANES), (4, PIECE, LANES)
    one, low, high = (PIECE, LANES), (96, LANES), (PIECE - 96, LANES)
    shapes = [two, two, four, four, four, low, high, one, one, one, one]
    return [pltpu.VMEM(shape, BF) for shape in shapes] + [
        pltpu.VMEM((RING, RING, PIECE, LANES), BF),
        pltpu.SemaphoreType.DMA((40,)),
        pltpu.SemaphoreType.DMA((40,)),
        pltpu.SemaphoreType.DMA((3,)),
    ]


REDUCE_NAMES = ["job%d" % i for i in range(30)]


def reduce_kernel(grads, out, *bufs):
    env = neighbours()
    enter(env.reduce_partners)
    sent, local = [], []
    half = len(bufs) // 2
    run_jobs(
        [
            reduce_job(env, True, 0, grads, out, bufs[:half], sent, local),
            reduce_job(env, False, 1, grads, out, bufs[half:], sent, local),
        ]
    )
    for copy in sent:
        copy.wait_send()
    for copy in local:
        copy.wait()


def reduce_call(cid, grads):
    return pl.pallas_call(
        reduce_kernel,
        out_shape=jax.ShapeDtypeStruct(grads.shape, BF),
        in_specs=[pl.BlockSpec(memory_space=pltpu.VMEM)],
        out_specs=pl.BlockSpec(memory_space=pl.ANY),
        scratch_shapes=reduce_scratch() * 2,
        compiler_params=pltpu.CompilerParams(
            collective_id=cid, has_side_effects=True, vmem_limit_bytes=CALL_VMEM
        ),
    )(grads)


QB = 256


def head_only(values, head):
    lane = lax.broadcasted_iota(jnp.int32, values.shape, 1)
    keep = (lane // 64) == head
    return jnp.where(keep, values, jnp.zeros_like(values))


def probs_of(q_pad, keys, slope, start):
    count = keys.shape[0]
    scores = lax.dot_general(keys, q_pad, NT, preferred_element_type=F32)
    key_pos = lax.broadcasted_iota(jnp.int32, (count, QB), 0)
    query_pos = lax.broadcasted_iota(jnp.int32, (count, QB), 1) + start
    scores = scores + slope * key_pos.astype(F32)
    scores = jnp.where(key_pos <= query_pos, scores, -1000000000.0)
    top = jnp.max(scores, axis=0, keepdims=True)
    exponent = jnp.exp(scores - top)
    total = jnp.sum(exponent, axis=0, keepdims=True)
    return exponent * (1.0 / total)


def attention_forward(slopes, qkv, ctx):
    value_t = qkv[:, 2 * BLK : 3 * BLK].astype(F32).T.astype(BF)
    for start in range(0, qkv.shape[0], QB):
        count = start + QB
        queries = qkv[start : start + QB, 0:BLK] * jnp.asarray(0.125, BF)
        keys = qkv[0:count, BLK : 2 * BLK]
        parts = []
        for head in range(2):
            probs = probs_of(head_only(queries, head), keys, slopes[head], start).astype(BF)
            ctx_t = jnp.dot(value_t[:, 0:count], probs, preferred_element_type=F32)
            parts.append(ctx_t[head * 64 : head * 64 + 64])
        ctx[start : start + QB, :] = jnp.concatenate(parts, axis=0).T.astype(BF)


def attention_backward(slopes, qkv, gctx, dqkv, dk, dv):
    key_t = qkv[:, BLK : 2 * BLK].astype(F32).T.astype(BF)
    dk[...] = jnp.zeros_like(dk)
    dv[...] = jnp.zeros_like(dv)
    for start in range(0, qkv.shape[0], QB):
        count = start + QB
        queries = qkv[start : start + QB, 0:BLK] * jnp.asarray(0.125, BF)
        keys = qkv[0:count, BLK : 2 * BLK]
        values = qkv[0:count, 2 * BLK : 3 * BLK]
        grads = gctx[start : start + QB, :]
        parts = []
        for head in range(2):
            q_pad = head_only(queries, head)
            g_pad = head_only(grads, head)
            probs = probs_of(q_pad, keys, slopes[head], start)
            grad_probs = lax.dot_general(values, g_pad, NT, preferred_element_type=F32)
            inner = jnp.sum(probs * grad_probs, axis=0, keepdims=True)
            grad_scores = (probs * (grad_probs - inner)).astype(BF)
            dk[0:count, :] += jnp.dot(grad_scores, q_pad, preferred_element_type=F32)
            dv[0:count, :] += jnp.dot(probs.astype(BF), g_pad, preferred_element_type=F32)
            dq_t = jnp.dot(key_t[:, 0:count], grad_scores, preferred_element_type=F32)
            parts.append(dq_t[head * 64 : head * 64 + 64] * 0.125)
        dqkv[start : start + QB, 0:BLK] = jnp.concatenate(parts, axis=0).T.astype(BF)
    dqkv[:, BLK : 2 * BLK] = dk[...].astype(BF)
    dqkv[:, 2 * BLK : 3 * BLK] = dv[...].astype(BF)


VECTORS = (
    "ln1_gain", "ln1_bias", "dense_bias", "ln2_gain", "ln2_bias", "down_bias", "q_bias", "v_bias",
)


def chain_kernel(names, *refs):
    ref = SimpleNamespace(**dict(zip(names, refs)))
    env = neighbours()
    z, c, xl, y = env.z, env.c, env.xl, env.y
    shard, rank = xl * RING + y, c * RING + y
    up, down, far = lax.rem(y + 1, RING), lax.rem(y + 3, RING), lax.rem(y + 2, RING)
    oc, ox = 1 - c, 1 - xl
    sib, nxt, prv, xnb = env.sib, {"y": up}, {"y": down}, {"xl": ox}
    plane = [
        (lax.rem(xl + dx, 2), lax.rem(y + dy, RING))
        for dx, dy in ((0, 2), (1, 2), (1, 1), (1, 3), (0, 1), (0, 3), (1, 0))
    ]
    peers = [{"xl": px, "y": py} for px, py in plane]
    z_far = {"z": lax.rem(z + 2, RING)}
    enter(peers + [z_far] + env.reduce_partners)

    sent, jobs, job_sent, reduced, fillers = [], [], [], [], []
    counts = SimpleNamespace(push=0, store=0)

    def push(src, dst, target, track=True):
        i = counts.push
        counts.push += 1
        copy = pltpu.make_async_remote_copy(
            src_ref=src, dst_ref=dst, send_sem=ref.send.at[i], recv_sem=ref.recv.at[i],
            device_id=target, device_id_type=MESH,
        )
        copy.start()
        if track:
            sent.append(copy)
        return copy

    def store(src, dst):
        copy = pltpu.make_async_copy(src, dst, ref.local.at[counts.store])
        counts.store += 1
        copy.start()
        return copy

    def work(amount):
        for _ in range(min(amount, len(fillers))):
            fillers.pop(0)()

    def rows(group, q, offset=0, size=BLK):
        return pl.ds(pl.multiple_of((group * RING + q) * BLK + offset, HALF), size)

    def ship_columns(raw, layer, dst, parts):
        per = dst.shape[3] // parts
        quarter = pl.ds(pl.multiple_of(z * dst.shape[2], dst.shape[2]), dst.shape[2])
        copies, keeps = [], []
        for j in range(parts):
            for (_, py), peer in zip(plane, peers):
                cols = pl.ds(pl.multiple_of((j * 2 * RING + c * RING + py) * per, per), per)
                copies.append(
                    push(raw.at[layer, quarter, cols], dst.at[shard, z, :, pl.ds(j * per, per)], peer)
                )
            cols = pl.ds(pl.multiple_of((j * 2 * RING + rank) * per, per), per)
            keeps.append(store(raw.at[layer, quarter, cols], dst.at[shard, z, :, pl.ds(j * per, per)]))
        return dst, copies, keeps

    def ship_quarters(step):
        dst, copies, keeps = step
        for copy in copies:
            copy.wait_recv()
        for copy in keeps:
            copy.wait()
        view = dst.at[:, z]
        return [push(view, view, target) for target in (env.z_next, env.z_prev, z_far)]

    def ship_rows(raw, layer, dst):
        i = counts.push
        counts.push += 1
        copy = pltpu.make_async_remote_copy(
            src_ref=raw.at[layer], dst_ref=dst, send_sem=ref.send.at[i], recv_sem=ref.recv.at[i],
            device_id=xnb, device_id_type=MESH,
        )
        keep = pltpu.make_async_copy(raw.at[layer], dst, ref.local.at[counts.store])
        counts.store += 1

        @pl.when(c == xl)
        def _():
            copy.start()
            keep.start()

        def finish():
            @pl.when(c == xl)
            def _():
                copy.wait_send()
                keep.wait()

            @pl.when(c != xl)
            def _():
                copy.wait_recv()

        return finish

    def wait_all(copies):
        for copy in copies:
            copy.wait_recv()

    def tall(weight):
        return weight[...].reshape(WIDTH, weight.shape[3])

    def gather_start(gbuf, block):
        own = rows(c, y)
        low, high = rows(c, y, 0, HALF), rows(c, y, HALF, HALF)
        gbuf[own, :] = block
        return [
            push(gbuf.at[low], gbuf.at[low], nxt),
            push(gbuf.at[high], gbuf.at[high], prv),
            push(gbuf.at[own], gbuf.at[own], sib),
            push(gbuf.at[high], gbuf.at[high], nxt),
            push(gbuf.at[low], gbuf.at[low], prv),
        ]

    def gather_rest(gbuf, first, consume):
        low_n, high_p, own_s, high_n, low_p = first
        if consume:
            consume(c, y)
        yield 0
        low_n.wait_recv()
        part = gbuf.at[rows(c, down, 0, HALF)]
        fwd_n = push(part, part, nxt)
        high_p.wait_recv()
        part = gbuf.at[rows(c, up, HALF, HALF)]
        fwd_p = push(part, part, prv)
        own_s.wait_recv()
        if consume:
            consume(oc, y)
        yield 0
        high_n.wait_recv()
        part = gbuf.at[rows(c, down)]
        sib_a = push(part, part, sib)
        low_p.wait_recv()
        part = gbuf.at[rows(c, up)]
        sib_b = push(part, part, sib)
        if consume:
            consume(c, down)
            consume(c, up)
            sib_a.wait_recv()
            consume(oc, down)
            sib_b.wait_recv()
            consume(oc, up)
        yield 0
        fwd_n.wait_recv()
        fwd_p.wait_recv()
        part = gbuf.at[rows(c, far)]
        sib_c = push(part, part, sib)
        if consume:
            consume(c, far)
        else:
            yield 0
            sib_a.wait_recv()
            sib_b.wait_recv()
        sib_c.wait_recv()
        if consume:
            consume(oc, far)

    def gather(gbuf, block, consume, between=None, fill=1):
        steps = gather_rest(gbuf, gather_start(gbuf, block), consume)
        if between:
            between()
        while next(steps, 1) == 0:
            advance(jobs, 1)
            work(fill)

    def swap_in(src, dst):
        copies = [push(src.at[rows(ox, q)], dst.at[rows(xl, q)], xnb, False) for q in order]
        mine = pl.ds(pl.multiple_of(xl * RING * BLK, BLK), RING * BLK)
        dst[mine, :] = src[mine, :]
        return copies

    def swap_out(src, dst, q):
        copy = push(src.at[rows(ox, q)], dst.at[rows(xl, q)], xnb, False)
        dst[rows(xl, q), :] = src[rows(xl, q), :]
        return copy

    def swap_done(copies):
        for copy in copies:
            copy.wait()

    order = [far, up, down, y]
    turn = [0]
    leaving = []

    def scatter(lhs, weight, dims, chunks=None, hook=None, fill=5):
        for copy in leaving:
            copy.wait_send()
        leaving.clear()
        which = turn[0] % 2
        turn[0] += 1
        own, sib_out, sib_in, stage = ref.own, ref.sib_out, ref.sib_in.at[which], ref.stage
        near_n, near_p = ref.near_n.at[which], ref.near_p.at[which]
        far_n, far_p = ref.far_n.at[which], ref.far_p.at[which]
        low, high = pl.ds(0, HALF), pl.ds(HALF, HALF)
        ring = SimpleNamespace()
        passed = []

        def leave(src, dst, target):
            copy = push(src, dst, target, False)
            leaving.append(copy)
            return copy

        def partial(group, q):
            return lax.dot_general(
                lhs[rows(group, q), :], weight(), dims, preferred_element_type=F32
            )

        def begin(slot):
            if chunks:
                chunks[slot].wait_recv()
            sib_out[slot] = partial(oc, order[slot]).astype(BF)
            passed.append(leave(sib_out.at[slot], sib_in.at[slot], sib))
            own[slot] = partial(c, order[slot])

        def finish(slot):
            passed[slot].wait_recv()
            total = own[slot] + sib_in[slot].astype(F32)
            if slot == 0:
                stage[0] = total.astype(BF)
                ring.fn = leave(stage.at[0, low], far_n, nxt)
                ring.fp = leave(stage.at[0, high], far_p, prv)
            elif slot == 1:
                stage[1, high, :] = total[HALF:].astype(BF)
                ring.nh = leave(stage.at[1, high], near_n.at[high], nxt)
                own[1, low, :] = total[:HALF]
            elif slot == 2:
                stage[2, low, :] = total[:HALF].astype(BF)
                ring.pl = leave(stage.at[2, low], near_p.at[low], prv)
                own[2, high, :] = total[HALF:]
            else:
                own[3] = total

        begin(0)
        begin(1)
        finish(0)
        begin(2)
        finish(1)
        begin(3)
        finish(2)
        finish(3)
        if hook:
            hook()
        ring.fn.wait_recv()
        stage[1, low, :] = (own[1, low, :] + far_n[...].astype(F32)).astype(BF)
        ring.nl = leave(stage.at[1, low], near_n.at[low], nxt)
        ring.fp.wait_recv()
        stage[2, high, :] = (own[2, high, :] + far_p[...].astype(F32)).astype(BF)
        ring.ph = leave(stage.at[2, high], near_p.at[high], prv)
        advance(jobs, 1)
        work(fill)
        for copy in (ring.nh, ring.pl, ring.nl, ring.ph):
            copy.wait_recv()
        if chunks:
            for copy in chunks:
                copy.wait_send()
        return own[3] + near_n[...].astype(F32) + near_p[...].astype(F32)

    def norm_back(dy, values, stream, layer, row, gain):
        xhat, r = norm_parts(values)
        sums = ref.norms.at[layer]
        sums[row : row + 1, :] = jnp.sum(dy * xhat, axis=0, keepdims=True)
        sums[row + 1 : row + 2, :] = jnp.sum(dy, axis=0, keepdims=True)
        scaled = dy * gain
        return stream + r * (
            scaled
            - jnp.mean(scaled, axis=-1, keepdims=True)
            - xhat * jnp.mean(scaled * xhat, axis=-1, keepdims=True)
        )

    def product(left, right):
        return lax.dot_general(left, right, TN, preferred_element_type=F32).astype(BF)

    def column_sums(values):
        return jnp.sum(values.astype(F32), axis=0, keepdims=True)

    def grads_of(layer):
        return ref.grads1 if layer else ref.grads0

    def fill_up(layer, t):
        out, g_up = grads_of(layer), product(
            ref.gather_b[layer, :, t * BLK : (t + 1) * BLK], ref.grad_pre[layer]
        )
        for i in range(8):
            x, zr, part = i // 2, i % 2, slice(i * 16, i * 16 + 16)
            out[x, zr * 2, t * 16 : t * 16 + 16, 384:512] = g_up[part, 0:128]
            out[x, zr * 2 + 1, t * 16 : t * 16 + 16, 0:384] = g_up[part, 128:512]

    def fill_qkv(layer, t):
        out, g_qkv = grads_of(layer), product(
            ref.gather_a[layer, :, t * BLK : (t + 1) * BLK], ref.dproj[layer]
        )
        for i in range(8):
            x, zr, part = i // 2, i % 2, slice(i * 16, i * 16 + 16)
            out[x, zr * 2, t * 16 : t * 16 + 16, 0:384] = g_qkv[part]

    def fill_down(layer, t):
        out = grads_of(layer)
        g_down = product(ref.active[layer, :, t * BLK : (t + 1) * BLK], ref.gather_m[layer])
        for half in range(2):
            i = t * 2 + half
            x, zr = i // 2, i % 2
            for zc in range(2):
                lanes = slice(zc * COLS, zc * COLS + COLS)
                out[x, zr * 2 + zc, 144:208, :] = g_down[half * 64 : half * 64 + 64, lanes]

    def fill_dense(layer):
        out = grads_of(layer)
        g_dense = product(ref.ctx_rows[layer], ref.gather_t[layer])
        for i in range(8):
            x, zr = i // 2, i % 2
            for zc in range(2):
                lanes = slice(zc * COLS, zc * COLS + COLS)
                out[x, zr * 2 + zc, 128:144, :] = g_dense[i * 16 : i * 16 + 16, lanes]

    def fill_spare(layer):
        out = grads_of(layer)
        here = pl.ds(pl.multiple_of(rank * BLK, BLK), BLK)
        sums_p, sums_u = column_sums(ref.dproj[layer]), column_sums(ref.grad_pre[layer])
        parts = [sums_p[:, :BLK], sums_p[:, 2 * BLK :]]
        parts += [column_sums(ref.gather_t[layer, :, here]), column_sums(ref.gather_m[layer, :, here])]
        parts += [sums_u[:, i * BLK : (i + 1) * BLK] for i in range(4)]
        vectors = jnp.concatenate(parts, axis=0)
        empty = jnp.zeros((16, BLK), BF)
        for t in range(2 * RING):
            spare = jnp.concatenate(
                [jnp.where(rank == t, vectors, jnp.zeros_like(vectors)),
                 ref.norms[layer, 0:4, t * BLK : (t + 1) * BLK], jnp.zeros((4, BLK), F32)],
                axis=0,
            ).astype(BF)
            for i in range(8):
                x, zr = i // 2, i % 2
                out[x, zr * 2 + 1, t * 16 : t * 16 + 16, 384:512] = spare if i == 0 else empty

    def queue(function, layer, amount):
        for t in range(amount):
            fillers.append(functools.partial(function, layer, t))

    vec = ref.vec
    pack = ref.pack
    for i, name in enumerate(VECTORS):
        pack[2 * i : 2 * i + 2, :] = getattr(ref, name)[...].astype(F32)
    for i in range(8):
        part = slice((i % 4) * BLK, (i % 4 + 1) * BLK)
        pack[16 + i : 17 + i, :] = ref.up_bias[i // 4 : i // 4 + 1, part].astype(F32)
    pack_copies = [push(ref.pack, vec.at[shard], peer) for peer in peers]
    first_weights = ship_columns(ref.raw_qkv, 0, ref.w_qkv.at[0], 3)
    vec[shard] = ref.pack[...]
    wait_all(pack_copies)

    def vector(number, layer):
        row = number * 2 + layer
        return jnp.concatenate([vec[s, row : row + 1, :] for s in range(2 * RING)], axis=1)

    def rank_vector(row):
        return vec[rank, row : row + 1, :]

    def normed(values, number, layer):
        xhat, _ = norm_parts(values)
        return (xhat * vector(number, layer) + vector(number + 1, layer)).astype(BF)

    swaps = []

    def project(layer):
        done = []
        bias = jnp.concatenate(
            [rank_vector(12 + layer), jnp.zeros((1, BLK), F32), rank_vector(14 + layer)], axis=1
        )

        def consume(group, q):
            where = rows(group, q)
            value = jnp.dot(
                ref.gather_a[layer, where, :], tall(ref.w_qkv.at[layer]), preferred_element_type=F32
            )
            ref.pbuf[where, :] = (value + bias).astype(BF)
            if any(q is other for other in done):
                swaps.append(swap_out(ref.pbuf, ref.qkv.at[layer], q))
            done.append(q)

        return consume

    def lift(layer):
        bias = jnp.concatenate([rank_vector(16 + 4 * layer + i) for i in range(4)], axis=1)

        def consume(group, q):
            where = rows(group, q)
            pre = jnp.dot(
                ref.gather_b[layer, where, :], tall(ref.w_up.at[layer]), preferred_element_type=F32
            ) + bias
            sq = pre * pre
            t = jnp.tanh(0.7978845608028654 * (pre + 0.044715 * sq * pre))
            ref.active[layer, where, :] = (0.5 * pre * (1.0 + t)).astype(BF)
            ref.slope[layer, where, :] = (
                0.5 * (1.0 + t)
                + 0.5 * pre * (1.0 - t * t) * (0.7978845608028654 * (1.0 + 3.0 * 0.044715 * sq))
            ).astype(BF)

        return consume

    def lower(layer):
        def consume(group, q):
            where = rows(group, q)
            value = lax.dot_general(
                ref.gather_m[layer, where, :], ref.w_down[layer], NT, preferred_element_type=F32
            )
            ref.grad_pre[layer, where, :] = (value * ref.slope[layer, where, :].astype(F32)).astype(BF)

        return consume

    def spread_context(layer):
        done = []

        def consume(group, q):
            where = rows(group, q)
            value = lax.dot_general(
                ref.gather_t[layer, where, :], ref.w_dense[layer], NT, preferred_element_type=F32
            )
            ref.ctx[where, :] = value.astype(BF)
            if any(q is other for other in done):
                swaps.append(swap_out(ref.ctx, ref.gctx, q))
            done.append(q)

        return consume

    shipping = SimpleNamespace()

    def ship_a():
        shipping.quarters = ship_quarters(first_weights)
        shipping.up0 = ship_columns(ref.raw_up, 0, ref.w_up.at[0], 1)
        shipping.dense0 = ship_rows(ref.raw_dense, 0, ref.w_dense.at[0])
        wait_all(shipping.quarters)

    def ship_b():
        shipping.quarters = ship_quarters(shipping.up0)
        shipping.qkv1 = ship_columns(ref.raw_qkv, 1, ref.w_qkv.at[1], 3)

    def ship_c():
        shipping.down0 = ship_rows(ref.raw_down, 0, ref.w_down.at[0])

    def ship_d():
        wait_all(shipping.quarters)
        shipping.quarters = ship_quarters(shipping.qkv1)
        shipping.up1 = ship_columns(ref.raw_up, 1, ref.w_up.at[1], 1)
        shipping.dense1 = ship_rows(ref.raw_dense, 1, ref.w_dense.at[1])

    def ship_e():
        wait_all(shipping.quarters)
        shipping.quarters = ship_quarters(shipping.up1)
        shipping.down1 = ship_rows(ref.raw_down, 1, ref.w_down.at[1])

    gather(ref.gather_a.at[0], normed(ref.tokens[...].astype(F32), 0, 0), project(0), ship_a)
    ship_b()
    jobs.append(gather_rest(ref.gather_m.at[1], gather_start(ref.gather_m.at[1], ref.grad_out[...]), None))
    advance(jobs, 1)
    for layer in range(2):
        swap_done(swaps)
        swaps.clear()
        attention_forward(ref.slopes, ref.qkv.at[layer], ref.ctx)
        chunks = swap_in(ref.ctx, ref.ctx_rows.at[layer])
        if layer == 0:
            advance(jobs, 1)
            shipping.dense0()
        else:
            shipping.dense1()
        acc = scatter(
            ref.ctx_rows.at[layer], lambda: ref.w_dense[layer], NN, chunks,
            ship_c if layer == 0 else None,
        )
        stream = ref.tokens[...].astype(F32) if layer == 0 else ref.stream1[...]
        middle = stream + (acc + vector(2, layer))
        ref.middle[layer] = middle
        if layer == 0:
            wait_all(shipping.quarters)
            shipping.quarters = []
        gather(ref.gather_b.at[layer], normed(middle, 3, layer), lift(layer), ship_d if layer == 0 else None)
        if layer == 0:
            shipping.down0()
        else:
            run_jobs(jobs)
            shipping.down1()
            lower_rows = lower(1)
            for core in range(2):
                for q in range(RING):
                    fillers.append(functools.partial(lower_rows, core, q))
        acc = scatter(ref.active.at[layer], lambda: ref.w_down[layer], NN, None, None, 8)
        result = ref.middle[layer] + (acc + vector(5, layer))
        if layer == 0:
            ref.stream1[...] = result
            wait_all(shipping.quarters)
            shipping.quarters = []
            gather(ref.gather_a.at[1], normed(result, 0, 1), project(1), ship_e)
            wait_all(shipping.quarters)
        else:
            ref.output[...] = result

    grad = ref.grad_out[...].astype(F32)
    for layer in (1, 0):
        work(len(fillers))
        queue(fill_up, layer, 8)
        queue(fill_down, layer, 4)
        if layer:
            ref.kept[...] = grad
        acc = scatter(ref.grad_pre.at[layer], lambda: tall(ref.w_up.at[layer]), NT)
        grad = norm_back(acc, ref.middle[layer], ref.kept[...], layer, 2, vector(3, layer))
        ref.kept[...] = grad
        gather(ref.gather_t.at[layer], grad.astype(BF), spread_context(layer), None, 2)
        fillers.insert(0, functools.partial(fill_dense, layer))
        advance(jobs, 1)
        swap_done(swaps)
        swaps.clear()
        attention_backward(ref.slopes, ref.qkv.at[layer], ref.gctx, ref.pbuf, ref.dk, ref.dv)
        advance(jobs, 1)
        chunks = swap_in(ref.pbuf, ref.dproj.at[layer])
        queue(fill_qkv, layer, 8)
        acc = scatter(ref.dproj.at[layer], lambda: tall(ref.w_qkv.at[layer]), NT, chunks)
        values = ref.stream1[...] if layer else ref.tokens[...].astype(F32)
        grad = norm_back(acc, values, ref.kept[...], layer, 0, vector(0, layer))
        fillers.append(functools.partial(fill_spare, layer))
        if layer:
            ref.kept[...] = grad
            gather(ref.gather_m.at[0], grad.astype(BF), lower(0), None, 3)
            work(len(fillers))
            bufs = [getattr(ref, name) for name in REDUCE_NAMES]
            half = len(bufs) // 2
            for one in range(2):
                jobs.append(
                    reduce_job(
                        env, one == 0, one, ref.grads1, ref.totals,
                        bufs[one * half : one * half + half], job_sent, reduced,
                    )
                )
            advance(jobs, 1)
        else:
            ref.grad_tokens[...] = grad
    run_jobs(jobs)
    work(len(fillers))
    for copy in sent + leaving + job_sent:
        copy.wait_send()
    for copy in reduced:
        copy.wait()


NN = (((1,), (0,)), ((), ()))
NT = (((1,), (1,)), ((), ()))
TN = (((0,), (0,)), ((), ()))


def chain_call(cid, **operands):
    full, packed = 2 * RING * BLK, (RING, RING, PIECE, COLS)
    vmem = pltpu.VMEM
    outs = dict(
        output=((BLK, WIDTH), F32, vmem),
        grad_tokens=((BLK, WIDTH), F32, vmem),
        grads0=(packed, BF, vmem),
        totals=(packed, BF, pl.ANY),
    )
    scratch = dict(
        pack=vmem((24, BLK), F32),
        vec=vmem((2 * RING, 24, BLK), F32),
        w_qkv=vmem((2, 8, 4, 32, 384), BF),
        w_up=vmem((2, 8, 4, 32, 512), BF),
        w_dense=vmem((2, BLK, WIDTH), BF),
        w_down=vmem((2, 512, WIDTH), BF),
        gather_a=vmem((2, full, WIDTH), BF),
        gather_b=vmem((2, full, WIDTH), BF),
        gather_m=vmem((2, full, WIDTH), BF),
        gather_t=vmem((2, full, WIDTH), BF),
        pbuf=vmem((full, 384), BF),
        qkv=vmem((2, full, 384), BF),
        ctx=vmem((full, BLK), BF),
        ctx_rows=vmem((2, full, BLK), BF),
        active=vmem((2, full, 512), BF),
        slope=vmem((2, full, 512), BF),
        grad_pre=vmem((2, full, 512), BF),
        gctx=vmem((full, BLK), BF),
        dproj=vmem((2, full, 384), BF),
        dk=vmem((full, BLK), F32),
        dv=vmem((full, BLK), F32),
        stream1=vmem((BLK, WIDTH), F32),
        middle=vmem((2, BLK, WIDTH), F32),
        kept=vmem((BLK, WIDTH), F32),
        norms=vmem((2, 8, WIDTH), F32),
        own=vmem((RING, BLK, WIDTH), F32),
        sib_out=vmem((RING, BLK, WIDTH), BF),
        sib_in=vmem((2, RING, BLK, WIDTH), BF),
        stage=vmem((3, BLK, WIDTH), BF),
        near_n=vmem((2, BLK, WIDTH), BF),
        near_p=vmem((2, BLK, WIDTH), BF),
        far_n=vmem((2, HALF, WIDTH), BF),
        far_p=vmem((2, HALF, WIDTH), BF),
        grads1=vmem(packed, BF),
        send=pltpu.SemaphoreType.DMA((320,)),
        recv=pltpu.SemaphoreType.DMA((320,)),
        local=pltpu.SemaphoreType.DMA((24,)),
    )
    scratch.update(zip(REDUCE_NAMES, reduce_scratch() * 2))

    def space(name):
        if name.startswith("raw_"):
            return pl.ANY
        return pltpu.SMEM if name == "slopes" else vmem

    results = pl.pallas_call(
        functools.partial(chain_kernel, list(operands) + list(outs) + list(scratch)),
        out_shape=[jax.ShapeDtypeStruct(shape, dtype) for shape, dtype, _ in outs.values()],
        in_specs=[pl.BlockSpec(memory_space=space(name)) for name in operands],
        out_specs=[pl.BlockSpec(memory_space=where) for _, _, where in outs.values()],
        scratch_shapes=list(scratch.values()),
        compiler_params=pltpu.CompilerParams(
            collective_id=cid, has_side_effects=True, vmem_limit_bytes=CALL_VMEM
        ),
    )(*operands.values())
    return results


def unpack_kernel(final0, final1, qkv, up, dense, down, spare):
    layer, x = pl.program_id(0), pl.program_id(1)

    def write(final):
        for zr in range(2):
            rows = slice(zr * 16, zr * 16 + 16)
            for k in range(2 * RING):
                slot = slice(k * 16, k * 16 + 16)
                left = final[0, zr * 2, slot, :].astype(F32)
                right = final[0, zr * 2 + 1, slot, :].astype(F32)
                for j in range(3):
                    at = j * WIDTH + k * BLK
                    qkv[0, rows, at : at + BLK] = left[:, j * BLK : (j + 1) * BLK]
                up[0, rows, k * 512 : k * 512 + 128] = left[:, 384:512]
                up[0, rows, k * 512 + 128 : k * 512 + 512] = right[:, 0:384]
            for zc in range(2):
                lanes = slice(zc * COLS, zc * COLS + COLS)
                dense[0, rows, lanes] = final[0, zr * 2 + zc, 128:144, :].astype(F32)
                down[0, zr * 64 : zr * 64 + 64, lanes] = final[0, zr * 2 + zc, 144:208, :].astype(F32)

        @pl.when(x == 0)
        def _():
            total = final[0, 1, 0:16, 384:512].astype(F32)
            for k in range(1, 2 * RING):
                total = total + final[0, 1, k * 16 : k * 16 + 16, 384:512].astype(F32)
            spare[0] = total

    @pl.when(layer == 0)
    def _():
        write(final0)

    @pl.when(layer == 1)
    def _():
        write(final1)


def unpack_call(final0, final1):
    layers = 2

    def block(index):
        def at(layer, x):
            return (jnp.where(layer == index, x, (RING - 1) * (1 - index)), 0, 0, 0)

        return pl.BlockSpec((1, RING, PIECE, COLS), at)

    def rows(count, width):
        return pl.BlockSpec((1, count, width), lambda layer, x: (layer, x, 0))

    return pl.pallas_call(
        unpack_kernel,
        grid=(layers, RING),
        out_shape=[
            jax.ShapeDtypeStruct((layers, BLK, 3 * WIDTH), F32),
            jax.ShapeDtypeStruct((layers, BLK, 4 * WIDTH), F32),
            jax.ShapeDtypeStruct((layers, BLK, WIDTH), F32),
            jax.ShapeDtypeStruct((layers, 4 * BLK, WIDTH), F32),
            jax.ShapeDtypeStruct((layers, 16, BLK), F32),
        ],
        in_specs=[block(0), block(1)],
        out_specs=[
            rows(32, 3 * WIDTH), rows(32, 4 * WIDTH), rows(32, WIDTH), rows(128, WIDTH),
            pl.BlockSpec((1, 16, BLK), lambda layer, x: (layer, 0, 0)),
        ],
        compiler_params=pltpu.CompilerParams(vmem_limit_bytes=CALL_VMEM),
    )(final0, final1)


def on_device(
    tokens,
    grad_out,
    slope_index,
    ln1_gain,
    ln1_bias,
    qkv_weight,
    q_bias,
    v_bias,
    dense_weight,
    dense_bias,
    ln2_gain,
    ln2_bias,
    up_weight,
    up_bias,
    down_weight,
    down_bias,
):
    layers = qkv_weight.shape[0]
    heads = slope_index.shape[0]
    rank = lax.axis_index("c") * RING + lax.axis_index("y")
    slopes_all = jnp.exp2(-8.0 * (slope_index.astype(F32) + 1.0) / heads)
    slopes = lax.dynamic_slice(slopes_all, (rank * 2,), (2,))

    output, grad_stream, grads0, final1 = chain_call(
        1, slopes=slopes, tokens=tokens, grad_out=grad_out, ln1_gain=ln1_gain, ln1_bias=ln1_bias,
        dense_bias=dense_bias, ln2_gain=ln2_gain, ln2_bias=ln2_bias, down_bias=down_bias,
        q_bias=q_bias, v_bias=v_bias, up_bias=up_bias, raw_qkv=qkv_weight,
        raw_up=up_weight, raw_dense=dense_weight, raw_down=down_weight,
    )
    final0 = reduce_call(2, grads0)
    g_qkv, g_up, g_dense, g_down, spare = unpack_call(final0, final1)
    return (
        output,
        grad_stream,
        spare[:, 8],
        spare[:, 9],
        g_qkv,
        spare[:, 0],
        spare[:, 1],
        g_dense,
        spare[:, 2],
        spare[:, 10],
        spare[:, 11],
        g_up,
        spare[:, 4:8].reshape(layers, -1),
        g_down,
        spare[:, 3],
    )


def solution(mesh):
    replica, shard = mesh.devices.shape
    fine = Mesh(mesh.devices.reshape(replica // 4, 2, 2, shard // RING, RING), AXES)
    rows = P(AXES, None)
    flat = P(None, ("xl", "y"))
    wide = P(None, ("xl", "y"), None)
    return jax.shard_map(
        on_device,
        mesh=fine,
        in_specs=(
            rows, rows, P(), flat, flat, wide, flat, flat, wide, flat, flat, flat, wide, flat,
            wide, flat,
        ),
        out_specs=(
            rows, rows, flat, flat, wide, flat, flat, wide, flat, flat, flat, wide, flat, wide,
            flat,
        ),
        check_vma=False,
    )
```
